32 devices in a mesh: dp: 16 (over z, x, core), tensor: 2 (over y).
Axes of the slice: x: 2, y: 2, z: 4, core: 2. Of those that a mesh axis runs over, the one named last changes fastest.
Arguments:
- tokens: bfloat16 [4096, 768], P(('dp', 'tensor')), may hold values from -6 to 6
- gain_one: bfloat16 [768], replicated, may hold values from 0.5 to 1.5
- w_query: bfloat16 [768, 768], P('dp', 'tensor'), may hold values from -0.21875 to 0.21875
- w_key: bfloat16 [768, 768], P('dp', 'tensor'), may hold values from -0.21875 to 0.21875
- w_value: bfloat16 [768, 768], P('dp', 'tensor'), may hold values from -0.21875 to 0.21875
- w_out: bfloat16 [768, 768], P('dp', 'tensor'), may hold values from -0.875 to 0.875
- bias_table: float32 [32, 12], replicated, may hold values from -4 to 4
- gain_two: bfloat16 [768], replicated, may hold values from 0.5 to 1.5
- w_router: bfloat16 [768, 8], replicated, may hold values from -0.15625 to 0.15625
- w_up: bfloat16 [768, 24576], P(None, ('dp', 'tensor')), may hold values from -0.21875 to 0.21875
- w_down: bfloat16 [768, 24576], P(None, ('dp', 'tensor')), may hold values from -0.875 to 0.875
- routes: int32 [4096, 1], P('dp'), may hold values from 0 to 7; in each aligned block of 256 rows (0 to 255, 256 to 511, ...) at most 40 rows name the same one
- doc_lengths: int32 [8, 8], replicated, may hold values from 1 to 385, as said below
- buckets: int32 [1023], replicated, may hold values from 0 to 31
- cotangent: bfloat16 [4096, 768], P('dp'), may hold values from -6 to 6
Outputs:
- activations: bfloat16 [4096, 768], P(('dp', 'tensor'))
- input_grad: float32 [4096, 768], P(('dp', 'tensor'))
- grad_gain_one: float32 [768], replicated
- grad_w_query: float32 [768, 768], P('dp', 'tensor')
- grad_w_key: float32 [768, 768], P('dp', 'tensor')
- grad_w_value: float32 [768, 768], P('dp', 'tensor')
- grad_w_out: float32 [768, 768], P('dp', 'tensor')
- grad_bias: float32 [32, 12], replicated
- grad_gain_two: float32 [768], replicated
- grad_w_router: float32 [768, 8], replicated
- grad_w_up: float32 [768, 24576], P(None, ('dp', 'tensor'))
- grad_w_down: float32 [768, 24576], P(None, ('dp', 'tensor'))
The draws below stay inside these ranges and needn't reach their ends.
Inputs may be any that keep to these rules, and one draw needn't show every extreme that they name: `routes`: in each aligned block of 256 rows no expert is named by more than 40 rows; in every draw some block has an expert named by exactly 40 rows. `doc_lengths`: each row holds the lengths of the 8 documents of one sequence in order; they sum to 512, and exactly one of them has 385 tokens.
All inputs are finite; a program needn't handle non-finite values.
Results may differ from the reference program's by a relative error of at most 0.014.
Values may be sent and summed in bfloat16 or wider, within the bound.
No kernel may reach another device: no remote copies, remote signals or barrier semaphores. Data moves between devices by JAX's collectives and lax.ppermute only.
A program may use at most 128 MiB of HBM per device.

```python
import math
import jax
import jax.numpy as jnp
import numpy as np
from jax import lax

D = 768
HEADS = 12
FF = 3072
BUCKETS = 32
TOK_DEV = 128
GROUP = 2
DOCS = 8
EXPERTS = 8
LEN = 512
SEQS = 8
TOKENS = 4096
CAP = 40
N_TENSOR = 2


def draw_doc_lengths(key, part):
    key = jax.random.fold_in(key, 7)
    rest = LEN // 4 - 1
    spare = rest - (DOCS - 1)
    key_cut, key_place = jax.random.split(key)
    cuts = jnp.sort(jax.random.randint(key_cut, (SEQS, DOCS - 2), 0, spare + 1), axis=1)
    edges = jnp.concatenate([jnp.zeros((SEQS, 1), jnp.int32), cuts.astype(jnp.int32), jnp.full((SEQS, 1), spare, jnp.int32)], axis=1)
    others = 1 + edges[:, 1:] - edges[:, :-1]
    longest = LEN - rest
    placed = jax.random.randint(key_place, (SEQS, 1), 0, DOCS)
    order = jnp.arange(DOCS, dtype=jnp.int32)[None, :]
    before = jnp.concatenate([others, others[:, -1:]], axis=1)
    after = jnp.concatenate([others[:, :1], others], axis=1)
    return jnp.where(order < placed, before, jnp.where(order == placed, longest, after)).astype(jnp.int32)


def place_ends(entries, stream_key, smallest, top_value):
    longest = entries.shape.index(max(entries.shape))
    spots = []
    for shift in (0, 1):
        where = [jax.random.randint(jax.random.fold_in(stream_key, axis), (), 0, length) for axis, length in enumerate(entries.shape)]
        where[longest] = (where[longest] + shift) % entries.shape[longest]
        spots.append(tuple(where))
    return entries.at[spots[0]].set(smallest).at[spots[1]].set(top_value)


def levels(own_key, shape, cuts, low, high):
    factor_of = 1.0
    for axis_at, blocks in cuts:
        heights = jax.random.uniform(jax.random.fold_in(jax.random.fold_in(own_key, 6), axis_at), (blocks,), jnp.float32, low / len(cuts), high / len(cuts))
        factor_of = factor_of * jnp.repeat(jnp.exp(heights), shape[axis_at] // blocks).reshape((-1,) + (1,) * (len(shape) - 1 - axis_at))
    return factor_of


def routed_block(own_key, own, number, rows, count, top, most, skew):
    ranking = jax.random.permutation(own_key, count)
    packed, ordinary = shares(count, rows * top, most, skew, True), shares(count, rows * top, most, skew, False)
    places = jnp.arange(count)

    def named(sizes, offset_by):
        used = int((sizes > 0).sum())
        fixed = max(1, used // 4)
        passed = fixed + (places - fixed + offset_by * (used - fixed)) % max(1, count - fixed)
        return jnp.zeros((count,), jnp.int32).at[ranking[jnp.where(places < fixed, places, passed)]].set(jnp.asarray(sizes, jnp.int32))

    sizes = jnp.where(number % 4 == 0, named(packed, number // 4), named(ordinary, number - number // 4 - 1))
    mixed = jax.random.permutation(jax.random.fold_in(own, 3), count)
    donor, sink = mixed[0:count // 2 * 2:2], mixed[1:count // 2 * 2:2]
    margin = jnp.minimum(sizes[donor] - 1, most - sizes[sink]) // 2
    margin = jnp.where((donor == ranking[0]) | (sink == ranking[0]) | (sizes[sink] == 0), 0, jnp.maximum(margin, 0))
    passed = jax.random.randint(jax.random.fold_in(own, 4), (count // 2,), 0, 1 << 20) % (margin + 1)
    sizes = sizes.at[donor].add(-passed).at[sink].add(passed)
    members = jnp.searchsorted(jnp.cumsum(sizes), jnp.arange(rows * top), side="right").astype(jnp.int32)
    table = members.reshape(top, rows).T
    table = table[jax.random.permutation(jax.random.fold_in(own, 1), rows)]
    offset_by = jax.random.randint(jax.random.fold_in(own, 2), (rows, 1), 0, top)
    return jnp.take_along_axis(table, (jnp.arange(top)[None, :] + offset_by) % top, axis=1)


def shares(amount, total, reach, lean, full):
    weights = [(1 << 20) // math.isqrt(rank ** lean) + 1 for rank in range(1, amount + 1)]
    largest = reach if full else min(reach, max(-(-total // amount), total * weights[0] // sum(weights)))
    least = 1 if total - largest >= amount - 1 else 0
    holding, surplus = [largest] + [least] * (amount - 1), total - largest - least * (amount - 1)
    while surplus > 0:
        free = [i for i in range(1, amount) if holding[i] < largest] or [i for i in range(1, amount) if holding[i] < reach]
        mass, budget = sum([weights[i] for i in free]), surplus
        for i in free:
            more = min(reach - holding[i], max(1, budget * weights[i] // mass), surplus)
            holding[i] = holding[i] + more
            surplus = surplus - more
    return np.array(holding)


def noise(rng, shape, scale, reach, shards=(), kind=jnp.bfloat16):
    factor_of = levels(rng, shape, shards, -0.22, 0.18) if shards else 1.0
    drawn = jax.random.normal(rng, shape, jnp.float32) * scale * factor_of
    return jnp.minimum(jnp.maximum(drawn, -reach), reach).astype(kind)


def setup_inputs(seed: int = 0) -> dict:
    key_of = jax.random.split(jax.random.key(seed), 16)
    tokens = noise(key_of[0], (TOKENS, D), 1.0, 6.0, ((0, 32),))
    gain_one = jnp.clip(1.0 + 0.1 * jax.random.normal(key_of[1], (D,), jnp.float32), 0.5, 1.5).astype(jnp.bfloat16)
    w_query = noise(key_of[2], (D, D), D ** -0.5, 0.21875, ((0, 16), (1, 2)))
    w_key = noise(key_of[3], (D, D), D ** -0.5, 0.21875, ((0, 16), (1, 2)))
    w_value = noise(key_of[4], (D, D), D ** -0.5, 0.21875, ((0, 16), (1, 2)))
    w_out = noise(key_of[5], (D, D), (D // 16) ** -0.5, 0.875, ((0, 16), (1, 2)))
    bias_table = noise(key_of[6], (BUCKETS, HEADS), 1.0, 4.0, (), jnp.float32)
    gain_two = jnp.clip(1.0 + 0.1 * jax.random.normal(key_of[7], (D,), jnp.float32), 0.5, 1.5).astype(jnp.bfloat16)
    w_router = noise(key_of[8], (D, EXPERTS), 0.025, 0.15625)
    w_up = noise(key_of[9], (D, EXPERTS * FF), D ** -0.5, 0.21875, ((1, 32),))
    w_down = noise(key_of[10], (D, EXPERTS * FF), (max(1, FF // (EXPERTS * EXPERTS))) ** -0.5, 0.875, ((1, 32),))
    routes_keys = jax.random.split(jax.random.fold_in(key_of[11], 1), TOKENS // (N_TENSOR * TOK_DEV))
    routes_turns = jax.random.permutation(jax.random.fold_in(key_of[11], 3), TOKENS // (N_TENSOR * TOK_DEV))
    routes = jax.vmap(lambda own, number: routed_block(jax.random.fold_in(key_of[11], 2), own, number, N_TENSOR * TOK_DEV, EXPERTS, 1, CAP, 2))(routes_keys, routes_turns).reshape((TOKENS, 1))
    doc_lengths = draw_doc_lengths(jax.random.fold_in(key_of[15], 71), 0)
    buckets = place_ends(jax.random.randint(key_of[13], (2 * LEN - 1,), 0, BUCKETS), jax.random.fold_in(key_of[13], 1), 0, BUCKETS - 1).astype(jnp.int32)
    cotangent = noise(key_of[14], (TOKENS, D), 1.0, 6.0, ((0, 16),))
    return dict(tokens=tokens, gain_one=gain_one, w_query=w_query, w_key=w_key, w_value=w_value, w_out=w_out, bias_table=bias_table, gain_two=gain_two, w_router=w_router, w_up=w_up, w_down=w_down, routes=routes, doc_lengths=doc_lengths, buckets=buckets, cotangent=cotangent)


@jax.custom_vjp
def low(v):
    return lax.optimization_barrier(v.astype(jnp.bfloat16)).astype(jnp.float32)

@jax.custom_vjp
def low_back(v):
    return v

def low_keep(v):
    return (low(v), None)

def low_pass(kept, grad):
    return (grad,)

def back_keep(v):
    return (v, None)

def back_low(kept, grad):
    return (low(grad),)
low.defvjp(low_keep, low_pass)
low_back.defvjp(back_keep, back_low)
exact = lax.Precision.HIGHEST
norm_eps = 1e-06

def rms_scale(values, gain):
    return values * lax.rsqrt(lax.optimization_barrier(jnp.mean(values * values, axis=-1, keepdims=True)) + norm_eps) * gain

def take_rows(matrix, indices):
    return jnp.take(matrix, indices, axis=0)

def sequence_layer(weights, seq_tokens, lengths_row, route_seq, buckets):
    gain_one, w_query, w_key, w_value, w_out, bias_table, gain_two, w_router, w_up, w_down = weights
    seq_length, width = seq_tokens.shape
    head_count = bias_table.shape[1]
    head_size = width // head_count
    score_scale = head_size ** (-0.5)
    normed = low(rms_scale(seq_tokens, gain_one))
    query = low_back(low(jnp.dot(normed, w_query, precision=exact)))
    key_proj = low_back(low(jnp.dot(normed, w_key, precision=exact)))
    value_proj = low_back(low(jnp.dot(normed, w_value, precision=exact)))
    ends = jnp.cumsum(lengths_row)
    places = jnp.arange(seq_length, dtype=jnp.int32)
    document = lax.optimization_barrier(jnp.sum((ends[None, :] <= places[:, None]).astype(jnp.int32), axis=1))
    same_doc = document[:, None] == document[None, :]
    offsets = places[None, :] - places[:, None] + seq_length - 1
    bias = jnp.moveaxis(bias_table[buckets[offsets]], 2, 0)
    query_heads = query.reshape(seq_length, head_count, head_size)
    key_heads = key_proj.reshape(seq_length, head_count, head_size)
    value_heads = value_proj.reshape(seq_length, head_count, head_size)
    scores = jnp.einsum('qhd,khd->hqk', query_heads, key_heads, precision=exact) * score_scale + bias
    scores = jnp.where(same_doc[None], low_back(scores), -1e+30)
    probs = jax.nn.softmax(scores, axis=-1)
    mixed = jnp.einsum('hqk,khd->qhd', low(probs), value_heads, precision=exact).reshape(seq_length, width)
    mixed = low_back(low(mixed))
    attended = low_back(jnp.dot(mixed, w_out.T, precision=exact))
    hidden = seq_tokens + attended
    normed_two = low(rms_scale(hidden, gain_two))
    logits = low_back(jnp.dot(normed_two, w_router, precision=exact))
    gates = jax.nn.softmax(logits, axis=-1)
    experts = w_router.shape[1]
    choose = route_seq[:, None] == jnp.arange(experts, dtype=jnp.int32)[None, :]
    chosen = lax.optimization_barrier(jnp.sum(jnp.where(choose, gates, 0.0), axis=1))
    block_rows = seq_length // GROUP
    capacity = max(2, (5 * block_rows + 4 * experts - 1) // (4 * experts))
    routes_block = route_seq.reshape(GROUP, block_rows)
    picks = (routes_block[:, :, None] == jnp.arange(experts, dtype=jnp.int32)[None, None, :]).astype(jnp.int32)
    slot_index = lax.optimization_barrier(jnp.sum((jnp.cumsum(picks, axis=1) - 1) * picks, axis=2))
    target = routes_block * capacity + slot_index
    slots = jnp.arange(experts * capacity, dtype=jnp.int32)
    table = (target[:, None, :] == slots[None, :, None]).astype(jnp.float32)
    dispatched = jnp.einsum('gsb,gbd->gsd', table, normed_two.reshape(GROUP, block_rows, width), precision=exact)
    dispatched = dispatched.reshape(GROUP, experts, capacity, width)
    up_cube = w_up.reshape(width, experts, -1)
    down_cube = w_down.reshape(width, experts, -1)
    upward = low_back(jnp.einsum('gecd,def->gecf', dispatched, up_cube, precision=exact))
    active = low(jax.nn.gelu(upward))
    expert_out = low_back(jnp.einsum('gecf,def->gecd', active, down_cube, precision=exact))
    expert_out = expert_out.reshape(GROUP, experts * capacity, width)
    returned = jax.vmap(take_rows)(expert_out, target).reshape(seq_length, width)
    return hidden + chosen[:, None] * returned

def reference(tokens, gain_one, w_query, w_key, w_value, w_out, bias_table, gain_two, w_router, w_up, w_down, routes, doc_lengths, buckets, cotangent):
    weights = tuple((entry.astype(jnp.float32) for entry in (gain_one, w_query, w_key, w_value, w_out, bias_table, gain_two, w_router, w_up, w_down)))
    inputs = tokens.astype(jnp.float32)
    batch = math.gcd(SEQS, 8)
    steps_count = SEQS // batch

    def forward(values, params):

        def some_sequences(items):
            seq_tokens, lengths_rows, route_seqs = items

            def single(seq_one, lengths_one, route_one):
                return sequence_layer(params, seq_one, lengths_one, route_one, buckets)
            return jax.vmap(single)(seq_tokens, lengths_rows, route_seqs)
        outputs = lax.map(jax.checkpoint(some_sequences), (values.reshape(steps_count, batch, LEN, D), doc_lengths.reshape(steps_count, batch, DOCS), routes.reshape(steps_count, batch, LEN)))
        return outputs.reshape(TOKENS, D)
    result, pull = jax.vjp(forward, inputs, weights)
    grad_inputs, grads = pull(cotangent.astype(jnp.float32))
    return (result.astype(jnp.bfloat16), grad_inputs, grads[0], grads[1], grads[2], grads[3], grads[4], grads[5], grads[6], grads[7], grads[8], grads[9])
```

```python
import functools

import jax
import jax.numpy as jnp
from jax import lax
from jax.experimental import pallas as pl
from jax.experimental.pallas import tpu as pltpu
from jax.sharding import Mesh, PartitionSpec as P

HD = 64
GROUP = 2
DIRECT = 8
TILE = 128

norm_eps = 1e-06
masked_value = -1e30
exact = lax.Precision.HIGHEST
bf16 = jnp.bfloat16
f32 = jnp.float32

VMEM = pl.BlockSpec(memory_space=pltpu.VMEM)
SMEM = pl.BlockSpec(memory_space=pltpu.SMEM)


def across(shard, axis, bits):
    return lax.ppermute(shard, axis, [(i, i ^ bits) for i in range(lax.axis_size(axis))])


def call(body, name, outs, args, smem=0, scratch=(), flops=0, limit=40):
    moved = sum(a.size * a.dtype.itemsize for a in args) + sum(
        o.size * jnp.dtype(o.dtype).itemsize for o in outs
    )
    return pl.pallas_call(
        body,
        name=name,
        out_shape=outs,
        in_specs=[SMEM] * smem + [VMEM] * (len(args) - smem),
        out_specs=[VMEM] * len(outs),
        scratch_shapes=scratch,
        compiler_params=pltpu.CompilerParams(vmem_limit_bytes=limit * 1024 * 1024),
        cost_estimate=pl.CostEstimate(flops=flops, bytes_accessed=moved, transcendentals=0),
    )(*args)


def out(shape, dtype):
    return jax.ShapeDtypeStruct(shape, dtype)


def mm(a, b):
    return jnp.dot(a, b, preferred_element_type=f32)


def mm_bt(a, b):
    return lax.dot_general(a, b, (((1,), (1,)), ((), ())), preferred_element_type=f32)


def mm_at(a, b):
    return lax.dot_general(a, b, (((0,), (0,)), ((), ())), preferred_element_type=f32)


def project_kernel(parts, ids, own_ref, other_ref, *refs):
    pieces = refs[:parts]
    wqkv_ref, wo_ref, seq_ref, qkv_ref = refs[parts:]
    core = ids[0]
    me = ids[1]
    rows = pieces[0].shape[0]
    cols = wqkv_ref.shape[1]
    half = own_ref.shape[0]
    seq_ref[pl.ds(pl.multiple_of(core * half, half), half), :] = own_ref[...]
    seq_ref[pl.ds(pl.multiple_of((1 - core) * half, half), half), :] = other_ref[...]
    for i, piece in enumerate(pieces):
        start = 0 if parts == 1 else pl.multiple_of((me ^ i) * rows, rows)
        wqkv_ref[pl.ds(start, rows), :] = piece[:, :cols]
        wo_ref[pl.ds(start, rows), :] = piece[:, cols:]
    for i in range(0, 2 * half, 256):
        qkv_ref[i : i + 256, :] = mm(seq_ref[i : i + 256, :], wqkv_ref[...]).astype(bf16)


def attend_kernel(heads, ids, qkv_ref, vec_ref, row_docs, col_docs, *refs):
    probs_ref, mixed_ref, keep_ref, send_ref = refs
    core = ids[0]
    seq = qkv_ref.shape[0]
    width = heads * HD
    half = seq // GROUP
    span = seq + TILE
    for h in range(heads):
        at = h * HD
        key = qkv_ref[:, width + at : width + at + HD]
        value = qkv_ref[:, 2 * width + at : 2 * width + at + HD]
        for i in range(0, seq, TILE):
            base = seq - TILE - i
            seg = jnp.broadcast_to(vec_ref[h : h + 1, base : base + span], (TILE, span))
            bias = pltpu.roll(seg, span - TILE + 1, 1, stride=1, stride_axis=0)[:, :seq]
            scores = mm_bt(qkv_ref[i : i + TILE, at : at + HD], key) * HD**-0.5 + bias
            scores = jnp.where(row_docs[i : i + TILE, :] == col_docs[...], scores, masked_value)
            peak = jnp.max(scores, axis=1, keepdims=True)
            exp_scores = jnp.exp(scores - peak)
            probs = exp_scores / jnp.sum(exp_scores, axis=1, keepdims=True)
            probs_ref[h, i : i + TILE, :] = probs
            mixed_ref[i : i + TILE, at : at + HD] = mm(probs.astype(bf16), value).astype(bf16)
    keep_ref[...] = mixed_ref[pl.ds(pl.multiple_of(core * half, half), half), :]
    send_ref[...] = mixed_ref[pl.ds(pl.multiple_of((1 - core) * half, half), half), :]


def attended_kernel(keep_ref, got_ref, wo_ref, wo_other_ref, out_ref):
    total = mm_bt(keep_ref[...], wo_ref[...]) + mm_bt(got_ref[...], wo_other_ref[...])
    out_ref[...] = total.astype(bf16)


def dispatch_kernel(x_ref, own_ref, got_ref, gain_ref, table_ref, hidden_ref, *blocks):
    hidden = x_ref[...].astype(f32) + (own_ref[...].astype(f32) + got_ref[...].astype(f32))
    hidden_ref[...] = hidden
    scale = lax.rsqrt(jnp.mean(hidden * hidden, axis=1, keepdims=True) + norm_eps)
    normed = (hidden * scale * gain_ref[...]).astype(bf16)
    slots = mm(table_ref[...], normed)
    rows = blocks[0].shape[0]
    for i, block in enumerate(blocks):
        block[...] = slots[i * rows : (i + 1) * rows, :].astype(bf16)


def expert_kernel(ids, own_ref, other_ref, h_ref, wup_ref, wr_ref, *refs):
    active_ref, gup_ref, chosen_ref, keep_ref, send_ref, router_ref = refs
    rows = own_ref.shape[0]
    step = rows // 2
    router = jnp.zeros(router_ref.shape, f32)
    root = 0.7978845608028654
    for i in range(0, 2 * rows, step):
        src = own_ref if i < rows else other_ref
        at = i % rows
        slots = src[at : at + step, :]
        logits = mm(slots, wr_ref[...])
        peak = jnp.max(logits, axis=1, keepdims=True)
        exp_logits = jnp.exp(logits - peak)
        gates = exp_logits / jnp.sum(exp_logits, axis=1, keepdims=True)
        mine = lax.broadcasted_iota(jnp.int32, gates.shape, 1) == ids[1]
        chosen = jnp.sum(jnp.where(mine, gates, 0.0), axis=1, keepdims=True)
        chosen_ref[i : i + step, :] = chosen
        up = mm(slots, wup_ref[...])
        square = up * up
        bent = jnp.tanh(root * (up + 0.044715 * up * square))
        low = (0.5 * up * (1.0 + bent)).astype(bf16)
        active_ref[i : i + step, :] = low
        slope = 0.5 * (1.0 + bent) + 0.5 * up * (1.0 - bent * bent) * root * (
            1.0 + 3.0 * 0.044715 * square
        )
        back = h_ref[i : i + step, :]
        gup = (chosen * back * slope).astype(bf16)
        gup_ref[i : i + step, :] = gup
        grad_chosen = jnp.sum(low.astype(f32) * back, axis=1, keepdims=True)
        grad_logits = gates * (jnp.where(mine, 1.0, 0.0) - chosen) * grad_chosen
        grad_logits = grad_logits.astype(bf16)
        router = router + mm_at(slots, grad_logits)
        grad = mm_bt(gup, wup_ref[...]) + mm_bt(grad_logits, wr_ref[...])
        if i < rows:
            keep_ref[at : at + step, :] = grad
        else:
            send_ref[at : at + step, :] = grad.astype(bf16)
    router_ref[...] = router


def expert_rest_kernel(own_ref, other_ref, cots_ref, active_ref, gup_ref, chosen_ref, wdown_ref, *refs):
    keep_ref, send_ref, gwup_ref, gwdown_ref = refs
    rows = own_ref.shape[0]
    result = mm_bt(active_ref[...], wdown_ref[...]) * chosen_ref[...]
    keep_ref[...] = result[:rows, :]
    send_ref[...] = result[rows:, :].astype(bf16)
    gwup_ref[...] = mm_at(own_ref[...], gup_ref[:rows, :]) + mm_at(other_ref[...], gup_ref[rows:, :])
    grads = (chosen_ref[...] * cots_ref[...].astype(f32)).astype(bf16)
    gwdown_ref[...] = mm_at(grads, active_ref[...])


def join_kernel(keep_ref, got_ref, *blocks):
    total = keep_ref[...] + got_ref[...].astype(f32)
    rows = blocks[0].shape[0]
    for i, block in enumerate(blocks):
        block[...] = total[i * rows : (i + 1) * rows, :].astype(bf16)


def gather_kernel(back_table_ref, *refs):
    blocks = refs[:-1]
    slots = jnp.concatenate([b[...].astype(f32) for b in blocks], axis=0).astype(bf16)
    refs[-1][...] = mm(back_table_ref[...], slots).astype(bf16)


def hidden_back_kernel(hidden_ref, own_ref, got_ref, cot_ref, gain_ref, grad_ref, low_ref, dgain_ref):
    hidden = hidden_ref[...]
    grad_normed = own_ref[...].astype(f32) + got_ref[...].astype(f32)
    scale = lax.rsqrt(jnp.mean(hidden * hidden, axis=1, keepdims=True) + norm_eps)
    dgain_ref[...] = jnp.sum(grad_normed * hidden * scale, axis=0, keepdims=True)
    pulled = gain_ref[...] * grad_normed
    inner = jnp.mean(pulled * hidden, axis=1, keepdims=True)
    grad = cot_ref[...].astype(f32) + scale * pulled - hidden * (scale * scale * scale) * inner
    grad_ref[...] = grad
    low_ref[...] = grad.astype(bf16)


def attend_back_kernel(heads, parts, ids, own_ref, other_ref, wo_ref, qkv_ref, probs_ref, seq_ref, mixed_ref, *refs):
    dqkv_ref, gwo_ref, diag_ref = refs[:3]
    blocks = refs[3 : 3 + parts]
    ga_ref, gm_ref, ds_ref, gw_ref = refs[3 + parts :]
    core = ids[0]
    me = ids[1]
    half = own_ref.shape[0]
    seq = qkv_ref.shape[0]
    width = heads * HD
    span = seq + TILE
    ga_ref[pl.ds(pl.multiple_of(core * half, half), half), :] = own_ref[...]
    ga_ref[pl.ds(pl.multiple_of((1 - core) * half, half), half), :] = other_ref[...]
    gm_ref[...] = mm(ga_ref[...], wo_ref[...]).astype(bf16)
    gwo_ref[...] = mm_at(ga_ref[...], mixed_ref[...]).astype(bf16)
    flip = (
        lax.broadcasted_iota(jnp.int32, (TILE, TILE), 0)
        + lax.broadcasted_iota(jnp.int32, (TILE, TILE), 1)
        == TILE - 1
    ).astype(bf16)
    diag_ref[...] = jnp.zeros_like(diag_ref)
    for h in range(heads):
        at = h * HD
        key = qkv_ref[:, width + at : width + at + HD]
        value = qkv_ref[:, 2 * width + at : 2 * width + at + HD]
        for i in range(0, seq, TILE):
            probs = probs_ref[h, i : i + TILE, :]
            grad_probs = mm_bt(gm_ref[i : i + TILE, at : at + HD], value)
            inner = jnp.sum(probs * grad_probs, axis=1, keepdims=True)
            grad_scores = (probs * (grad_probs - inner)).astype(bf16)
            ds_ref[i : i + TILE, :] = grad_scores
            dqkv_ref[i : i + TILE, at : at + HD] = (mm(grad_scores, key) * HD**-0.5).astype(bf16)
            flipped = mm(flip, grad_scores)
            padded = jnp.concatenate([flipped, jnp.zeros((TILE, TILE), f32)], axis=1)
            skewed = pltpu.roll(padded, 0, 1, stride=1, stride_axis=0)
            base = seq - TILE - i
            diag_ref[h : h + 1, base : base + span] += jnp.sum(skewed, axis=0, keepdims=True)
        dqkv_ref[:, width + at : width + at + HD] = (
            mm_at(ds_ref[...], qkv_ref[:, at : at + HD]) * HD**-0.5
        ).astype(bf16)
        dqkv_ref[:, 2 * width + at : 2 * width + at + HD] = mm_at(
            probs_ref[h].astype(bf16), gm_ref[:, at : at + HD]
        ).astype(bf16)
    gw_ref[...] = mm_at(seq_ref[...], dqkv_ref[...])
    rows = blocks[0].shape[0]
    for i, block in enumerate(blocks):
        start = 0 if parts == 1 else pl.multiple_of((me ^ i) * rows, rows)
        block[...] = gw_ref[pl.ds(start, rows), :].astype(bf16)


def normed_back_kernel(ids, dqkv_ref, wqkv_ref, keep_ref, send_ref):
    core = ids[0]
    half = keep_ref.shape[0]
    mine = dqkv_ref[pl.ds(pl.multiple_of(core * half, half), half), :]
    keep_ref[...] = mm_bt(mine, wqkv_ref[...])
    theirs = dqkv_ref[pl.ds(pl.multiple_of((1 - core) * half, half), half), :]
    send_ref[...] = mm_bt(theirs, wqkv_ref[...]).astype(bf16)


def rms_scale(values, gain):
    return values * lax.rsqrt(jnp.mean(values * values, axis=-1, keepdims=True) + norm_eps) * gain


def in_order(first, mine, other):
    return jnp.where(first, jnp.concatenate([mine, other]), jnp.concatenate([other, mine]))


def per_device(
    tokens,
    gain_one,
    w_query,
    w_key,
    w_value,
    w_out,
    bias_table,
    gain_two,
    w_router,
    w_up,
    w_down,
    routes,
    doc_lengths,
    buckets,
    cotangent,
):
    own_rows, width = tokens.shape
    block_rows = routes.shape[0]
    seq = block_rows * GROUP
    cols = w_query.shape[1] // GROUP
    heads = cols // HD
    experts = w_router.shape[1]
    capacity = max(2, (5 * block_rows + 4 * experts - 1) // (4 * experts))
    slots = experts * capacity
    nodes = lax.axis_size("node")
    core = lax.axis_index("core")
    side = lax.axis_index("tensor")
    me = lax.axis_index("node")
    direct = nodes == DIRECT
    parts = nodes if direct else 1
    ids = jnp.stack([core, me]).astype(jnp.int32)
    node_rows = width // nodes

    def trade(blocks):
        if direct:
            return [blocks[0]] + [across(blocks[i], "node", i) for i in range(1, nodes)]
        stacked = blocks[0].reshape(nodes, -1, blocks[0].shape[1])
        back = lax.all_to_all(stacked, "node", split_axis=0, concat_axis=0, tiled=True)
        return [back.reshape(blocks[0].shape)]

    def trade_natural(rows):
        stacked = rows.reshape(nodes, -1, rows.shape[-1])
        return lax.all_to_all(stacked, "node", split_axis=0, concat_axis=0, tiled=True)

    def reorder(stacked):
        if not direct:
            return stacked
        return jnp.concatenate(
            [lax.dynamic_slice_in_dim(stacked, me ^ i, 1, 0) for i in range(nodes)]
        )

    shares = jnp.stack([w_query, w_key, w_value, w_out]).reshape(4, -1, GROUP, cols)
    shares = jnp.moveaxis(shares, 0, 2).reshape(-1, GROUP, 4 * cols)
    share_kept = lax.dynamic_index_in_dim(shares, core, 1, keepdims=False)
    share_sent = lax.dynamic_index_in_dim(shares, 1 - core, 1, keepdims=False)
    piece = in_order(core == 0, share_kept, across(share_sent, "core", 1))
    if direct:
        pieces = {0: piece}
        for i in (2, 4, 6):
            pieces[i] = across(piece, "node", i)
        for i in (0, 2, 4, 6):
            pieces[i + 1] = across(pieces[i], "node", 1)
        pieces = [pieces[i] for i in range(nodes)]
    else:
        pieces = [lax.all_gather(piece, "node", axis=0, tiled=True)]

    x_rows = in_order(side == 0, tokens, across(tokens, "tensor", 1))
    gain_first = gain_one.astype(f32)
    gain_second = gain_two.astype(f32)[None, :]
    normed = rms_scale(x_rows.astype(f32), gain_first).astype(bf16)
    normed_other = across(normed, "core", 1)

    expert_ids = routes[:, 0]
    picks = (expert_ids[:, None] == jnp.arange(experts, dtype=jnp.int32)[None, :]).astype(jnp.int32)
    slot_index = jnp.sum((jnp.cumsum(picks, axis=0) - 1) * picks, axis=1)
    target = expert_ids * capacity + slot_index
    codes = jnp.arange(slots, dtype=jnp.int32)
    turned = ((codes // capacity) ^ me) * capacity + codes % capacity if direct else codes
    table = (turned[:, None] == target[None, :]).astype(bf16)
    back_table = (target[:, None] == turned[None, :]).astype(bf16)
    plain_table = (codes[:, None] == target[None, :]).astype(bf16)

    cot_slots = mm(plain_table, cotangent).astype(bf16)
    cots_own = reorder(trade_natural(cot_slots)).reshape(slots, width)
    cots = jnp.concatenate([cots_own, across(cots_own, "core", 1)])
    back_active = mm(cots, w_down)

    lengths_row = lax.dynamic_slice_in_dim(doc_lengths, me, 1, 0)[0]
    ends = jnp.cumsum(lengths_row)
    places = jnp.arange(seq, dtype=jnp.int32)
    docs = jnp.sum((ends[None, :] <= places[:, None]).astype(jnp.int32), axis=1)
    bucket_count = bias_table.shape[0]
    bucket_hot = (
        jnp.pad(buckets, (0, 1))[:, None] == jnp.arange(bucket_count, dtype=jnp.int32)[None, :]
    ).astype(f32)
    head_start = (side * GROUP + core) * heads
    bias_here = lax.dynamic_slice_in_dim(bias_table, head_start, heads, 1)
    bias_vectors = lax.dot_general(
        bias_here, bucket_hot, (((0,), (1,)), ((), ())), precision=exact, preferred_element_type=f32
    )

    wqkv, wo, normed_seq, qkv = call(
        functools.partial(project_kernel, parts),
        "project",
        [
            out((width, 3 * cols), bf16),
            out((width, cols), bf16),
            out((seq, width), bf16),
            out((seq, 3 * cols), bf16),
        ],
        [ids, normed, normed_other, *pieces],
        smem=1,
        flops=2 * seq * width * 3 * cols,
    )
    wo_other = across(wo, "core", 1)
    probs, mixed, mixed_kept, mixed_sent = call(
        functools.partial(attend_kernel, heads),
        "attend",
        [
            out((heads, seq, seq), f32),
            out((seq, cols), bf16),
            out((block_rows, cols), bf16),
            out((block_rows, cols), bf16),
        ],
        [ids, qkv, bias_vectors, docs[:, None], docs[None, :]],
        smem=1,
        flops=8 * heads * seq * seq * 256,
    )
    mixed_got = across(mixed_sent, "core", 1)
    attended = call(
        attended_kernel,
        "attended",
        [out((block_rows, width), bf16)],
        [mixed_kept, mixed_got, wo, wo_other],
        flops=4 * block_rows * width * cols,
    )[0]
    attended_got = across(attended, "tensor", 1)

    block_shapes = [out((slots // parts, width), bf16)] * parts
    hidden, *blocks = call(
        dispatch_kernel,
        "dispatch",
        [out((block_rows, width), f32), *block_shapes],
        [x_rows, attended, attended_got, gain_second, table],
        flops=2 * slots * block_rows * width,
    )
    received = trade(blocks)
    slots_own = jnp.concatenate(received)
    slots_other = across(slots_own, "core", 1)
    active, grad_upward, chosen, grad_kept, grad_sent, router_part = call(
        expert_kernel,
        "expert",
        [
            out((2 * slots, w_up.shape[1]), bf16),
            out((2 * slots, w_up.shape[1]), bf16),
            out((2 * slots, 1), f32),
            out((slots, width), f32),
            out((slots, width), bf16),
            out(w_router.shape, f32),
        ],
        [ids, slots_own, slots_other, back_active, w_up, w_router],
        smem=1,
        flops=8 * slots * width * w_up.shape[1],
    )
    grad_blocks = call(
        join_kernel, "join_grad", block_shapes, [grad_kept, across(grad_sent, "core", 1)]
    )
    grad_back = trade(grad_blocks)
    grad_normed_two = call(
        gather_kernel,
        "gather_grad",
        [out((block_rows, width), bf16)],
        [back_table, *grad_back],
        flops=2 * slots * block_rows * width,
    )[0]
    grad_normed_two_got = across(grad_normed_two, "tensor", 1)

    out_kept, out_sent, grad_w_up_here, grad_w_down_here = call(
        expert_rest_kernel,
        "expert_rest",
        [
            out((slots, width), f32),
            out((slots, width), bf16),
            out(w_up.shape, f32),
            out(w_down.shape, f32),
        ],
        [slots_own, slots_other, cots, active, grad_upward, chosen, w_down],
        flops=12 * slots * width * w_up.shape[1],
    )
    out_slots = (out_kept + across(out_sent, "core", 1).astype(f32)).astype(bf16)
    out_slots = reorder(out_slots.reshape(nodes, -1, width))
    out_back = trade_natural(out_slots).reshape(slots, width)
    returned = lax.dot_general(
        plain_table, out_back, (((0,), (0,)), ((), ())), preferred_element_type=f32
    ).astype(bf16)

    def half_of(rows, index):
        return lax.dynamic_slice_in_dim(rows, index * own_rows, own_rows, 0)

    returned_got = across(half_of(returned, 1 - side), "tensor", 1)
    activations = (
        half_of(hidden, side) + (half_of(returned, side).astype(f32) + returned_got.astype(f32))
    ).astype(bf16)

    grad_hidden, grad_attended, gain_two_part = call(
        hidden_back_kernel,
        "hidden_back",
        [out((block_rows, width), f32), out((block_rows, width), bf16), out((1, width), f32)],
        [hidden, grad_normed_two, grad_normed_two_got, cotangent, gain_second],
    )
    grad_attended_other = across(grad_attended, "core", 1)
    dqkv, gwo, diagonals, *grad_weights = call(
        functools.partial(attend_back_kernel, heads, parts),
        "attend_back",
        [
            out((seq, 3 * cols), bf16),
            out((width, cols), bf16),
            out((heads, 2 * seq), f32),
            *([out((width // parts, 3 * cols), bf16)] * parts),
        ],
        [ids, grad_attended, grad_attended_other, wo, qkv, probs, normed_seq, mixed],
        smem=1,
        scratch=[
            pltpu.VMEM((seq, width), bf16),
            pltpu.VMEM((seq, cols), bf16),
            pltpu.VMEM((seq, seq), bf16),
            pltpu.VMEM((width, 3 * cols), f32),
        ],
        flops=16 * heads * seq * seq * 256,
    )
    received_weights = trade(grad_weights)
    summed_weights = sum(r.reshape(-1, node_rows, 3 * cols).astype(f32).sum(0) for r in received_weights)
    summed_out = jnp.sum(trade_natural(gwo).astype(f32), axis=0)
    node_sums = jnp.concatenate([summed_weights, summed_out], axis=1)
    shard_rows = w_query.shape[0]
    sums_kept = lax.dynamic_slice_in_dim(node_sums, core * shard_rows, shard_rows, 0)
    sums_sent = lax.dynamic_slice_in_dim(node_sums, (1 - core) * shard_rows, shard_rows, 0)
    sums_got = across(sums_sent, "core", 1)

    def columns(index):
        mine = sums_kept[:, index * cols : (index + 1) * cols]
        theirs = sums_got[:, index * cols : (index + 1) * cols]
        return jnp.where(
            core == 0,
            jnp.concatenate([mine, theirs], axis=1),
            jnp.concatenate([theirs, mine], axis=1),
        )

    grad_kept, grad_sent = call(
        normed_back_kernel,
        "normed_back",
        [out((block_rows, width), f32), out((block_rows, width), bf16)],
        [ids, dqkv, wqkv],
        smem=1,
        flops=2 * seq * width * 3 * cols,
    )
    grad_normed = grad_kept + across(grad_sent, "core", 1).astype(f32)
    x_wide = x_rows.astype(f32)
    scale = lax.rsqrt(jnp.mean(x_wide * x_wide, axis=1, keepdims=True) + norm_eps)
    gain_one_part = jnp.sum(grad_normed * x_wide * scale, axis=0)
    grad_normed_got = across(half_of(grad_normed, 1 - side).astype(bf16), "tensor", 1)
    grad_normed_own = half_of(grad_normed, side) + grad_normed_got.astype(f32)
    x_own = tokens.astype(f32)
    norm_first, norm_pull_one = jax.vjp(lambda v: rms_scale(v, gain_first), x_own)
    input_grad = half_of(grad_hidden, side) + norm_pull_one(grad_normed_own)[0]

    bias_part = lax.dot_general(
        bucket_hot, diagonals, (((0,), (1,)), ((), ())), precision=exact, preferred_element_type=f32
    )
    bias_full = lax.dynamic_update_slice(
        jnp.zeros(bias_table.shape, f32), bias_part, (jnp.int32(0), head_start)
    )
    gain_two_part = jnp.where(side == 0, gain_two_part[0], 0.0)
    small = jnp.concatenate(
        [gain_one_part, gain_two_part, bias_full.reshape(-1), router_part.reshape(-1)]
    ).reshape(-1, 128)
    small = small + across(small, "core", 1)
    small = small + across(small, "tensor", 1)
    if direct:
        for bits in (1, 2, 4):
            small = small + across(small, "node", bits)
    else:
        small = lax.psum(small, "node")
    small = small.reshape(-1)
    bias_size = bias_table.size
    return (
        activations,
        input_grad,
        small[:width],
        columns(0),
        columns(1),
        columns(2),
        columns(3),
        small[2 * width : 2 * width + bias_size].reshape(bias_table.shape),
        small[width : 2 * width],
        small[2 * width + bias_size :].reshape(w_router.shape),
        grad_w_up_here,
        grad_w_down_here,
    )


def solution(mesh):
    dp, tensor = mesh.shape["dp"], mesh.shape["tensor"]
    grid = Mesh(mesh.devices.reshape(dp // GROUP, GROUP, tensor), ("node", "core", "tensor"))
    dp = ("node", "core")
    every = ("node", "core", "tensor")
    in_specs = (
        P(every, None),
        P(),
        P(dp, "tensor"),
        P(dp, "tensor"),
        P(dp, "tensor"),
        P(dp, "tensor"),
        P(),
        P(),
        P(),
        P(None, every),
        P(None, every),
        P(dp, None),
        P(),
        P(),
        P(dp, None),
    )
    out_specs = (
        P(every, None),
        P(every, None),
        P(),
        P(dp, "tensor"),
        P(dp, "tensor"),
        P(dp, "tensor"),
        P(dp, "tensor"),
        P(),
        P(),
        P(),
        P(None, every),
        P(None, every),
    )
    return jax.shard_map(
        per_device, mesh=grid, in_specs=in_specs, out_specs=out_specs, check_vma=False
    )
```

```python
import functools

import jax
import jax.numpy as jnp
from jax import lax
from jax.experimental import pallas as pl
from jax.experimental.pallas import tpu as pltpu
from jax.sharding import Mesh, PartitionSpec as P

HD = 64
GROUP = 2
DIRECT = 8
TILE = 128

norm_eps = 1e-06
masked_value = -1e30
exact = lax.Precision.HIGHEST
bf16 = jnp.bfloat16
f32 = jnp.float32

VMEM = pl.BlockSpec(memory_space=pltpu.VMEM)
SMEM = pl.BlockSpec(memory_space=pltpu.SMEM)
ANY = pl.BlockSpec(memory_space=pl.ANY)


def across(shard, axis, bits):
    return lax.ppermute(shard, axis, [(i, i ^ bits) for i in range(lax.axis_size(axis))])


def call(body, name, outs, args, smem=0, scratch=(), flops=0, after=()):
    held = [a for a in args] + list(outs)
    moved = sum(a.size * jnp.dtype(a.dtype).itemsize for a in held)
    kept = sum(padded_bytes(a) for a in held) + sum(padded_bytes(a) for a in scratch)
    count = len(args)

    def kernel(*refs):
        body(*refs[:count], *refs[count + len(after) :])

    return pl.pallas_call(
        kernel,
        name=name,
        out_shape=outs,
        in_specs=[SMEM] * smem + [VMEM] * (count - smem) + [ANY] * len(after),
        out_specs=[VMEM] * len(outs),
        scratch_shapes=scratch,
        compiler_params=pltpu.CompilerParams(vmem_limit_bytes=kept + 12 * 1024 * 1024),
        cost_estimate=pl.CostEstimate(flops=flops, bytes_accessed=moved, transcendentals=0),
    )(*args, *after)


def padded_bytes(array):
    *lead, rows, cols = (1, 1, *array.shape)
    size = jnp.dtype(array.dtype).itemsize
    for extent in lead:
        size *= extent
    return size * (-(-rows // 16) * 16) * (-(-cols // 128) * 128)


def out(shape, dtype):
    return jax.ShapeDtypeStruct(shape, dtype)


def mm(a, b):
    return jnp.dot(a, b, preferred_element_type=f32)


def mm_bt(a, b):
    return lax.dot_general(a, b, (((1,), (1,)), ((), ())), preferred_element_type=f32)


def mm_at(a, b):
    return lax.dot_general(a, b, (((0,), (0,)), ((), ())), preferred_element_type=f32)


def project_kernel(parts, ids, own_ref, other_ref, gain_ref, *refs):
    pieces = refs[:parts]
    wqkv_ref, wo_ref, x_ref, seq_ref, qkv_ref = refs[parts:]
    core = ids[0]
    me = ids[1]
    rows = pieces[0].shape[0]
    cols = wqkv_ref.shape[1]
    half = own_ref.shape[0]
    for place, source in ((core, own_ref), (1 - core, other_ref)):
        at = pl.ds(pl.multiple_of(place * half, half), half)
        x = source[...]
        x_ref[at, :] = x
        wide = x.astype(f32)
        scale = lax.rsqrt(jnp.mean(wide * wide, axis=1, keepdims=True) + norm_eps)
        seq_ref[at, :] = (wide * scale * gain_ref[...]).astype(bf16)
    for i, piece in enumerate(pieces):
        start = 0 if parts == 1 else pl.multiple_of((me ^ i) * rows, rows)
        wqkv_ref[pl.ds(start, rows), :] = piece[:, :cols]
        wo_ref[pl.ds(start, rows), :] = piece[:, cols:]
    for i in range(0, 2 * half, 256):
        qkv_ref[i : i + 256, :] = mm(seq_ref[i : i + 256, :], wqkv_ref[...]).astype(bf16)


def slots_kernel(table_ref, rows_ref, out_ref):
    out_ref[...] = mm(table_ref[...], rows_ref[...]).astype(bf16)


def cots_kernel(parts, ids, own_ref, other_ref, wdown_ref, cots_ref, back_ref, *scratch):
    slots = cots_ref.shape[0] // 2
    me = ids[1]
    for at, source in ((0, own_ref), (slots, other_ref)):
        if parts == 1:
            cots_ref[at : at + slots, :] = source[...]
        else:
            rows = slots // parts
            for i in range(parts):
                scratch[0][i * rows : (i + 1) * rows, :] = source[me ^ i].astype(f32)
            cots_ref[at : at + slots, :] = scratch[0][...].astype(bf16)
        back_ref[at : at + slots, :] = mm(cots_ref[at : at + slots, :], wdown_ref[...])


def attend_kernel(heads, ids, qkv_ref, vec_ref, row_docs, col_docs, *refs):
    mixed_ref, keep_ref, send_ref, *probs_refs = refs
    core = ids[0]
    seq = qkv_ref.shape[0]
    width = heads * HD
    half = seq // GROUP
    span = seq + TILE
    for h in range(heads):
        at = h * HD
        key = qkv_ref[:, width + at : width + at + HD]
        value = qkv_ref[:, 2 * width + at : 2 * width + at + HD]
        for i in range(0, seq, TILE):
            base = seq - TILE - i
            seg = jnp.broadcast_to(vec_ref[h : h + 1, base : base + span], (TILE, span))
            bias = pltpu.roll(seg, span - TILE + 1, 1, stride=1, stride_axis=0)[:, :seq]
            scores = mm_bt(qkv_ref[i : i + TILE, at : at + HD], key) * HD**-0.5 + bias
            scores = jnp.where(row_docs[i : i + TILE, :] == col_docs[...], scores, masked_value)
            peak = jnp.max(scores, axis=1, keepdims=True)
            exp_scores = jnp.exp(scores - peak)
            probs = exp_scores / jnp.sum(exp_scores, axis=1, keepdims=True)
            probs_refs[h][i : i + TILE, :] = probs
            mixed_ref[i : i + TILE, at : at + HD] = mm(probs.astype(bf16), value).astype(bf16)
    keep_ref[...] = mixed_ref[pl.ds(pl.multiple_of(core * half, half), half), :]
    send_ref[...] = mixed_ref[pl.ds(pl.multiple_of((1 - core) * half, half), half), :]


def attended_kernel(keep_ref, got_ref, wo_ref, wo_other_ref, out_ref):
    total = mm_bt(keep_ref[...], wo_ref[...]) + mm_bt(got_ref[...], wo_other_ref[...])
    out_ref[...] = total.astype(bf16)


def dispatch_kernel(x_ref, own_ref, got_ref, gain_ref, table_ref, hidden_ref, *blocks):
    hidden = x_ref[...].astype(f32) + (own_ref[...].astype(f32) + got_ref[...].astype(f32))
    hidden_ref[...] = hidden
    scale = lax.rsqrt(jnp.mean(hidden * hidden, axis=1, keepdims=True) + norm_eps)
    normed = (hidden * scale * gain_ref[...]).astype(bf16)
    slots = mm(table_ref[...], normed)
    rows = blocks[0].shape[0]
    for i, block in enumerate(blocks):
        block[...] = slots[i * rows : (i + 1) * rows, :].astype(bf16)


def expert_kernel(ids, own_ref, other_ref, h_ref, wup_ref, wr_ref, *refs):
    active_ref, gup_ref, chosen_ref, keep_ref, send_ref, router_ref = refs
    rows = own_ref.shape[0]
    step = rows // 2
    router = jnp.zeros(router_ref.shape, f32)
    root = 0.7978845608028654
    for i in range(0, 2 * rows, step):
        src = own_ref if i < rows else other_ref
        at = i % rows
        slots = src[at : at + step, :]
        logits = mm(slots, wr_ref[...])
        peak = jnp.max(logits, axis=1, keepdims=True)
        exp_logits = jnp.exp(logits - peak)
        gates = exp_logits / jnp.sum(exp_logits, axis=1, keepdims=True)
        mine = lax.broadcasted_iota(jnp.int32, gates.shape, 1) == ids[1]
        chosen = jnp.sum(jnp.where(mine, gates, 0.0), axis=1, keepdims=True)
        chosen_ref[i : i + step, :] = chosen
        up = mm(slots, wup_ref[...])
        square = up * up
        bent = jnp.tanh(root * (up + 0.044715 * up * square))
        low = (0.5 * up * (1.0 + bent)).astype(bf16)
        active_ref[i : i + step, :] = low
        slope = 0.5 * (1.0 + bent) + 0.5 * up * (1.0 - bent * bent) * root * (
            1.0 + 3.0 * 0.044715 * square
        )
        back = h_ref[i : i + step, :]
        gup = (chosen * back * slope).astype(bf16)
        gup_ref[i : i + step, :] = gup
        grad_chosen = jnp.sum(low.astype(f32) * back, axis=1, keepdims=True)
        grad_logits = gates * (jnp.where(mine, 1.0, 0.0) - chosen) * grad_chosen
        grad_logits = grad_logits.astype(bf16)
        router = router + mm_at(grad_logits, slots)
        grad = mm_bt(gup, wup_ref[...]) + mm_bt(grad_logits, wr_ref[...])
        if i < rows:
            keep_ref[at : at + step, :] = grad
        else:
            send_ref[at : at + step, :] = grad.astype(bf16)
    router_ref[...] = router


def expert_rest_kernel(own_ref, other_ref, cots_ref, active_ref, gup_ref, chosen_ref, wdown_ref, *refs):
    keep_ref, send_ref, gwup_ref, gwdown_ref = refs
    rows = own_ref.shape[0]
    result = mm_bt(active_ref[...], wdown_ref[...]) * chosen_ref[...]
    keep_ref[...] = result[:rows, :]
    send_ref[...] = result[rows:, :].astype(bf16)
    gwup_ref[...] = mm_at(own_ref[...], gup_ref[:rows, :]) + mm_at(other_ref[...], gup_ref[rows:, :])
    grads = (chosen_ref[...] * cots_ref[...].astype(f32)).astype(bf16)
    gwdown_ref[...] = mm_at(grads, active_ref[...])


def join_kernel(keep_ref, got_ref, *blocks):
    total = keep_ref[...] + got_ref[...].astype(f32)
    rows = blocks[0].shape[0]
    for i, block in enumerate(blocks):
        block[...] = total[i * rows : (i + 1) * rows, :].astype(bf16)


def join_natural_kernel(parts, ids, keep_ref, got_ref, out_ref):
    total = keep_ref[...] + got_ref[...].astype(f32)
    if parts == 1:
        out_ref[...] = total.astype(bf16)
        return
    rows = out_ref.shape[1]
    for i in range(parts):
        out_ref[ids[1] ^ i] = total[i * rows : (i + 1) * rows, :].astype(bf16)


def gather_kernel(back_table_ref, *refs):
    blocks = refs[:-1]
    slots = jnp.concatenate([b[...].astype(f32) for b in blocks], axis=0).astype(bf16)
    refs[-1][...] = mm(back_table_ref[...], slots).astype(bf16)


def hidden_back_kernel(hidden_ref, own_ref, got_ref, cot_ref, gain_ref, grad_ref, low_ref, dgain_ref):
    hidden = hidden_ref[...]
    grad_normed = own_ref[...].astype(f32) + got_ref[...].astype(f32)
    scale = lax.rsqrt(jnp.mean(hidden * hidden, axis=1, keepdims=True) + norm_eps)
    dgain_ref[...] = jnp.sum(grad_normed * hidden * scale, axis=0, keepdims=True)
    pulled = gain_ref[...] * grad_normed
    inner = jnp.mean(pulled * hidden, axis=1, keepdims=True)
    grad = cot_ref[...].astype(f32) + scale * pulled - hidden * (scale * scale * scale) * inner
    grad_ref[...] = grad
    low_ref[...] = grad.astype(bf16)


def heads_back(heads, first, qkv_ref, gm_ref, probs, dqkv_ref, diag_ref, ds_ref):
    seq = qkv_ref.shape[0]
    width = heads * HD
    here = len(probs) * HD
    span = seq + TILE
    flip = (
        lax.broadcasted_iota(jnp.int32, (TILE, TILE), 0)
        + lax.broadcasted_iota(jnp.int32, (TILE, TILE), 1)
        == TILE - 1
    ).astype(bf16)
    for h, probs_ref in enumerate(probs):
        at = (first + h) * HD
        to = h * HD
        key = qkv_ref[:, width + at : width + at + HD]
        value = qkv_ref[:, 2 * width + at : 2 * width + at + HD]
        for i in range(0, seq, TILE):
            probs_rows = probs_ref[i : i + TILE, :]
            grad_probs = mm_bt(gm_ref[i : i + TILE, at : at + HD], value)
            inner = jnp.sum(probs_rows * grad_probs, axis=1, keepdims=True)
            grad_scores = (probs_rows * (grad_probs - inner)).astype(bf16)
            ds_ref[i : i + TILE, :] = grad_scores
            dqkv_ref[i : i + TILE, to : to + HD] = (mm(grad_scores, key) * HD**-0.5).astype(bf16)
            flipped = mm(flip, grad_scores)
            padded = jnp.concatenate([flipped, jnp.zeros((TILE, TILE), f32)], axis=1)
            skewed = pltpu.roll(padded, 0, 1, stride=1, stride_axis=0)
            base = seq - TILE - i
            row = first + h
            diag_ref[row : row + 1, base : base + span] += jnp.sum(skewed, axis=0, keepdims=True)
        dqkv_ref[:, here + to : here + to + HD] = (
            mm_at(ds_ref[...], qkv_ref[:, at : at + HD]) * HD**-0.5
        ).astype(bf16)
        dqkv_ref[:, 2 * here + to : 2 * here + to + HD] = mm_at(
            probs_ref[...].astype(bf16), gm_ref[:, at : at + HD]
        ).astype(bf16)


def send_rows(parts, me, gw_ref, outs):
    if parts == 1:
        outs[0][...] = gw_ref[...].astype(bf16)
        return
    rows = gw_ref.shape[0] // parts
    for i in range(parts // 2):
        at = slice(i * rows, (i + 1) * rows)
        outs[0][at, :] = gw_ref[pl.ds(pl.multiple_of((me ^ 2 * i) * rows, rows), rows), :]
        there = pl.ds(pl.multiple_of((me ^ 2 * i ^ 1) * rows, rows), rows)
        outs[1][at, :] = gw_ref[there, :].astype(bf16)


def first_back_kernel(heads, parts, ids, own_ref, other_ref, wo_ref, qkv_ref, probs_ref, seq_ref, mixed_ref, *refs):
    gm_ref, dqkv_ref, diag_ref, *outs = refs[:-3]
    ga_ref, ds_ref, gw_ref = refs[-3:]
    core = ids[0]
    half = own_ref.shape[0]
    ga_ref[pl.ds(pl.multiple_of(core * half, half), half), :] = own_ref[...]
    ga_ref[pl.ds(pl.multiple_of((1 - core) * half, half), half), :] = other_ref[...]
    gm_ref[...] = mm(ga_ref[...], wo_ref[...]).astype(bf16)
    diag_ref[...] = jnp.zeros_like(diag_ref)
    heads_back(heads, 0, qkv_ref, gm_ref, [probs_ref], dqkv_ref, diag_ref, ds_ref)
    cut = dqkv_ref.shape[1]
    gw_ref[:, :cut] = mm_at(seq_ref[...], dqkv_ref[...])
    gw_ref[:, cut:] = mm_at(ga_ref[...], mixed_ref[...])
    send_rows(parts, ids[1], gw_ref, outs)


def second_back_kernel(
    heads, parts, ids, gm_ref, qkv_ref, first_ref, diag_in_ref, hot_ref, x_ref, seq_ref, wqkv_ref, gain_ref, router_ref, *refs
):
    probs = refs[: heads - 1]
    keep_ref, send_ref, small_ref, *outs = refs[heads - 1 : -5]
    diag_ref, dqkv_ref, all_ref, ds_ref, gw_ref = refs[-5:]
    core, me, side = ids[0], ids[1], ids[2]
    half = keep_ref.shape[0]
    diag_ref[...] = diag_in_ref[...]
    heads_back(heads, 1, qkv_ref, gm_ref, probs, dqkv_ref, diag_ref, ds_ref)
    gw_ref[...] = mm_at(seq_ref[...], dqkv_ref[...])
    send_rows(parts, me, gw_ref, outs)
    rest = (heads - 1) * HD
    for i in range(3):
        at = i * heads * HD
        all_ref[:, at : at + HD] = first_ref[:, i * HD : (i + 1) * HD]
        all_ref[:, at + HD : at + heads * HD] = dqkv_ref[:, i * rest : (i + 1) * rest]
    gain = jnp.zeros((1, x_ref.shape[1]), f32)
    for place, mine in ((core, True), (1 - core, False)):
        rows = pl.ds(pl.multiple_of(place * half, half), half)
        grad = mm_bt(all_ref[rows, :], wqkv_ref[...])
        wide = x_ref[rows, :].astype(f32)
        scale = lax.rsqrt(jnp.mean(wide * wide, axis=1, keepdims=True) + norm_eps)
        gain = gain + jnp.sum(grad * wide * scale, axis=0, keepdims=True)
        if mine:
            keep_ref[...] = grad
        else:
            send_ref[...] = grad.astype(bf16)
    small_ref[...] = jnp.zeros_like(small_ref)
    small_ref[0:1, :] = gain
    small_ref[1:2, :] = jnp.where(side == 0, gain_ref[...], 0.0)
    experts = router_ref.shape[0]
    small_ref[2 : 2 + experts, :] = router_ref[...]
    bias = jnp.dot(diag_ref[...], hot_ref[...], precision=exact, preferred_element_type=f32)
    lanes = bias.shape[1]
    for i in range(2 * GROUP):
        small_ref[2 + experts : 2 + experts + heads, i * lanes : (i + 1) * lanes] = jnp.where(
            side * GROUP + core == i, bias[:heads, :], 0.0
        )


def fold_kernel(keep_ref, got_ref, own_ref, *sends):
    total = keep_ref[...] + got_ref[...].astype(f32)
    rows = own_ref.shape[0]
    own_ref[...] = total[:rows, :]
    for i, send in enumerate(sends):
        send[...] = total[(i + 1) * rows : (i + 2) * rows, :].astype(bf16)


def fold_small_kernel(keep_ref, got_ref, small_ref, small_got_ref, own_ref, *sends):
    total = keep_ref[...] + got_ref[...].astype(f32)
    rows = keep_ref.shape[0] // (len(sends) + 1)
    cols = own_ref.shape[1]
    small = small_ref[...] + small_got_ref[...]
    high = small.shape[0]
    for i, block in enumerate((own_ref, *sends)):
        block[:rows, :] = total[i * rows : (i + 1) * rows, :].astype(block.dtype)
        block[rows : rows + high, :] = small[:, :cols].astype(bf16).astype(block.dtype)
        block[rows + high :, :] = small[:, cols:].astype(bf16).astype(block.dtype)


def sum_nodes_kernel(ids, *refs):
    first, second = refs[:4], refs[4:8]
    keep_ref, send_ref, small_ref = refs[8:]
    core = ids[0]
    rows = keep_ref.shape[0]
    cols = keep_ref.shape[1] // 2

    def part(group, at):
        a, b, c, d = (r[at, :].astype(f32) for r in group)
        return (a + b) + (c + d)

    mine = pl.ds(pl.multiple_of(core * rows, rows), rows)
    theirs = pl.ds(pl.multiple_of((1 - core) * rows, rows), rows)
    keep_ref[:, :cols] = part(first, mine)
    keep_ref[:, cols:] = part(second, mine)
    send_ref[:, :cols] = part(first, theirs)
    send_ref[:, cols:] = part(second, theirs)
    high = small_ref.shape[0]
    small_ref[:, :cols] = part(second, slice(2 * rows, 2 * rows + high))
    small_ref[:, cols:] = part(second, slice(2 * rows + high, 2 * rows + 2 * high))


def columns_kernel(heads, ids, keep_ref, got_ref, *outs):
    core = ids[0]
    cols = heads * HD
    rest = cols - HD
    zero = core == 0
    pair = (jnp.where(zero, keep_ref[...], got_ref[...]), jnp.where(zero, got_ref[...], keep_ref[...]))
    middle = keep_ref.shape[1] // 2
    for c, part in enumerate(pair):
        at = c * cols
        for i in range(3):
            outs[i][:, at : at + HD] = part[:, i * HD : (i + 1) * HD]
            start = middle + i * rest
            outs[i][:, at + HD : at + cols] = part[:, start : start + rest]
        outs[3][:, at : at + cols] = part[:, 3 * HD : 3 * HD + cols]


def input_kernel(keep_ref, got_ref, grad_ref, x_ref, gain_ref, out_ref):
    grad_normed = keep_ref[...] + got_ref[...].astype(f32)
    wide = x_ref[...].astype(f32)
    scale = lax.rsqrt(jnp.mean(wide * wide, axis=1, keepdims=True) + norm_eps)
    pulled = gain_ref[...] * grad_normed
    inner = jnp.mean(pulled * wide, axis=1, keepdims=True)
    out_ref[...] = grad_ref[...] + scale * pulled - wide * (scale * scale * scale) * inner


def in_order(first, mine, other):
    return jnp.where(first, jnp.concatenate([mine, other]), jnp.concatenate([other, mine]))


def per_device(
    tokens,
    gain_one,
    w_query,
    w_key,
    w_value,
    w_out,
    bias_table,
    gain_two,
    w_router,
    w_up,
    w_down,
    routes,
    doc_lengths,
    buckets,
    cotangent,
):
    own_rows, width = tokens.shape
    block_rows = routes.shape[0]
    seq = block_rows * GROUP
    cols = w_query.shape[1] // GROUP
    heads = cols // HD
    experts = w_router.shape[1]
    capacity = max(2, (5 * block_rows + 4 * experts - 1) // (4 * experts))
    slots = experts * capacity
    nodes = lax.axis_size("node")
    core = lax.axis_index("core")
    side = lax.axis_index("tensor")
    me = lax.axis_index("node")
    direct = nodes == DIRECT
    parts = nodes if direct else 1
    ids = jnp.stack([core, me, side]).astype(jnp.int32)
    node_rows = width // nodes

    def trade(blocks):
        if direct:
            return [blocks[0]] + [across(blocks[i], "node", i) for i in range(1, nodes)]
        stacked = blocks[0].reshape(nodes, -1, blocks[0].shape[1])
        back = lax.all_to_all(stacked, "node", split_axis=0, concat_axis=0, tiled=True)
        return [back.reshape(blocks[0].shape)]

    def trade_natural(rows):
        stacked = rows.reshape(nodes, -1, rows.shape[-1])
        return lax.all_to_all(stacked, "node", split_axis=0, concat_axis=0, tiled=True)

    shares = jnp.stack([w_query, w_key, w_value, w_out]).reshape(4, -1, GROUP, cols)
    shares = jnp.moveaxis(shares, 0, 2).reshape(-1, GROUP, 4 * cols)
    share_kept = lax.dynamic_index_in_dim(shares, core, 1, keepdims=False)
    share_sent = lax.dynamic_index_in_dim(shares, 1 - core, 1, keepdims=False)
    piece = in_order(core == 0, share_kept, across(share_sent, "core", 1))
    if direct:
        pieces = {0: piece}
        for i in (2, 4, 6):
            pieces[i] = across(piece, "node", i)
        for i in (0, 2, 4, 6):
            pieces[i + 1] = across(pieces[i], "node", 1)
        pieces = [pieces[i] for i in range(nodes)]
    else:
        pieces = [lax.all_gather(piece, "node", axis=0, tiled=True)]

    x_rows = in_order(side == 0, tokens, across(tokens, "tensor", 1))
    x_other = across(x_rows, "core", 1)
    gain_first = gain_one.astype(f32)[None, :]
    gain_second = gain_two.astype(f32)[None, :]

    expert_ids = routes[:, 0]
    picks = (expert_ids[:, None] == jnp.arange(experts, dtype=jnp.int32)[None, :]).astype(jnp.int32)
    slot_index = jnp.sum((jnp.cumsum(picks, axis=0) - 1) * picks, axis=1)
    target = expert_ids * capacity + slot_index
    codes = jnp.arange(slots, dtype=jnp.int32)
    turned = ((codes // capacity) ^ me) * capacity + codes % capacity if direct else codes
    table = (turned[:, None] == target[None, :]).astype(bf16)
    back_table = (target[:, None] == turned[None, :]).astype(bf16)
    plain_table = (codes[:, None] == target[None, :]).astype(bf16)

    natural = (nodes, slots // nodes, width) if direct else (slots, width)
    cot_slots = call(
        slots_kernel,
        "cot_slots",
        [out((slots, width), bf16)],
        [plain_table, cotangent],
        flops=2 * slots * block_rows * width,
        after=[pieces[min(2, parts - 1)]],
    )[0]
    cots_own = trade_natural(cot_slots).reshape(natural)
    cots, back_active = call(
        functools.partial(cots_kernel, parts),
        "cots",
        [out((2 * slots, width), bf16), out((2 * slots, w_down.shape[1]), f32)],
        [ids, cots_own, across(cots_own, "core", 1), w_down],
        smem=1,
        scratch=[pltpu.VMEM((slots, width), f32)] if direct else [],
        flops=4 * slots * width * w_down.shape[1],
    )

    lengths_row = lax.dynamic_slice_in_dim(doc_lengths, me, 1, 0)[0]
    ends = jnp.cumsum(lengths_row)
    places = jnp.arange(seq, dtype=jnp.int32)
    docs = jnp.sum((ends[None, :] <= places[:, None]).astype(jnp.int32), axis=1)
    bucket_count = bias_table.shape[0]
    bucket_hot = (
        jnp.pad(buckets, (0, 1))[:, None] == jnp.arange(128, dtype=jnp.int32)[None, :]
    ).astype(f32)
    head_start = (side * GROUP + core) * heads
    bias_here = lax.dynamic_slice_in_dim(bias_table, head_start, heads, 1)
    bias_here = jnp.pad(bias_here, ((0, 128 - bucket_count), (0, 0)))
    bias_vectors = lax.dot_general(
        bias_here, bucket_hot, (((0,), (1,)), ((), ())), precision=exact, preferred_element_type=f32
    )

    wqkv, wo, x_seq, normed_seq, qkv = call(
        functools.partial(project_kernel, parts),
        "project",
        [
            out((width, 3 * cols), bf16),
            out((width, cols), bf16),
            out((seq, width), bf16),
            out((seq, width), bf16),
            out((seq, 3 * cols), bf16),
        ],
        [ids, x_rows, x_other, gain_first, *pieces],
        smem=1,
        flops=2 * seq * width * 3 * cols,
    )
    wo_other = across(wo, "core", 1)
    mixed, mixed_kept, mixed_sent, *probs = call(
        functools.partial(attend_kernel, heads),
        "attend",
        [
            out((seq, cols), bf16),
            out((block_rows, cols), bf16),
            out((block_rows, cols), bf16),
            *([out((seq, seq), f32)] * heads),
        ],
        [ids, qkv, bias_vectors, docs[:, None], docs[None, :]],
        smem=1,
        flops=8 * heads * seq * seq * 256,
    )
    mixed_got = across(mixed_sent, "core", 1)
    attended = call(
        attended_kernel,
        "attended",
        [out((block_rows, width), bf16)],
        [mixed_kept, mixed_got, wo, wo_other],
        flops=4 * block_rows * width * cols,
    )[0]
    attended_got = across(attended, "tensor", 1)

    block_shapes = [out((slots // parts, width), bf16)] * parts
    hidden, *blocks = call(
        dispatch_kernel,
        "dispatch",
        [out((block_rows, width), f32), *block_shapes],
        [x_rows, attended, attended_got, gain_second, table],
        flops=2 * slots * block_rows * width,
    )
    received = trade(blocks)
    slots_own = jnp.concatenate(received)
    slots_other = across(slots_own, "core", 1)
    active, grad_upward, chosen, grad_kept, grad_sent, router_part = call(
        expert_kernel,
        "expert",
        [
            out((2 * slots, w_up.shape[1]), bf16),
            out((2 * slots, w_up.shape[1]), bf16),
            out((2 * slots, 1), f32),
            out((slots, width), f32),
            out((slots, width), bf16),
            out(w_router.shape[::-1], f32),
        ],
        [ids, slots_own, slots_other, back_active, w_up, w_router],
        smem=1,
        flops=8 * slots * width * w_up.shape[1],
    )
    grad_blocks = call(
        join_kernel, "join_grad", block_shapes, [grad_kept, across(grad_sent, "core", 1)]
    )
    grad_back = trade(grad_blocks)
    grad_normed_two = call(
        gather_kernel,
        "gather_grad",
        [out((block_rows, width), bf16)],
        [back_table, *grad_back],
        flops=2 * slots * block_rows * width,
    )[0]
    grad_normed_two_got = across(grad_normed_two, "tensor", 1)

    out_kept, out_sent, grad_w_up_here, grad_w_down_here = call(
        expert_rest_kernel,
        "expert_rest",
        [
            out((slots, width), f32),
            out((slots, width), bf16),
            out(w_up.shape, f32),
            out(w_down.shape, f32),
        ],
        [slots_own, slots_other, cots, active, grad_upward, chosen, w_down],
        flops=12 * slots * width * w_up.shape[1],
        after=grad_blocks[-1:],
    )
    out_slots = call(
        functools.partial(join_natural_kernel, parts),
        "join_out",
        [out(natural, bf16)],
        [ids, out_kept, across(out_sent, "core", 1)],
        smem=1,
        after=[grad_normed_two],
    )[0]
    out_back = trade_natural(out_slots.reshape(slots, width)).reshape(slots, width)
    returned = lax.dot_general(
        plain_table, out_back, (((0,), (0,)), ((), ())), preferred_element_type=f32
    ).astype(bf16)

    def half_of(rows, index):
        return lax.dynamic_slice_in_dim(rows, index * own_rows, own_rows, 0)

    returned_got = across(half_of(returned, 1 - side), "tensor", 1)
    activations = (
        half_of(hidden, side) + (half_of(returned, side).astype(f32) + returned_got.astype(f32))
    ).astype(bf16)

    grad_hidden, grad_attended, gain_two_part = call(
        hidden_back_kernel,
        "hidden_back",
        [out((block_rows, width), f32), out((block_rows, width), bf16), out((1, width), f32)],
        [hidden, grad_normed_two, grad_normed_two_got, cotangent, gain_second],
    )
    grad_attended_other = across(grad_attended, "core", 1)
    chunk = 3 * HD + cols
    other_chunk = 3 * (cols - HD)
    if direct:
        half_width = width // 2
        chunk_shapes = [[out((half_width, c), f32), out((half_width, c), bf16)] for c in (chunk, other_chunk)]
    else:
        chunk_shapes = [[out((width, c), bf16)] for c in (chunk, other_chunk)]
    grad_mixed, first_dqkv, diagonals, *first_chunk = call(
        functools.partial(first_back_kernel, heads, parts),
        "first_back",
        [
            out((seq, cols), bf16),
            out((seq, 3 * HD), bf16),
            out((8, 2 * seq), f32),
            *chunk_shapes[0],
        ],
        [ids, grad_attended, grad_attended_other, wo, qkv, probs[0], normed_seq, mixed],
        smem=1,
        scratch=[
            pltpu.VMEM((seq, width), bf16),
            pltpu.VMEM((seq, seq), bf16),
            pltpu.VMEM((width, chunk), f32),
        ],
        flops=16 * seq * seq * 256,
    )
    small_rows = -(-(2 + experts + heads) // 16) * 16
    grad_kept, grad_sent, small, *second_chunk = call(
        functools.partial(second_back_kernel, heads, parts),
        "second_back",
        [
            out((block_rows, width), f32),
            out((block_rows, width), bf16),
            out((small_rows, width), f32),
            *chunk_shapes[1],
        ],
        [
            ids,
            grad_mixed,
            qkv,
            first_dqkv,
            diagonals,
            bucket_hot,
            x_seq,
            normed_seq,
            wqkv,
            gain_two_part,
            router_part,
            *probs[1:],
        ],
        smem=1,
        scratch=[
            pltpu.VMEM((8, 2 * seq), f32),
            pltpu.VMEM((seq, other_chunk), bf16),
            pltpu.VMEM((seq, 3 * cols), bf16),
            pltpu.VMEM((seq, seq), bf16),
            pltpu.VMEM((width, other_chunk), f32),
        ],
        flops=16 * (heads - 1) * seq * seq * 256,
    )

    shard_rows = w_query.shape[0]
    if direct:
        own_one, *send_one = call(
            fold_kernel,
            "fold_first",
            [out((node_rows, chunk), f32), *([out((node_rows, chunk), bf16)] * 3)],
            [first_chunk[0], across(first_chunk[1], "node", 1)],
        )
        got_one = [across(b, "node", 2 * i + 2) for i, b in enumerate(send_one)]
        small = small + across(small, "tensor", 1)
        small = small + across(small, "core", 1)
        tall = node_rows + 2 * small_rows
        own_two, *send_two = call(
            fold_small_kernel,
            "fold_second",
            [out((tall, other_chunk), f32), *([out((tall, other_chunk), bf16)] * 3)],
            [second_chunk[0], across(second_chunk[1], "node", 1), small, across(small, "node", 1)],
        )
        got_two = [across(b, "node", 2 * i + 2) for i, b in enumerate(send_two)]
        sums_kept, sums_sent, small = call(
            sum_nodes_kernel,
            "sum_nodes",
            [
                out((shard_rows, 2 * chunk), f32),
                out((shard_rows, 2 * chunk), f32),
                out((small_rows, width), f32),
            ],
            [ids, own_one, *got_one, own_two, *got_two],
            smem=1,
        )
    else:
        sums = jnp.concatenate(
            [
                jnp.sum(trade_natural(c[0]).astype(f32), axis=0)
                for c in (first_chunk, second_chunk)
            ],
            axis=1,
        )
        sums_kept = lax.dynamic_slice_in_dim(sums, core * shard_rows, shard_rows, 0)
        sums_sent = lax.dynamic_slice_in_dim(sums, (1 - core) * shard_rows, shard_rows, 0)
        small = lax.psum(small, ("node", "core", "tensor"))
    weight_grads = call(
        functools.partial(columns_kernel, heads),
        "columns",
        [out(w_query.shape, f32)] * 4,
        [ids, sums_kept, across(sums_sent, "core", 1)],
        smem=1,
    )

    grad_normed = grad_kept + across(grad_sent, "core", 1).astype(f32)
    grad_normed_got = across(half_of(grad_normed, 1 - side).astype(bf16), "tensor", 1)
    input_grad = call(
        input_kernel,
        "input_grad",
        [out((own_rows, width), f32)],
        [
            half_of(grad_normed, side),
            grad_normed_got,
            half_of(grad_hidden, side),
            tokens,
            gain_first,
        ],
    )[0]
    bias_rows = small[2 + experts : 2 + experts + heads, : 4 * 128].reshape(heads, 4, 128)
    grad_bias = bias_rows[:, :, :bucket_count].transpose(2, 1, 0).reshape(bias_table.shape)
    return (
        activations,
        input_grad,
        small[0],
        *weight_grads,
        grad_bias,
        small[1],
        small[2 : 2 + experts].T,
        grad_w_up_here,
        grad_w_down_here,
    )


def solution(mesh):
    dp, tensor = mesh.shape["dp"], mesh.shape["tensor"]
    grid = Mesh(mesh.devices.reshape(dp // GROUP, GROUP, tensor), ("node", "core", "tensor"))
    dp = ("node", "core")
    every = ("node", "core", "tensor")
    in_specs = (
        P(every, None),
        P(),
        P(dp, "tensor"),
        P(dp, "tensor"),
        P(dp, "tensor"),
        P(dp, "tensor"),
        P(),
        P(),
        P(),
        P(None, every),
        P(None, every),
        P(dp, None),
        P(),
        P(),
        P(dp, None),
    )
    out_specs = (
        P(every, None),
        P(every, None),
        P(),
        P(dp, "tensor"),
        P(dp, "tensor"),
        P(dp, "tensor"),
        P(dp, "tensor"),
        P(),
        P(),
        P(),
        P(None, every),
        P(None, every),
    )
    return jax.shard_map(
        per_device, mesh=grid, in_specs=in_specs, out_specs=out_specs, check_vma=False
    )
```

```python
import functools

import jax
import jax.numpy as jnp
from jax import lax
from jax.experimental import pallas as pl
from jax.experimental.pallas import tpu as pltpu
from jax.sharding import Mesh, PartitionSpec as P

HD = 64
GROUP = 2
FLOPS1 = 0
FLOPS2 = 0
DIRECT = 8
TILE = 128

norm_eps = 1e-06
masked_value = -1e30
exact = lax.Precision.HIGHEST
bf16 = jnp.bfloat16
f32 = jnp.float32

VMEM = pl.BlockSpec(memory_space=pltpu.VMEM)
SMEM = pl.BlockSpec(memory_space=pltpu.SMEM)
ANY = pl.BlockSpec(memory_space=pl.ANY)


def across(shard, axis, bits):
    return lax.ppermute(shard, axis, [(i, i ^ bits) for i in range(lax.axis_size(axis))])


class Near:
    def __init__(self, array):
        self.array = array


class Raw(Near):
    pass


class Far(Raw):
    pass


def call(body, name, outs, args, smem=0, scratch=(), flops=0):
    arrays = [a.array if isinstance(a, Near) else a for a in args]
    results = [o.array if isinstance(o, Near) else o for o in outs]
    kept = sum(padded_bytes(a) for a in [*arrays, *results, *scratch] if is_plain(a))
    space = {Near: pltpu.VMEM, Far: pltpu.HBM}
    given = [
        pltpu.with_memory_space_constraint(x, space[type(a)]) if type(a) in space else x
        for a, x in zip(args, arrays)
    ]
    return pl.pallas_call(
        body,
        name=name,
        out_shape=[
            space[type(o)](x.shape, x.dtype) if type(o) in space else x
            for o, x in zip(outs, results)
        ],
        in_specs=[SMEM] * smem + [ANY if isinstance(a, Raw) else VMEM for a in args[smem:]],
        out_specs=[ANY if isinstance(o, Raw) else VMEM for o in outs],
        scratch_shapes=scratch,
        compiler_params=pltpu.CompilerParams(vmem_limit_bytes=kept + 10 * 1024 * 1024),
        cost_estimate=pl.CostEstimate(flops=flops, bytes_accessed=0, transcendentals=0),
    )(*given)


def is_plain(array):
    return array.dtype in (bf16, f32, jnp.int32)


def padded_bytes(array):
    *lead, rows, cols = (1, 1, *array.shape)
    size = jnp.dtype(array.dtype).itemsize
    for extent in lead:
        size *= extent
    return size * (-(-rows // 16) * 16) * (-(-cols // 128) * 128)


def out(shape, dtype):
    return jax.ShapeDtypeStruct(shape, dtype)


def mm(a, b):
    return jnp.dot(a, b, preferred_element_type=f32)


def mm_bt(a, b):
    return lax.dot_general(a, b, (((1,), (1,)), ((), ())), preferred_element_type=f32)


def mm_at(a, b):
    return lax.dot_general(a, b, (((0,), (0,)), ((), ())), preferred_element_type=f32)


def shares_kernel(ids, *refs):
    weights, (keep_ref, send_ref, near_ref, sems) = refs[:4], refs[4:]
    copies = [
        pltpu.make_async_copy(w, near_ref.at[i], sems.at[i]) for i, w in enumerate(weights)
    ]
    for copy in copies:
        copy.start()
    for copy in copies:
        copy.wait()
    first = ids[0] == 0
    cols = keep_ref.shape[1] // 4
    for i in range(4):
        low, high = near_ref[i, :, :cols], near_ref[i, :, cols:]
        keep_ref[:, i * cols : (i + 1) * cols] = jnp.where(first, low, high)
        send_ref[:, i * cols : (i + 1) * cols] = jnp.where(first, high, low)


def rows_kernel(ids, own_ref, got_ref, held_ref, out_ref):
    rows = own_ref.shape[0]
    out_ref[pl.ds(pl.multiple_of(ids[2] * rows, rows), rows), :] = own_ref[...]
    out_ref[pl.ds(pl.multiple_of((1 - ids[2]) * rows, rows), rows), :] = got_ref[...]


def move_kernel(count, *refs):
    sources, targets, sems = refs[:count], refs[-count - 1 : -1], refs[-1]
    copies = [
        pltpu.make_async_copy(a, b, sems.at[i]) for i, (a, b) in enumerate(zip(sources, targets))
    ]
    for copy in copies:
        copy.start()
    for copy in copies:
        copy.wait()


def unit_rows(x):
    wide = x.astype(f32)
    return wide * lax.rsqrt(jnp.mean(wide * wide, axis=1, keepdims=True) + norm_eps)


def slots_kernel(table_ref, rows_ref, held_ref, out_ref):
    out_ref[...] = mm(table_ref[...], rows_ref[...]).astype(bf16)


def cots_kernel(parts, ids, own_ref, other_ref, wdown_ref, held_ref, cots_ref, back_ref, *scratch):
    slots = cots_ref.shape[0] // 2
    me = ids[1]
    for at, source in ((0, own_ref), (slots, other_ref)):
        if parts == 1:
            cots_ref[at : at + slots, :] = source[...]
        else:
            rows = slots // parts
            for i in range(parts):
                scratch[0][i * rows : (i + 1) * rows, :] = source[me ^ i].astype(f32)
            cots_ref[at : at + slots, :] = scratch[0][...].astype(bf16)
        back_ref[at : at + slots, :] = mm(cots_ref[at : at + slots, :], wdown_ref[...])


def attend_kernel(heads, parts, ids, own_ref, other_ref, gain_ref, vec_ref, row_docs, col_docs, *refs):
    pieces = refs[:parts]
    w_ref, wo_ref, x_ref, qkv_ref, mixed_ref, keep_ref, send_ref, *probs_refs = refs[parts:-1]
    seq_ref = refs[-1]
    core = ids[0]
    me = ids[1]
    seq = x_ref.shape[0]
    width = heads * HD
    half = seq // GROUP
    span = seq + TILE
    rows = pieces[0].shape[0]
    for i, piece in enumerate(pieces):
        start = 0 if parts == 1 else pl.multiple_of((me ^ i) * rows, rows)
        w_ref[pl.ds(start, rows), :] = piece[...]
    for place, source in ((core, own_ref), (1 - core, other_ref)):
        at = pl.ds(pl.multiple_of(place * half, half), half)
        x = source[...]
        x_ref[at, :] = x
        seq_ref[at, :] = (unit_rows(x) * gain_ref[...]).astype(bf16)
    wo_ref[...] = w_ref[:, 3 * width :]
    for i in range(0, seq, 256):
        qkv_ref[i : i + 256, :] = mm(seq_ref[i : i + 256, :], w_ref[:, : 3 * width]).astype(bf16)
    for h in range(heads):
        at = h * HD
        key = qkv_ref[:, width + at : width + at + HD]
        value = qkv_ref[:, 2 * width + at : 2 * width + at + HD]
        for i in range(0, seq, TILE):
            base = seq - TILE - i
            seg = jnp.broadcast_to(vec_ref[h : h + 1, base : base + span], (TILE, span))
            bias = pltpu.roll(seg, span - TILE + 1, 1, stride=1, stride_axis=0)[:, :seq]
            scores = mm_bt(qkv_ref[i : i + TILE, at : at + HD], key) * HD**-0.5 + bias
            scores = jnp.where(row_docs[i : i + TILE, :] == col_docs[...], scores, masked_value)
            peak = jnp.max(scores, axis=1, keepdims=True)
            exp_scores = jnp.exp(scores - peak)
            probs = exp_scores / jnp.sum(exp_scores, axis=1, keepdims=True)
            probs_refs[h][i : i + TILE, :] = probs.astype(bf16)
            mixed_ref[i : i + TILE, at : at + HD] = mm(probs.astype(bf16), value).astype(bf16)
    keep_ref[...] = mixed_ref[pl.ds(pl.multiple_of(core * half, half), half), :]
    send_ref[...] = mixed_ref[pl.ds(pl.multiple_of((1 - core) * half, half), half), :]


def attended_kernel(keep_ref, got_ref, wo_ref, wo_other_ref, held_ref, out_ref):
    total = mm_bt(keep_ref[...], wo_ref[...]) + mm_bt(got_ref[...], wo_other_ref[...])
    out_ref[...] = total.astype(bf16)


def dispatch_kernel(x_ref, own_ref, got_ref, gain_ref, table_ref, hidden_ref, *blocks):
    hidden = x_ref[...].astype(f32) + (own_ref[...].astype(f32) + got_ref[...].astype(f32))
    hidden_ref[...] = hidden
    scale = lax.rsqrt(jnp.mean(hidden * hidden, axis=1, keepdims=True) + norm_eps)
    normed = (hidden * scale * gain_ref[...]).astype(bf16)
    slots = mm(table_ref[...], normed)
    rows = blocks[0].shape[0]
    for i, block in enumerate(blocks):
        block[...] = slots[i * rows : (i + 1) * rows, :].astype(bf16)


def expert_kernel(ids, own_ref, other_ref, h_ref, wup_ref, wr_ref, *refs):
    active_ref, gup_ref, chosen_ref, keep_ref, send_ref, router_ref, all_ref = refs
    rows = own_ref.shape[0]
    step = rows // 2
    router = jnp.zeros(router_ref.shape, f32)
    root = 0.7978845608028654
    for i in range(0, 2 * rows, step):
        src = own_ref if i < rows else other_ref
        at = i % rows
        slots = src[at : at + step, :]
        all_ref[i : i + step, :] = slots
        logits = mm_bt(slots, wr_ref[...])
        peak = jnp.max(logits, axis=1, keepdims=True)
        exp_logits = jnp.exp(logits - peak)
        gates = exp_logits / jnp.sum(exp_logits, axis=1, keepdims=True)
        mine = lax.broadcasted_iota(jnp.int32, gates.shape, 1) == ids[1]
        chosen = jnp.sum(jnp.where(mine, gates, 0.0), axis=1, keepdims=True)
        chosen_ref[i : i + step, :] = chosen
        up = mm(slots, wup_ref[...])
        square = up * up
        bent = jnp.tanh(root * (up + 0.044715 * up * square))
        low = (0.5 * up * (1.0 + bent)).astype(bf16)
        active_ref[i : i + step, :] = low
        slope = 0.5 * (1.0 + bent) + 0.5 * up * (1.0 - bent * bent) * root * (
            1.0 + 3.0 * 0.044715 * square
        )
        back = h_ref[i : i + step, :]
        gup = (chosen * back * slope).astype(bf16)
        gup_ref[i : i + step, :] = gup
        grad_chosen = jnp.sum(low.astype(f32) * back, axis=1, keepdims=True)
        grad_logits = gates * (jnp.where(mine, 1.0, 0.0) - chosen) * grad_chosen
        grad_logits = grad_logits.astype(bf16)
        router = router + mm_at(grad_logits, slots)
        grad = mm_bt(gup, wup_ref[...]) + mm(grad_logits, wr_ref[...])
        if i < rows:
            keep_ref[at : at + step, :] = grad
        else:
            send_ref[at : at + step, :] = grad.astype(bf16)
    router_ref[...] = router


def expert_out_kernel(active_ref, chosen_ref, wdown_ref, held_ref, keep_ref, send_ref):
    rows = keep_ref.shape[0]
    result = mm_bt(active_ref[...], wdown_ref[...]) * chosen_ref[...]
    keep_ref[...] = result[:rows, :]
    send_ref[...] = result[rows:, :].astype(bf16)


def expert_grads_kernel(slots_ref, cots_ref, active_ref, gup_ref, chosen_ref, held_ref, gwup_ref, gwdown_ref):
    gwup_ref[...] = mm_at(slots_ref[...], gup_ref[...])
    grads = (chosen_ref[...] * cots_ref[...].astype(f32)).astype(bf16)
    gwdown_ref[...] = mm_at(grads, active_ref[...])


def join_kernel(keep_ref, got_ref, *blocks):
    total = keep_ref[...] + got_ref[...].astype(f32)
    rows = blocks[0].shape[0]
    for i, block in enumerate(blocks):
        block[...] = total[i * rows : (i + 1) * rows, :].astype(bf16)


def join_natural_kernel(parts, ids, keep_ref, got_ref, out_ref):
    total = keep_ref[...] + got_ref[...].astype(f32)
    if parts == 1:
        out_ref[...] = total.astype(bf16)
        return
    rows = out_ref.shape[1]
    for i in range(parts):
        out_ref[ids[1] ^ i] = total[i * rows : (i + 1) * rows, :].astype(bf16)


def gather_kernel(back_table_ref, *refs):
    blocks = refs[:-1]
    slots = jnp.concatenate([b[...].astype(f32) for b in blocks], axis=0).astype(bf16)
    refs[-1][...] = mm(back_table_ref[...], slots).astype(bf16)


def hidden_back_kernel(ids, hidden_ref, own_ref, got_ref, cot_ref, gain_ref, held_ref, grad_ref, low_ref, dgain_ref, all_ref):
    hidden = hidden_ref[...]
    grad_normed = own_ref[...].astype(f32) + got_ref[...].astype(f32)
    scale = lax.rsqrt(jnp.mean(hidden * hidden, axis=1, keepdims=True) + norm_eps)
    dgain_ref[...] = jnp.sum(grad_normed * hidden * scale, axis=0, keepdims=True)
    pulled = gain_ref[...] * grad_normed
    inner = jnp.mean(pulled * hidden, axis=1, keepdims=True)
    grad = cot_ref[...].astype(f32) + scale * pulled - hidden * (scale * scale * scale) * inner
    low_ref[...] = grad.astype(bf16)
    all_ref[...] = grad
    rows = grad_ref.shape[0]
    grad_ref[...] = all_ref[pl.ds(pl.multiple_of(ids[2] * rows, rows), rows), :]


def returned_kernel(ids, table_ref, slots_ref, held_ref, keep_ref, send_ref):
    rows = keep_ref.shape[0]
    mine = table_ref[pl.ds(pl.multiple_of(ids[2] * rows, rows), rows), :]
    keep_ref[...] = mm(mine, slots_ref[...]).astype(bf16)
    theirs = table_ref[pl.ds(pl.multiple_of((1 - ids[2]) * rows, rows), rows), :]
    send_ref[...] = mm(theirs, slots_ref[...]).astype(bf16)


def activations_kernel(ids, hidden_ref, own_ref, got_ref, out_ref):
    rows = out_ref.shape[0]
    hidden = hidden_ref[pl.ds(pl.multiple_of(ids[2] * rows, rows), rows), :]
    out_ref[...] = (hidden + (own_ref[...].astype(f32) + got_ref[...].astype(f32))).astype(bf16)


def normed_sum_kernel(ids, keep_ref, got_ref, held_ref, own_ref, send_ref, all_ref):
    all_ref[...] = keep_ref[...] + got_ref[...].astype(f32)
    rows = own_ref.shape[0]
    own_ref[...] = all_ref[pl.ds(pl.multiple_of(ids[2] * rows, rows), rows), :]
    theirs = pl.ds(pl.multiple_of((1 - ids[2]) * rows, rows), rows)
    send_ref[...] = all_ref[theirs, :].astype(bf16)


def heads_back(heads, first, qkv_ref, gm_ref, probs, dqkv_ref, diag_ref, ds_ref):
    seq = qkv_ref.shape[0]
    width = heads * HD
    here = len(probs) * HD
    span = seq + TILE
    flip = (
        lax.broadcasted_iota(jnp.int32, (TILE, TILE), 0)
        + lax.broadcasted_iota(jnp.int32, (TILE, TILE), 1)
        == TILE - 1
    ).astype(bf16)
    for h, probs_ref in enumerate(probs):
        at = (first + h) * HD
        to = h * HD
        key = qkv_ref[:, width + at : width + at + HD]
        value = qkv_ref[:, 2 * width + at : 2 * width + at + HD]
        for i in range(0, seq, TILE):
            probs_rows = probs_ref[i : i + TILE, :].astype(f32)
            grad_probs = mm_bt(gm_ref[i : i + TILE, at : at + HD], value)
            inner = jnp.sum(probs_rows * grad_probs, axis=1, keepdims=True)
            grad_scores = (probs_rows * (grad_probs - inner)).astype(bf16)
            ds_ref[i : i + TILE, :] = grad_scores
            dqkv_ref[i : i + TILE, to : to + HD] = (mm(grad_scores, key) * HD**-0.5).astype(bf16)
            flipped = mm(flip, grad_scores)
            padded = jnp.concatenate([flipped, jnp.zeros((TILE, TILE), f32)], axis=1)
            skewed = pltpu.roll(padded, 0, 1, stride=1, stride_axis=0)
            base = seq - TILE - i
            row = first + h
            diag_ref[row : row + 1, base : base + span] += jnp.sum(skewed, axis=0, keepdims=True)
        dqkv_ref[:, here + to : here + to + HD] = (
            mm_at(ds_ref[...], qkv_ref[:, at : at + HD]) * HD**-0.5
        ).astype(bf16)
        dqkv_ref[:, 2 * here + to : 2 * here + to + HD] = mm_at(
            probs_ref[...], gm_ref[:, at : at + HD]
        ).astype(bf16)


def send_rows(parts, me, gw_ref, outs):
    if parts == 1:
        outs[0][...] = gw_ref[...].astype(bf16)
        return
    rows = gw_ref.shape[0] // parts
    for i in range(parts // 2):
        at = slice(i * rows, (i + 1) * rows)
        outs[0][at, :] = gw_ref[pl.ds(pl.multiple_of((me ^ 2 * i) * rows, rows), rows), :]
        there = pl.ds(pl.multiple_of((me ^ 2 * i ^ 1) * rows, rows), rows)
        outs[1][at, :] = gw_ref[there, :].astype(bf16)


def fetch(sources, targets, sems):
    copies = [
        pltpu.make_async_copy(a, b, sems.at[i]) for i, (a, b) in enumerate(zip(sources, targets))
    ]
    for copy in copies:
        copy.start()
    return copies


def first_back_kernel(heads, parts, ids, own_ref, other_ref, gain_ref, *refs):
    far = refs[:5]
    gm_ref, dqkv_ref, diag_ref, seq_ref, *outs = refs[5:-9]
    ga_ref, ds_ref, gw_ref = refs[-9:-6]
    wo_ref, qkv_ref, probs_ref, x_ref, mixed_ref = refs[-6:-1]
    copies = fetch(far, refs[-6:-1], refs[-1])
    core = ids[0]
    half = own_ref.shape[0]
    ga_ref[pl.ds(pl.multiple_of(core * half, half), half), :] = own_ref[...]
    ga_ref[pl.ds(pl.multiple_of((1 - core) * half, half), half), :] = other_ref[...]
    copies[0].wait()
    gm_ref[...] = mm(ga_ref[...], wo_ref[...]).astype(bf16)
    diag_ref[...] = jnp.zeros_like(diag_ref)
    copies[1].wait()
    copies[2].wait()
    heads_back(heads, 0, qkv_ref, gm_ref, [probs_ref], dqkv_ref, diag_ref, ds_ref)
    cut = dqkv_ref.shape[1]
    copies[3].wait()
    copies[4].wait()
    seq_ref[...] = (unit_rows(x_ref[...]) * gain_ref[...]).astype(bf16)
    gw_ref[:, :cut] = mm_at(seq_ref[...], dqkv_ref[...])
    gw_ref[:, cut:] = mm_at(ga_ref[...], mixed_ref[...])
    send_rows(parts, ids[1], gw_ref, outs)


def second_back_kernel(
    heads, parts, ids, gm_ref, first_ref, diag_in_ref, hot_ref, seq_ref, gain_ref, router_ref, *refs
):
    count = heads + 2
    far, near = refs[:count], refs[-count - 1 : -1]
    qkv_ref, *probs, x_ref, w_ref = near
    copies = fetch(far, near, refs[-1])
    refs = refs[count : -count - 1]
    keep_ref, send_ref, *outs = refs[:-6]
    diag_ref, dqkv_ref, all_ref, ds_ref, gw_ref, small_ref = refs[-6:]
    core, me, side = ids[0], ids[1], ids[2]
    half = keep_ref.shape[0]
    diag_ref[...] = diag_in_ref[...]
    for copy in copies[:heads]:
        copy.wait()
    heads_back(heads, 1, qkv_ref, gm_ref, probs, dqkv_ref, diag_ref, ds_ref)
    gw_ref[...] = mm_at(seq_ref[...], dqkv_ref[...])
    send_rows(parts, me, gw_ref, outs)
    rest = (heads - 1) * HD
    for i in range(3):
        at = i * heads * HD
        all_ref[:, at : at + HD] = first_ref[:, i * HD : (i + 1) * HD]
        all_ref[:, at + HD : at + heads * HD] = dqkv_ref[:, i * rest : (i + 1) * rest]
    for copy in copies[heads:]:
        copy.wait()
    gain = jnp.zeros((1, x_ref.shape[1]), f32)
    for place, mine in ((core, True), (1 - core, False)):
        rows = pl.ds(pl.multiple_of(place * half, half), half)
        grad = mm_bt(all_ref[rows, :], w_ref[:, : all_ref.shape[1]])
        gain = gain + jnp.sum(grad * unit_rows(x_ref[rows, :]), axis=0, keepdims=True)
        if mine:
            keep_ref[...] = grad
        else:
            send_ref[...] = grad.astype(bf16)
    small_ref[...] = jnp.zeros_like(small_ref)
    small_ref[0:1, :] = gain
    small_ref[1:2, :] = jnp.where(side == 0, gain_ref[...], 0.0)
    experts = router_ref.shape[0]
    small_ref[2 : 2 + experts, :] = router_ref[...]
    bias = jnp.dot(diag_ref[...], hot_ref[...], precision=exact, preferred_element_type=f32)
    lanes = bias.shape[1]
    for i in range(2 * GROUP):
        small_ref[2 + experts : 2 + experts + heads, i * lanes : (i + 1) * lanes] = jnp.where(
            side * GROUP + core == i, bias[:heads, :], 0.0
        )
    if parts == 1:
        outs[1][...] = small_ref[...]
        return
    high = small_ref.shape[0]
    end = outs[0].shape[0] - 2 * high
    cols = outs[0].shape[1]
    for i in range(2):
        low = small_ref[:, i * cols : (i + 1) * cols].astype(bf16)
        outs[0][end + i * high : end + (i + 1) * high, :] = low.astype(f32)
        outs[1][end + i * high : end + (i + 1) * high, :] = low


def fold_kernel(parts, keep_ref, got_ref, *refs):
    count = (len(refs) - parts // 2) // 2
    passed, (own_ref, *sends) = refs[:count], refs[2 * count :]
    for source, target in zip(passed, refs[count:]):
        target[...] = source[...]
    total = keep_ref[...] + got_ref[...].astype(f32)
    rows = own_ref.shape[0]
    own_ref[...] = total[:rows, :]
    for i, send in enumerate(sends):
        send[...] = total[(i + 1) * rows : (i + 2) * rows, :].astype(bf16)


def quarters(refs, at):
    a, b, c, d = (r[at, :].astype(f32) for r in refs)
    return (a + b) + (c + d)


def split_cores(core, refs, keep_ref, send_ref):
    rows = keep_ref.shape[0]
    keep_ref[...] = quarters(refs, pl.ds(pl.multiple_of(core * rows, rows), rows))
    send_ref[:rows, :] = quarters(refs, pl.ds(pl.multiple_of((1 - core) * rows, rows), rows))


def fold_second_kernel(small_rows, ids, keep_ref, got_ref, *refs):
    first = refs[:4]
    refs[5][...] = refs[4][...]
    keep_one_ref, send_one_ref, own_ref, *sends = refs[6:]
    total = keep_ref[...] + got_ref[...].astype(f32)
    rows = keep_one_ref.shape[0] * 2
    end = total.shape[0] - small_rows
    small = total[end:, :].astype(bf16)
    for i, block in enumerate((own_ref, *sends)):
        block[:rows, :] = total[i * rows : (i + 1) * rows, :].astype(block.dtype)
        block[rows:, :] = small.astype(block.dtype)
    split_cores(ids[0], first, keep_one_ref, send_one_ref)


def sum_nodes_kernel(ids, *refs):
    second = refs[:4]
    keep_ref, send_ref = refs[-2:]
    split_cores(ids[0], second, keep_ref, send_ref)
    rows = keep_ref.shape[0]
    send_ref[rows:, :] = quarters(second, slice(2 * rows, second[0].shape[0]))


def columns_kernel(heads, ids, keep_one, got_one, keep_two, got_two, *outs):
    core = ids[0]
    rows = keep_one.shape[0]
    cols = heads * HD
    rest = cols - HD
    for c in range(2):
        at = c * cols
        mine = core == c
        one = jnp.where(mine, keep_one[...], got_one[...])
        two = jnp.where(mine, keep_two[...], got_two[:rows, :])
        for i in range(3):
            outs[i][:, at : at + HD] = one[:, i * HD : (i + 1) * HD]
            outs[i][:, at + HD : at + cols] = two[:, i * rest : (i + 1) * rest]
        outs[3][:, at : at + cols] = one[:, 3 * HD : 3 * HD + cols]


def input_kernel(keep_ref, got_ref, grad_ref, x_ref, gain_ref, out_ref):
    grad_normed = keep_ref[...] + got_ref[...].astype(f32)
    wide = x_ref[...].astype(f32)
    scale = lax.rsqrt(jnp.mean(wide * wide, axis=1, keepdims=True) + norm_eps)
    pulled = gain_ref[...] * grad_normed
    inner = jnp.mean(pulled * wide, axis=1, keepdims=True)
    out_ref[...] = grad_ref[...] + scale * pulled - wide * (scale * scale * scale) * inner


def in_order(first, mine, other):
    return jnp.where(first, jnp.concatenate([mine, other]), jnp.concatenate([other, mine]))


def per_device(
    tokens,
    gain_one,
    w_query,
    w_key,
    w_value,
    w_out,
    bias_table,
    gain_two,
    w_router,
    w_up,
    w_down,
    routes,
    doc_lengths,
    buckets,
    cotangent,
):
    own_rows, width = tokens.shape
    block_rows = routes.shape[0]
    seq = block_rows * GROUP
    cols = w_query.shape[1] // GROUP
    heads = cols // HD
    experts = w_router.shape[1]
    capacity = max(2, (5 * block_rows + 4 * experts - 1) // (4 * experts))
    slots = experts * capacity
    nodes = lax.axis_size("node")
    core = lax.axis_index("core")
    side = lax.axis_index("tensor")
    me = lax.axis_index("node")
    direct = nodes == DIRECT
    parts = nodes if direct else 1
    ids = jnp.stack([core, me, side]).astype(jnp.int32)
    node_rows = width // nodes

    def trade(blocks):
        if direct:
            return [blocks[0]] + [across(blocks[i], "node", i) for i in range(1, nodes)]
        stacked = blocks[0].reshape(nodes, -1, blocks[0].shape[1])
        back = lax.all_to_all(stacked, "node", split_axis=0, concat_axis=0, tiled=True)
        return [back.reshape(blocks[0].shape)]

    def trade_natural(rows):
        stacked = rows.reshape(nodes, -1, rows.shape[-1])
        return lax.all_to_all(stacked, "node", split_axis=0, concat_axis=0, tiled=True)

    share = out((w_query.shape[0], 4 * cols), bf16)
    share_kept, share_sent = call(
        shares_kernel,
        "shares",
        [share, share],
        [ids, *(Far(w) for w in (w_query, w_key, w_value, w_out))],
        smem=1,
        scratch=[pltpu.VMEM((4, *w_query.shape), bf16), pltpu.SemaphoreType.DMA((4,))],
    )
    piece = in_order(core == 0, share_kept, across(share_sent, "core", 1))
    if direct:
        pieces = {0: piece}
        for i in (2, 4, 6):
            pieces[i] = across(piece, "node", i)
        for i in (0, 2, 4, 6):
            pieces[i + 1] = across(pieces[i], "node", 1)
        pieces = [pieces[i] for i in range(nodes)]
    else:
        pieces = [lax.all_gather(piece, "node", axis=0, tiled=True)]

    x_rows = call(
        rows_kernel,
        "rows",
        [out((block_rows, width), bf16)],
        [ids, tokens, across(tokens, "tensor", 1), Raw(pieces[min(1, parts - 1)])],
        smem=1,
    )[0]
    x_other = across(x_rows, "core", 1)
    gain_first = gain_one.astype(f32)[None, :]
    gain_second = gain_two.astype(f32)[None, :]

    expert_ids = routes[:, 0]
    picks = (expert_ids[:, None] == jnp.arange(experts, dtype=jnp.int32)[None, :]).astype(jnp.int32)
    slot_index = jnp.sum((jnp.cumsum(picks, axis=0) - 1) * picks, axis=1)
    target = expert_ids * capacity + slot_index
    codes = jnp.arange(slots, dtype=jnp.int32)
    turned = ((codes // capacity) ^ me) * capacity + codes % capacity if direct else codes
    table = (turned[:, None] == target[None, :]).astype(bf16)
    back_table = (target[:, None] == turned[None, :]).astype(bf16)
    plain_table = (codes[:, None] == target[None, :]).astype(bf16)
    plain_back_table = (target[:, None] == codes[None, :]).astype(bf16)

    lengths_row = lax.dynamic_slice_in_dim(doc_lengths, me, 1, 0)[0]
    ends = jnp.cumsum(lengths_row)
    places = jnp.arange(seq, dtype=jnp.int32)
    docs = jnp.sum((ends[None, :] <= places[:, None]).astype(jnp.int32), axis=1)
    bucket_count = bias_table.shape[0]
    bucket_hot = (
        jnp.pad(buckets, (0, 1))[:, None] == jnp.arange(128, dtype=jnp.int32)[None, :]
    ).astype(f32)
    head_start = (side * GROUP + core) * heads
    bias_here = lax.dynamic_slice_in_dim(bias_table, head_start, heads, 1)
    bias_here = jnp.pad(bias_here, ((0, 128 - bucket_count), (0, 0)))
    bias_vectors = lax.dot_general(
        bias_here, bucket_hot, (((0,), (1,)), ((), ())), precision=exact, preferred_element_type=f32
    )

    weights, wo, x_seq, qkv, mixed, mixed_kept, mixed_sent, *probs = call(
        functools.partial(attend_kernel, heads, parts),
        "attend",
        [
            out((width, 4 * cols), bf16),
            out((width, cols), bf16),
            out((seq, width), bf16),
            out((seq, 3 * cols), bf16),
            out((seq, cols), bf16),
            out((block_rows, cols), bf16),
            out((block_rows, cols), bf16),
            *([out((seq, seq), bf16)] * heads),
        ],
        [
            ids,
            x_rows,
            Near(x_other),
            gain_first,
            bias_vectors,
            docs[:, None],
            docs[None, :],
            *(Near(p) for p in pieces),
        ],
        smem=1,
        scratch=[pltpu.VMEM((seq, width), bf16)],
    )
    kept = [weights, wo, x_seq, qkv, mixed, *probs]
    weights, wo_far, x_seq, qkv, mixed, *probs = call(
        functools.partial(move_kernel, len(kept)),
        "park",
        [Far(out(a.shape, a.dtype)) for a in kept],
        [*(Near(a) for a in kept)],
        scratch=[pltpu.SemaphoreType.DMA((len(kept),))],
    )

    natural = (nodes, slots // nodes, width) if direct else (slots, width)
    cot_slots = call(
        slots_kernel,
        "cot_slots",
        [out((slots, width), bf16)],
        [plain_table, cotangent, Raw(mixed_sent)],
    )[0]
    cots_own = trade_natural(cot_slots).reshape(natural)
    cots_other = across(cots_own, "core", 1)

    mixed_got = across(mixed_sent, "core", 1)
    attended = call(
        attended_kernel,
        "attended",
        [out((block_rows, width), bf16)],
        [mixed_kept, mixed_got, wo, across(wo, "core", 1), Far(mixed)],
    )[0]
    attended_got = across(attended, "tensor", 1)
    block_shapes = [out((slots // parts, width), bf16)] * parts
    hidden, *blocks = call(
        dispatch_kernel,
        "dispatch",
        [Near(out((block_rows, width), f32)), *block_shapes],
        [Near(x_rows), attended, Near(attended_got), gain_second, Near(table)],
    )
    received = trade(blocks)
    cots, back_active = call(
        functools.partial(cots_kernel, parts),
        "cots",
        [Near(out((2 * slots, width), bf16)), Near(out((2 * slots, w_down.shape[1]), f32))],
        [ids, Near(cots_own), Near(cots_other), w_down, Raw(blocks[0])],
        smem=1,
        scratch=[pltpu.VMEM((slots, width), f32)] if direct else [],
    )
    slots_own = jnp.concatenate(received)
    slots_other = across(slots_own, "core", 1)
    active, grad_upward, chosen, grad_kept, grad_sent, router_part, slots_all = call(
        expert_kernel,
        "expert",
        [
            Near(out((2 * slots, w_up.shape[1]), bf16)),
            Near(out((2 * slots, w_up.shape[1]), bf16)),
            Near(out((2 * slots, 1), f32)),
            out((slots, width), f32),
            out((slots, width), bf16),
            Near(out(w_router.shape[::-1], f32)),
            Near(out((2 * slots, width), bf16)),
        ],
        [ids, slots_own, Near(slots_other), Near(back_active), w_up, w_router.T],
        smem=1,
    )
    grad_blocks = call(
        join_kernel, "join_grad", block_shapes, [grad_kept, Near(across(grad_sent, "core", 1))]
    )
    grad_back = trade(grad_blocks)
    grad_normed_two = call(
        gather_kernel,
        "gather_grad",
        [out((block_rows, width), bf16)],
        [Near(back_table), *grad_back],
    )[0]
    grad_normed_two_got = across(grad_normed_two, "tensor", 1)

    out_kept, out_sent = call(
        expert_out_kernel,
        "expert_out",
        [out((slots, width), f32), out((slots, width), bf16)],
        [Near(active), Near(chosen), w_down, Raw(grad_blocks[-1])],
    )
    out_slots = call(
        functools.partial(join_natural_kernel, parts),
        "join_out",
        [out(natural, bf16)],
        [ids, out_kept, Near(across(out_sent, "core", 1))],
        smem=1,
    )[0]
    out_back = trade_natural(out_slots.reshape(slots, width)).reshape(slots, width)
    half_block = (own_rows, width)

    grad_hidden, grad_attended, gain_two_part = call(
        hidden_back_kernel,
        "hidden_back",
        [Near(out(half_block, f32)), out((block_rows, width), bf16), Near(out((1, width), f32))],
        [
            ids,
            Near(hidden),
            grad_normed_two,
            Near(grad_normed_two_got),
            cotangent,
            gain_second,
            Raw(out_slots),
        ],
        smem=1,
        scratch=[pltpu.VMEM((block_rows, width), f32)],
    )
    grad_attended_other = across(grad_attended, "core", 1)
    chunk = 3 * HD + cols
    other_chunk = 3 * (cols - HD)
    small_rows = -(-(2 + experts + heads) // 16) * 16
    if direct:
        tall = width // 2 + 2 * small_rows
        first_shapes = [out((width // 2, chunk), t) for t in (f32, bf16)]
        second_shapes = [out((tall, other_chunk), t) for t in (f32, bf16)]
    else:
        first_shapes = [out((width, chunk), bf16)]
        second_shapes = [out((width, other_chunk), bf16), out((small_rows, width), f32)]
    grad_mixed, first_dqkv, diagonals, normed_seq, *first_chunk = call(
        functools.partial(first_back_kernel, heads, parts),
        "first_back",
        [
            out((seq, cols), bf16),
            out((seq, 3 * HD), bf16),
            out((8, 2 * seq), f32),
            out((seq, width), bf16),
            *first_shapes,
        ],
        [
            ids,
            grad_attended,
            Near(grad_attended_other),
            gain_first,
            *(Far(a) for a in (wo_far, qkv, probs[0], x_seq, mixed)),
        ],
        smem=1,
        flops=FLOPS1,
        scratch=[
            pltpu.VMEM((seq, width), bf16),
            pltpu.VMEM((seq, seq), bf16),
            pltpu.VMEM((width, chunk), f32),
            *(pltpu.VMEM(a.shape, bf16) for a in (wo_far, qkv, probs[0], x_seq, mixed)),
            pltpu.SemaphoreType.DMA((5,)),
        ],
    )
    grad_kept, grad_sent, *second_chunk = call(
        functools.partial(second_back_kernel, heads, parts),
        "second_back",
        [
            out((block_rows, width), f32),
            out((block_rows, width), bf16),
            *second_shapes,
        ],
        [
            ids,
            grad_mixed,
            first_dqkv,
            diagonals,
            bucket_hot,
            normed_seq,
            Near(gain_two_part),
            Near(router_part),
            *(Far(a) for a in (qkv, *probs[1:], x_seq, weights)),
        ],
        smem=1,
        flops=FLOPS2,
        scratch=[
            pltpu.VMEM((8, 2 * seq), f32),
            pltpu.VMEM((seq, other_chunk), bf16),
            pltpu.VMEM((seq, 3 * cols), bf16),
            pltpu.VMEM((seq, seq), bf16),
            pltpu.VMEM((width, other_chunk), f32),
            pltpu.VMEM((small_rows, width), f32),
            *(pltpu.VMEM(a.shape, bf16) for a in (qkv, *probs[1:], x_seq, weights)),
            pltpu.SemaphoreType.DMA((heads + 2,)),
        ],
    )

    shard_rows = w_query.shape[0]
    returned, returned_sent = call(
        returned_kernel,
        "returned",
        [out(half_block, bf16), out(half_block, bf16)],
        [ids, Near(plain_back_table), Near(out_back), Raw(grad_kept)],
        smem=1,
    )
    part = out((shard_rows, chunk), f32)
    if direct:
        passed = [second_chunk[1], grad_sent, returned_sent]
        second_sent, grad_sent, returned_sent, own_one, *send_one = call(
            functools.partial(fold_kernel, parts),
            "fold_first",
            [
                *(out(a.shape, a.dtype) for a in passed),
                out((node_rows, chunk), f32),
                *([out((node_rows, chunk), bf16)] * 3),
            ],
            [first_chunk[0], across(first_chunk[1], "node", 1), *passed],
        )
        got_one = [across(b, "node", 2 * i + 2) for i, b in enumerate(send_one)]
        first_done = send_one[0]
    else:
        sums = [jnp.sum(trade_natural(c[0]).astype(f32), axis=0) for c in (first_chunk, second_chunk)]
        kept_one, kept_two = (
            lax.dynamic_slice_in_dim(s, core * shard_rows, shard_rows, 0) for s in sums
        )
        sent_one, sent_two = (
            lax.dynamic_slice_in_dim(s, (1 - core) * shard_rows, shard_rows, 0) for s in sums
        )
        first_done, second_done = kept_one, kept_two
    grad_normed, grad_normed_sent = call(
        normed_sum_kernel,
        "normed_sum",
        [Near(out(half_block, f32)), out(half_block, bf16)],
        [ids, grad_kept, Near(across(grad_sent, "core", 1)), Raw(first_done)],
        smem=1,
        scratch=[pltpu.VMEM((block_rows, width), f32)],
    )
    if direct:
        high = node_rows + 2 * small_rows
        grad_normed_sent, kept_one, sent_one, own_two, *send_two = call(
            functools.partial(fold_second_kernel, 2 * small_rows),
            "fold_second",
            [out(half_block, bf16), part, part, out((high, chunk), f32), *([out((high, chunk), bf16)] * 3)],
            [
                ids,
                second_chunk[0],
                across(second_sent, "node", 1),
                own_one,
                *got_one,
                grad_normed_sent,
            ],
            smem=1,
        )
        got_two = [across(b, "node", 2 * i + 2) for i, b in enumerate(send_two)]
        second_done = send_two[0]
    grad_w_up_here, grad_w_down_here = call(
        expert_grads_kernel,
        "expert_grads",
        [out(w_up.shape, f32), out(w_down.shape, f32)],
        [
            *(Near(a) for a in (slots_all, cots, active, grad_upward, chosen)),
            Raw(second_done),
        ],
    )
    input_grad = call(
        input_kernel,
        "input_grad",
        [out(half_block, f32)],
        [
            Near(grad_normed),
            Near(across(grad_normed_sent, "tensor", 1)),
            Near(grad_hidden),
            tokens,
            gain_first,
        ],
    )[0]
    activations = call(
        activations_kernel,
        "activations",
        [out(half_block, bf16)],
        [ids, Near(hidden), Near(returned), Near(across(returned_sent, "tensor", 1))],
        smem=1,
    )[0]
    if direct:
        kept_two, sent_two = call(
            sum_nodes_kernel,
            "sum_nodes",
            [part, out((shard_rows + 2 * small_rows, chunk), f32)],
            [
                ids,
                own_two,
                *got_two,
                *(Far(a) for a in (grad_w_up_here, activations, input_grad)),
            ],
            smem=1,
        )
    got_one = across(sent_one, "core", 1)
    got_two = across(sent_two, "core", 1)
    if direct:
        small = sent_two[shard_rows:, :] + got_two[shard_rows:, :]
        small = small + across(small, "tensor", 1)
        small = jnp.concatenate([small[:small_rows], small[small_rows:]], axis=1)
    else:
        small = lax.psum(second_chunk[1], ("node", "core", "tensor"))
    weight_grads = call(
        functools.partial(columns_kernel, heads),
        "columns",
        [out(w_query.shape, f32)] * 4,
        [ids, kept_one, got_one, kept_two, got_two],
        smem=1,
    )

    bias_rows = small[2 + experts : 2 + experts + heads, : 4 * 128].reshape(heads, 4, 128)
    grad_bias = bias_rows[:, :, :bucket_count].transpose(2, 1, 0).reshape(bias_table.shape)
    return (
        activations,
        input_grad,
        small[0],
        *weight_grads,
        grad_bias,
        small[1],
        small[2 : 2 + experts].T,
        grad_w_up_here,
        grad_w_down_here,
    )


def solution(mesh):
    dp, tensor = mesh.shape["dp"], mesh.shape["tensor"]
    grid = Mesh(mesh.devices.reshape(dp // GROUP, GROUP, tensor), ("node", "core", "tensor"))
    dp = ("node", "core")
    every = ("node", "core", "tensor")
    in_specs = (
        P(every, None),
        P(),
        P(dp, "tensor"),
        P(dp, "tensor"),
        P(dp, "tensor"),
        P(dp, "tensor"),
        P(),
        P(),
        P(),
        P(None, every),
        P(None, every),
        P(dp, None),
        P(),
        P(),
        P(dp, None),
    )
    out_specs = (
        P(every, None),
        P(every, None),
        P(),
        P(dp, "tensor"),
        P(dp, "tensor"),
        P(dp, "tensor"),
        P(dp, "tensor"),
        P(),
        P(),
        P(),
        P(None, every),
        P(None, every),
    )
    return jax.shard_map(
        per_device, mesh=grid, in_specs=in_specs, out_specs=out_specs, check_vma=False
    )
```

```python
import functools

import jax
import jax.numpy as jnp
from jax import lax
from jax.experimental import pallas as pl
from jax.experimental.pallas import tpu as pltpu
from jax.sharding import Mesh, PartitionSpec as P

HD = 64
GROUP = 2
FLOPS1 = 0
FLOPS2 = 0
DIRECT = 8
FORWARD_TILE = 256
BACK_TILE = 512

norm_eps = 1e-06
masked_value = -1e30
exact = lax.Precision.HIGHEST
bf16 = jnp.bfloat16
f32 = jnp.float32

VMEM = pl.BlockSpec(memory_space=pltpu.VMEM)
SMEM = pl.BlockSpec(memory_space=pltpu.SMEM)
ANY = pl.BlockSpec(memory_space=pl.ANY)


def across(shard, axis, bits):
    return lax.ppermute(shard, axis, [(i, i ^ bits) for i in range(lax.axis_size(axis))])


class Near:
    def __init__(self, array):
        self.array = array


class Raw(Near):
    pass


class Far(Raw):
    pass


def call(body, name, outs, args, smem=0, scratch=(), flops=0):
    arrays = [a.array if isinstance(a, Near) else a for a in args]
    results = [o.array if isinstance(o, Near) else o for o in outs]
    kept = sum(padded_bytes(a) for a in [*arrays, *results, *scratch] if is_plain(a))
    space = {Near: pltpu.VMEM, Far: pltpu.HBM}
    given = [
        pltpu.with_memory_space_constraint(x, space[type(a)]) if type(a) in space else x
        for a, x in zip(args, arrays)
    ]
    return pl.pallas_call(
        body,
        name=name,
        out_shape=[
            space[type(o)](x.shape, x.dtype) if type(o) in space else x
            for o, x in zip(outs, results)
        ],
        in_specs=[SMEM] * smem + [ANY if isinstance(a, Raw) else VMEM for a in args[smem:]],
        out_specs=[ANY if isinstance(o, Raw) else VMEM for o in outs],
        scratch_shapes=scratch,
        compiler_params=pltpu.CompilerParams(vmem_limit_bytes=kept + 10 * 1024 * 1024),
        cost_estimate=pl.CostEstimate(flops=flops, bytes_accessed=0, transcendentals=0),
    )(*given)


def is_plain(array):
    return array.dtype in (bf16, f32, jnp.int32)


def padded_bytes(array):
    *lead, rows, cols = (1, 1, *array.shape)
    size = jnp.dtype(array.dtype).itemsize
    for extent in lead:
        size *= extent
    return size * (-(-rows // 16) * 16) * (-(-cols // 128) * 128)


def out(shape, dtype):
    return jax.ShapeDtypeStruct(shape, dtype)


def mm(a, b):
    return jnp.dot(a, b, preferred_element_type=f32)


def mm_bt(a, b):
    return lax.dot_general(a, b, (((1,), (1,)), ((), ())), preferred_element_type=f32)


def mm_at(a, b):
    return lax.dot_general(a, b, (((0,), (0,)), ((), ())), preferred_element_type=f32)


def shares_kernel(ids, *refs):
    weights, (keep_ref, send_ref, near_ref, sems) = refs[:4], refs[4:]
    copies = [
        pltpu.make_async_copy(w, near_ref.at[i], sems.at[i]) for i, w in enumerate(weights)
    ]
    for copy in copies:
        copy.start()
    for copy in copies:
        copy.wait()
    first = ids[0] == 0
    cols = keep_ref.shape[1] // 4
    for i in range(4):
        low, high = near_ref[i, :, :cols], near_ref[i, :, cols:]
        keep_ref[:, i * cols : (i + 1) * cols] = jnp.where(first, low, high)
        send_ref[:, i * cols : (i + 1) * cols] = jnp.where(first, high, low)


def rows_kernel(ids, own_ref, got_ref, held_ref, out_ref):
    rows = own_ref.shape[0]
    out_ref[pl.ds(pl.multiple_of(ids[2] * rows, rows), rows), :] = own_ref[...]
    out_ref[pl.ds(pl.multiple_of((1 - ids[2]) * rows, rows), rows), :] = got_ref[...]


def move_kernel(count, *refs):
    sources, targets, sems = refs[:count], refs[-count - 1 : -1], refs[-1]
    copies = [
        pltpu.make_async_copy(a, b, sems.at[i]) for i, (a, b) in enumerate(zip(sources, targets))
    ]
    for copy in copies:
        copy.start()
    for copy in copies:
        copy.wait()


def unit_rows(x):
    wide = x.astype(f32)
    return wide * lax.rsqrt(jnp.mean(wide * wide, axis=1, keepdims=True) + norm_eps)


def slots_kernel(table_ref, rows_ref, held_ref, out_ref):
    out_ref[...] = mm(table_ref[...], rows_ref[...]).astype(bf16)


def cots_kernel(parts, ids, own_ref, other_ref, wdown_ref, held_ref, cots_ref, back_ref, *scratch):
    slots = cots_ref.shape[0] // 2
    me = ids[1]
    for at, source in ((0, own_ref), (slots, other_ref)):
        if parts == 1:
            cots_ref[at : at + slots, :] = source[...]
        else:
            rows = slots // parts
            for i in range(parts):
                scratch[0][i * rows : (i + 1) * rows, :] = source[me ^ i].astype(f32)
            cots_ref[at : at + slots, :] = scratch[0][...].astype(bf16)
        back_ref[at : at + slots, :] = mm(cots_ref[at : at + slots, :], wdown_ref[...])


def attend_kernel(heads, parts, ids, own_ref, other_ref, gain_ref, vec_ref, row_docs, col_docs, *refs):
    pieces = refs[:parts]
    w_ref, wo_ref, x_ref, qkv_ref, mixed_ref, keep_ref, send_ref, *probs_refs = refs[parts:-1]
    seq_ref = refs[-1]
    core = ids[0]
    me = ids[1]
    seq = x_ref.shape[0]
    width = heads * HD
    half = seq // GROUP
    span = seq + FORWARD_TILE
    rows = pieces[0].shape[0]
    for i, piece in enumerate(pieces):
        start = 0 if parts == 1 else pl.multiple_of((me ^ i) * rows, rows)
        w_ref[pl.ds(start, rows), :] = piece[...]
    for place, source in ((core, own_ref), (1 - core, other_ref)):
        at = pl.ds(pl.multiple_of(place * half, half), half)
        x = source[...]
        x_ref[at, :] = x
        seq_ref[at, :] = (unit_rows(x) * gain_ref[...]).astype(bf16)
    wo_ref[...] = w_ref[:, 3 * width :]
    for i in range(0, seq, 256):
        qkv_ref[i : i + 256, :] = mm(seq_ref[i : i + 256, :], w_ref[:, : 3 * width]).astype(bf16)
    for h in range(heads):
        at = h * HD
        key = qkv_ref[:, width + at : width + at + HD]
        value = qkv_ref[:, 2 * width + at : 2 * width + at + HD]
        for i in range(0, seq, FORWARD_TILE):
            base = seq - FORWARD_TILE - i
            seg = jnp.broadcast_to(vec_ref[h : h + 1, base : base + span], (FORWARD_TILE, span))
            bias = pltpu.roll(seg, span - FORWARD_TILE + 1, 1, stride=1, stride_axis=0)[:, :seq]
            scores = mm_bt(qkv_ref[i : i + FORWARD_TILE, at : at + HD], key) * HD**-0.5 + bias
            scores = jnp.where(row_docs[i : i + FORWARD_TILE, :] == col_docs[...], scores, masked_value)
            peak = jnp.max(scores, axis=1, keepdims=True)
            exp_scores = jnp.exp(scores - peak)
            probs = exp_scores / jnp.sum(exp_scores, axis=1, keepdims=True)
            probs_refs[h][i : i + FORWARD_TILE, :] = probs.astype(bf16)
            mixed_ref[i : i + FORWARD_TILE, at : at + HD] = mm(probs.astype(bf16), value).astype(bf16)
    keep_ref[...] = mixed_ref[pl.ds(pl.multiple_of(core * half, half), half), :]
    send_ref[...] = mixed_ref[pl.ds(pl.multiple_of((1 - core) * half, half), half), :]


def attended_kernel(keep_ref, got_ref, wo_ref, wo_other_ref, held_ref, out_ref):
    total = mm_bt(keep_ref[...], wo_ref[...]) + mm_bt(got_ref[...], wo_other_ref[...])
    out_ref[...] = total.astype(bf16)


def dispatch_kernel(x_ref, own_ref, got_ref, gain_ref, table_ref, hidden_ref, *blocks):
    hidden = x_ref[...].astype(f32) + (own_ref[...].astype(f32) + got_ref[...].astype(f32))
    hidden_ref[...] = hidden
    scale = lax.rsqrt(jnp.mean(hidden * hidden, axis=1, keepdims=True) + norm_eps)
    normed = (hidden * scale * gain_ref[...]).astype(bf16)
    slots = mm(table_ref[...], normed)
    rows = blocks[0].shape[0]
    for i, block in enumerate(blocks):
        block[...] = slots[i * rows : (i + 1) * rows, :].astype(bf16)


def expert_kernel(ids, own_ref, other_ref, h_ref, wup_ref, wr_ref, *refs):
    active_ref, gup_ref, chosen_ref, keep_ref, send_ref, router_ref, all_ref = refs
    rows = own_ref.shape[0]
    step = rows // 2
    router = jnp.zeros(router_ref.shape, f32)
    root = 0.7978845608028654
    for i in range(0, 2 * rows, step):
        src = own_ref if i < rows else other_ref
        at = i % rows
        slots = src[at : at + step, :]
        all_ref[i : i + step, :] = slots
        logits = mm_bt(slots, wr_ref[...])
        peak = jnp.max(logits, axis=1, keepdims=True)
        exp_logits = jnp.exp(logits - peak)
        gates = exp_logits / jnp.sum(exp_logits, axis=1, keepdims=True)
        mine = lax.broadcasted_iota(jnp.int32, gates.shape, 1) == ids[1]
        chosen = jnp.sum(jnp.where(mine, gates, 0.0), axis=1, keepdims=True)
        chosen_ref[i : i + step, :] = chosen
        up = mm(slots, wup_ref[...])
        square = up * up
        bent = jnp.tanh(root * (up + 0.044715 * up * square))
        low = (0.5 * up * (1.0 + bent)).astype(bf16)
        active_ref[i : i + step, :] = low
        slope = 0.5 * (1.0 + bent) + 0.5 * up * (1.0 - bent * bent) * root * (
            1.0 + 3.0 * 0.044715 * square
        )
        back = h_ref[i : i + step, :]
        gup = (chosen * back * slope).astype(bf16)
        gup_ref[i : i + step, :] = gup
        grad_chosen = jnp.sum(low.astype(f32) * back, axis=1, keepdims=True)
        grad_logits = gates * (jnp.where(mine, 1.0, 0.0) - chosen) * grad_chosen
        grad_logits = grad_logits.astype(bf16)
        router = router + mm_at(grad_logits, slots)
        grad = mm_bt(gup, wup_ref[...]) + mm(grad_logits, wr_ref[...])
        if i < rows:
            keep_ref[at : at + step, :] = grad
        else:
            send_ref[at : at + step, :] = grad.astype(bf16)
    router_ref[...] = router


def expert_out_kernel(active_ref, chosen_ref, wdown_ref, held_ref, keep_ref, send_ref):
    rows = keep_ref.shape[0]
    result = mm_bt(active_ref[...], wdown_ref[...]) * chosen_ref[...]
    keep_ref[...] = result[:rows, :]
    send_ref[...] = result[rows:, :].astype(bf16)


def expert_grads_kernel(slots_ref, cots_ref, active_ref, gup_ref, chosen_ref, held_ref, gwup_ref, gwdown_ref):
    gwup_ref[...] = mm_at(slots_ref[...], gup_ref[...])
    grads = (chosen_ref[...] * cots_ref[...].astype(f32)).astype(bf16)
    gwdown_ref[...] = mm_at(grads, active_ref[...])


def join_kernel(keep_ref, got_ref, *blocks):
    total = keep_ref[...] + got_ref[...].astype(f32)
    rows = blocks[0].shape[0]
    for i, block in enumerate(blocks):
        block[...] = total[i * rows : (i + 1) * rows, :].astype(bf16)


def join_natural_kernel(parts, ids, keep_ref, got_ref, out_ref):
    total = keep_ref[...] + got_ref[...].astype(f32)
    if parts == 1:
        out_ref[...] = total.astype(bf16)
        return
    rows = out_ref.shape[1]
    for i in range(parts):
        out_ref[ids[1] ^ i] = total[i * rows : (i + 1) * rows, :].astype(bf16)


def gather_kernel(back_table_ref, *refs):
    blocks = refs[:-1]
    slots = jnp.concatenate([b[...].astype(f32) for b in blocks], axis=0).astype(bf16)
    refs[-1][...] = mm(back_table_ref[...], slots).astype(bf16)


def hidden_back_kernel(ids, hidden_ref, own_ref, got_ref, cot_ref, gain_ref, held_ref, grad_ref, low_ref, dgain_ref, all_ref):
    hidden = hidden_ref[...]
    grad_normed = own_ref[...].astype(f32) + got_ref[...].astype(f32)
    scale = lax.rsqrt(jnp.mean(hidden * hidden, axis=1, keepdims=True) + norm_eps)
    dgain_ref[...] = jnp.sum(grad_normed * hidden * scale, axis=0, keepdims=True)
    pulled = gain_ref[...] * grad_normed
    inner = jnp.mean(pulled * hidden, axis=1, keepdims=True)
    grad = cot_ref[...].astype(f32) + scale * pulled - hidden * (scale * scale * scale) * inner
    low_ref[...] = grad.astype(bf16)
    all_ref[...] = grad
    rows = grad_ref.shape[0]
    grad_ref[...] = all_ref[pl.ds(pl.multiple_of(ids[2] * rows, rows), rows), :]


def returned_kernel(ids, table_ref, slots_ref, held_ref, keep_ref, send_ref):
    rows = keep_ref.shape[0]
    mine = table_ref[pl.ds(pl.multiple_of(ids[2] * rows, rows), rows), :]
    keep_ref[...] = mm(mine, slots_ref[...]).astype(bf16)
    theirs = table_ref[pl.ds(pl.multiple_of((1 - ids[2]) * rows, rows), rows), :]
    send_ref[...] = mm(theirs, slots_ref[...]).astype(bf16)


def activations_kernel(ids, hidden_ref, own_ref, got_ref, out_ref):
    rows = out_ref.shape[0]
    hidden = hidden_ref[pl.ds(pl.multiple_of(ids[2] * rows, rows), rows), :]
    out_ref[...] = (hidden + (own_ref[...].astype(f32) + got_ref[...].astype(f32))).astype(bf16)


def normed_sum_kernel(ids, keep_ref, got_ref, held_ref, own_ref, send_ref, all_ref):
    all_ref[...] = keep_ref[...] + got_ref[...].astype(f32)
    rows = own_ref.shape[0]
    own_ref[...] = all_ref[pl.ds(pl.multiple_of(ids[2] * rows, rows), rows), :]
    theirs = pl.ds(pl.multiple_of((1 - ids[2]) * rows, rows), rows)
    send_ref[...] = all_ref[theirs, :].astype(bf16)


def heads_back(heads, first, qkv_ref, gm_ref, probs, dqkv_ref, diag_ref, ds_ref):
    seq = qkv_ref.shape[0]
    width = heads * HD
    here = len(probs) * HD
    span = seq + BACK_TILE
    flip = (
        lax.broadcasted_iota(jnp.int32, (BACK_TILE, BACK_TILE), 0)
        + lax.broadcasted_iota(jnp.int32, (BACK_TILE, BACK_TILE), 1)
        == BACK_TILE - 1
    ).astype(bf16)
    for h, probs_ref in enumerate(probs):
        at = (first + h) * HD
        to = h * HD
        key = qkv_ref[:, width + at : width + at + HD]
        value = qkv_ref[:, 2 * width + at : 2 * width + at + HD]
        for i in range(0, seq, BACK_TILE):
            probs_rows = probs_ref[i : i + BACK_TILE, :].astype(f32)
            grad_probs = mm_bt(gm_ref[i : i + BACK_TILE, at : at + HD], value)
            inner = jnp.sum(probs_rows * grad_probs, axis=1, keepdims=True)
            grad_scores = (probs_rows * (grad_probs - inner)).astype(bf16)
            ds_ref[i : i + BACK_TILE, :] = grad_scores
            dqkv_ref[i : i + BACK_TILE, to : to + HD] = (mm(grad_scores, key) * HD**-0.5).astype(bf16)
            flipped = mm(flip, grad_scores)
            padded = jnp.concatenate([flipped, jnp.zeros((BACK_TILE, BACK_TILE), f32)], axis=1)
            skewed = pltpu.roll(padded, 0, 1, stride=1, stride_axis=0)
            base = seq - BACK_TILE - i
            row = first + h
            diag_ref[row : row + 1, base : base + span] += jnp.sum(skewed, axis=0, keepdims=True)
        dqkv_ref[:, here + to : here + to + HD] = (
            mm_at(ds_ref[...], qkv_ref[:, at : at + HD]) * HD**-0.5
        ).astype(bf16)
        dqkv_ref[:, 2 * here + to : 2 * here + to + HD] = mm_at(
            probs_ref[...], gm_ref[:, at : at + HD]
        ).astype(bf16)


def send_rows(parts, me, gw_ref, outs):
    if parts == 1:
        outs[0][...] = gw_ref[...].astype(bf16)
        return
    rows = gw_ref.shape[0] // parts
    for i in range(parts // 2):
        at = slice(i * rows, (i + 1) * rows)
        outs[0][at, :] = gw_ref[pl.ds(pl.multiple_of((me ^ 2 * i) * rows, rows), rows), :]
        there = pl.ds(pl.multiple_of((me ^ 2 * i ^ 1) * rows, rows), rows)
        outs[1][at, :] = gw_ref[there, :].astype(bf16)


def first_back_kernel(heads, parts, ids, own_ref, other_ref, gain_ref, *refs):
    wo_ref, qkv_ref, probs_ref, x_ref, mixed_ref = refs[:5]
    gm_ref, dqkv_ref, diag_ref, seq_ref, *outs = refs[5:-3]
    ga_ref, ds_ref, gw_ref = refs[-3:]
    core = ids[0]
    half = own_ref.shape[0]
    ga_ref[pl.ds(pl.multiple_of(core * half, half), half), :] = own_ref[...]
    ga_ref[pl.ds(pl.multiple_of((1 - core) * half, half), half), :] = other_ref[...]
    gm_ref[...] = mm(ga_ref[...], wo_ref[...]).astype(bf16)
    diag_ref[...] = jnp.zeros_like(diag_ref)
    heads_back(heads, 0, qkv_ref, gm_ref, [probs_ref], dqkv_ref, diag_ref, ds_ref)
    cut = dqkv_ref.shape[1]
    seq_ref[...] = (unit_rows(x_ref[...]) * gain_ref[...]).astype(bf16)
    gw_ref[:, :cut] = mm_at(seq_ref[...], dqkv_ref[...])
    gw_ref[:, cut:] = mm_at(ga_ref[...], mixed_ref[...])
    send_rows(parts, ids[1], gw_ref, outs)


def second_back_kernel(
    heads, parts, ids, gm_ref, first_ref, diag_in_ref, hot_ref, seq_ref, gain_ref, router_ref, *refs
):
    count = heads + 2
    qkv_ref, *probs, x_ref, w_ref = refs[:count]
    refs = refs[count:]
    keep_ref, send_ref, small_ref, *outs = refs[:-5]
    diag_ref, dqkv_ref, all_ref, ds_ref, gw_ref = refs[-5:]
    core, me, side = ids[0], ids[1], ids[2]
    half = keep_ref.shape[0]
    diag_ref[...] = diag_in_ref[...]
    heads_back(heads, 1, qkv_ref, gm_ref, probs, dqkv_ref, diag_ref, ds_ref)
    gw_ref[...] = mm_at(seq_ref[...], dqkv_ref[...])
    send_rows(parts, me, gw_ref, outs)
    rest = (heads - 1) * HD
    for i in range(3):
        at = i * heads * HD
        all_ref[:, at : at + HD] = first_ref[:, i * HD : (i + 1) * HD]
        all_ref[:, at + HD : at + heads * HD] = dqkv_ref[:, i * rest : (i + 1) * rest]
    gain = jnp.zeros((1, x_ref.shape[1]), f32)
    for place, mine in ((core, True), (1 - core, False)):
        rows = pl.ds(pl.multiple_of(place * half, half), half)
        grad = mm_bt(all_ref[rows, :], w_ref[:, : all_ref.shape[1]])
        gain = gain + jnp.sum(grad * unit_rows(x_ref[rows, :]), axis=0, keepdims=True)
        if mine:
            keep_ref[...] = grad
        else:
            send_ref[...] = grad.astype(bf16)
    small_ref[...] = jnp.zeros_like(small_ref)
    small_ref[0:1, :] = gain
    small_ref[1:2, :] = jnp.where(side == 0, gain_ref[...], 0.0)
    experts = router_ref.shape[0]
    small_ref[2 : 2 + experts, :] = router_ref[...]
    bias = jnp.dot(diag_ref[...], hot_ref[...], precision=exact, preferred_element_type=f32)
    lanes = bias.shape[1]
    for i in range(2 * GROUP):
        small_ref[2 + experts : 2 + experts + heads, i * lanes : (i + 1) * lanes] = jnp.where(
            side * GROUP + core == i, bias[:heads, :], 0.0
        )


def fold_kernel(
    keep_ref, got_ref, small_ref, small_got_ref, second_ref, grad_ref, returned_ref,
    second_out, grad_out, returned_out, small_out, own_ref, *sends
):
    grad_out[...] = grad_ref[...]
    returned_out[...] = returned_ref[...]
    end, cols = second_ref.shape
    high = small_ref.shape[0]
    second_out[:end, :] = second_ref[...]
    for i in range(2):
        at = slice(i * cols, (i + 1) * cols)
        low = (small_ref[:, at] + small_got_ref[:, at]).astype(bf16)
        second_out[end + i * high : end + (i + 1) * high, :] = low
        small_out[i * high : (i + 1) * high, :] = low.astype(f32)
    total = keep_ref[...] + got_ref[...].astype(f32)
    rows = own_ref.shape[0]
    own_ref[...] = total[:rows, :]
    for i, send in enumerate(sends):
        send[...] = total[(i + 1) * rows : (i + 2) * rows, :].astype(bf16)


def quarters(refs, at):
    a, b, c, d = (r[at, :].astype(f32) for r in refs)
    return (a + b) + (c + d)


def split_cores(core, refs, keep_ref, send_ref):
    rows = keep_ref.shape[0]
    keep_ref[...] = quarters(refs, pl.ds(pl.multiple_of(core * rows, rows), rows))
    send_ref[:rows, :] = quarters(refs, pl.ds(pl.multiple_of((1 - core) * rows, rows), rows))


def fold_second_kernel(ids, keep_ref, got_ref, small_ref, grad_ref, *refs):
    first = refs[:4]
    grad_out, keep_one_ref, send_one_ref, own_ref, *sends = refs[4:]
    grad_out[...] = grad_ref[...]
    end = keep_ref.shape[0]
    total = keep_ref[...] + got_ref[:end, :].astype(f32)
    small = (small_ref[...] + got_ref[end:, :].astype(f32)).astype(bf16)
    rows = keep_one_ref.shape[0] * 2
    for i, block in enumerate((own_ref, *sends)):
        block[:rows, :] = total[i * rows : (i + 1) * rows, :].astype(block.dtype)
        block[rows:, :] = small.astype(block.dtype)
    split_cores(ids[0], first, keep_one_ref, send_one_ref)


def sum_nodes_kernel(ids, *refs):
    second = refs[:4]
    keep_ref, send_ref = refs[-2:]
    split_cores(ids[0], second, keep_ref, send_ref)
    rows = keep_ref.shape[0]
    send_ref[rows:, :] = quarters(second, slice(2 * rows, second[0].shape[0]))


def columns_kernel(heads, ids, keep_one, got_one, keep_two, got_two, *refs):
    outs = refs[:4] if len(refs) == 4 else refs[1:5]
    core = ids[0]
    rows = keep_one.shape[0]
    cols = heads * HD
    rest = cols - HD
    for c in range(2):
        at = c * cols
        mine = core == c
        one = jnp.where(mine, keep_one[...], got_one[...])
        two = jnp.where(mine, keep_two[...], got_two[:rows, :])
        for i in range(3):
            outs[i][:, at : at + HD] = one[:, i * HD : (i + 1) * HD]
            outs[i][:, at + HD : at + cols] = two[:, i * rest : (i + 1) * rest]
        outs[3][:, at : at + cols] = one[:, 3 * HD : 3 * HD + cols]
    if len(refs) == 4:
        return
    gain_one_ref, gain_two_ref, router_ref, bias_ref = refs[5:]
    small = refs[0][rows:, :] + got_two[rows:, :]
    high = small.shape[0] // 2
    wide = jnp.concatenate([small[:high, :], small[high:, :]], axis=1)
    experts = router_ref.shape[0]
    gain_one_ref[...] = wide[0:1, :]
    gain_two_ref[...] = wide[1:2, :]
    router_ref[...] = wide[2 : 2 + experts, :]
    for i in range(2 * GROUP):
        for h in range(heads):
            row = 2 + experts + h
            bias_ref[i * heads + h : i * heads + h + 1, :] = wide[
                row : row + 1, i * 128 : i * 128 + bias_ref.shape[1]
            ]


def input_kernel(keep_ref, got_ref, grad_ref, x_ref, gain_ref, out_ref):
    grad_normed = keep_ref[...] + got_ref[...].astype(f32)
    wide = x_ref[...].astype(f32)
    scale = lax.rsqrt(jnp.mean(wide * wide, axis=1, keepdims=True) + norm_eps)
    pulled = gain_ref[...] * grad_normed
    inner = jnp.mean(pulled * wide, axis=1, keepdims=True)
    out_ref[...] = grad_ref[...] + scale * pulled - wide * (scale * scale * scale) * inner


def in_order(first, mine, other):
    return jnp.where(first, jnp.concatenate([mine, other]), jnp.concatenate([other, mine]))


def per_device(
    tokens,
    gain_one,
    w_query,
    w_key,
    w_value,
    w_out,
    bias_table,
    gain_two,
    w_router,
    w_up,
    w_down,
    routes,
    doc_lengths,
    buckets,
    cotangent,
):
    own_rows, width = tokens.shape
    block_rows = routes.shape[0]
    seq = block_rows * GROUP
    cols = w_query.shape[1] // GROUP
    heads = cols // HD
    experts = w_router.shape[1]
    capacity = max(2, (5 * block_rows + 4 * experts - 1) // (4 * experts))
    slots = experts * capacity
    nodes = lax.axis_size("node")
    core = lax.axis_index("core")
    side = lax.axis_index("tensor")
    me = lax.axis_index("node")
    direct = nodes == DIRECT
    parts = nodes if direct else 1
    ids = jnp.stack([core, me, side]).astype(jnp.int32)
    node_rows = width // nodes

    def trade(blocks):
        if direct:
            return [blocks[0]] + [across(blocks[i], "node", i) for i in range(1, nodes)]
        stacked = blocks[0].reshape(nodes, -1, blocks[0].shape[1])
        back = lax.all_to_all(stacked, "node", split_axis=0, concat_axis=0, tiled=True)
        return [back.reshape(blocks[0].shape)]

    def trade_natural(rows):
        stacked = rows.reshape(nodes, -1, rows.shape[-1])
        return lax.all_to_all(stacked, "node", split_axis=0, concat_axis=0, tiled=True)

    share = out((w_query.shape[0], 4 * cols), bf16)
    share_kept, share_sent = call(
        shares_kernel,
        "shares",
        [share, share],
        [ids, *(Far(w) for w in (w_query, w_key, w_value, w_out))],
        smem=1,
        scratch=[pltpu.VMEM((4, *w_query.shape), bf16), pltpu.SemaphoreType.DMA((4,))],
    )
    piece = in_order(core == 0, share_kept, across(share_sent, "core", 1))
    if direct:
        pieces = {0: piece}
        for i in (4, 6, 2):
            pieces[i] = across(piece, "node", i)
        for i in (0, 2, 4, 6):
            pieces[i + 1] = across(pieces[i], "node", 1)
        pieces = [pieces[i] for i in range(nodes)]
    else:
        pieces = [lax.all_gather(piece, "node", axis=0, tiled=True)]

    x_rows = call(
        rows_kernel,
        "rows",
        [out((block_rows, width), bf16)],
        [ids, tokens, across(tokens, "tensor", 1), Raw(pieces[min(1, parts - 1)])],
        smem=1,
    )[0]
    x_other = across(x_rows, "core", 1)
    gain_first = gain_one.astype(f32)[None, :]
    gain_second = gain_two.astype(f32)[None, :]

    expert_ids = routes[:, 0]
    picks = (expert_ids[:, None] == jnp.arange(experts, dtype=jnp.int32)[None, :]).astype(jnp.int32)
    slot_index = jnp.sum((jnp.cumsum(picks, axis=0) - 1) * picks, axis=1)
    target = expert_ids * capacity + slot_index
    codes = jnp.arange(slots, dtype=jnp.int32)
    turned = ((codes // capacity) ^ me) * capacity + codes % capacity if direct else codes
    table = (turned[:, None] == target[None, :]).astype(bf16)
    back_table = (target[:, None] == turned[None, :]).astype(bf16)
    plain_table = (codes[:, None] == target[None, :]).astype(bf16)
    plain_back_table = (target[:, None] == codes[None, :]).astype(bf16)

    lengths_row = lax.dynamic_slice_in_dim(doc_lengths, me, 1, 0)[0]
    ends = jnp.cumsum(lengths_row)
    places = jnp.arange(seq, dtype=jnp.int32)
    docs = jnp.sum((ends[None, :] <= places[:, None]).astype(jnp.int32), axis=1)
    bucket_count = bias_table.shape[0]
    bucket_hot = (
        jnp.pad(buckets, (0, 1))[:, None] == jnp.arange(128, dtype=jnp.int32)[None, :]
    ).astype(f32)
    head_start = (side * GROUP + core) * heads
    bias_here = lax.dynamic_slice_in_dim(bias_table, head_start, heads, 1)
    bias_here = jnp.pad(bias_here, ((0, 128 - bucket_count), (0, 0)))
    bias_vectors = lax.dot_general(
        bias_here, bucket_hot, (((0,), (1,)), ((), ())), precision=exact, preferred_element_type=f32
    )

    weights, wo, x_seq, qkv, mixed, mixed_kept, mixed_sent, *probs = call(
        functools.partial(attend_kernel, heads, parts),
        "attend",
        [
            out((width, 4 * cols), bf16),
            out((width, cols), bf16),
            out((seq, width), bf16),
            out((seq, 3 * cols), bf16),
            out((seq, cols), bf16),
            out((block_rows, cols), bf16),
            out((block_rows, cols), bf16),
            *([out((seq, seq), bf16)] * heads),
        ],
        [
            ids,
            x_rows,
            Near(x_other),
            gain_first,
            bias_vectors,
            docs[:, None],
            docs[None, :],
            *(Near(p) for p in pieces),
        ],
        smem=1,
        scratch=[pltpu.VMEM((seq, width), bf16)],
    )
    kept = [weights, wo, x_seq, qkv, mixed, *probs]
    weights, wo_far, x_seq, qkv, mixed, *probs = call(
        functools.partial(move_kernel, len(kept)),
        "park",
        [Far(out(a.shape, a.dtype)) for a in kept],
        [*(Near(a) for a in kept)],
        scratch=[pltpu.SemaphoreType.DMA((len(kept),))],
    )

    natural = (nodes, slots // nodes, width) if direct else (slots, width)
    cot_slots = call(
        slots_kernel,
        "cot_slots",
        [out((slots, width), bf16)],
        [plain_table, cotangent, Raw(mixed_sent)],
    )[0]
    cots_own = trade_natural(cot_slots).reshape(natural)
    cots_other = across(cots_own, "core", 1)

    mixed_got = across(mixed_sent, "core", 1)
    attended = call(
        attended_kernel,
        "attended",
        [out((block_rows, width), bf16)],
        [mixed_kept, mixed_got, wo, across(wo, "core", 1), Far(mixed)],
    )[0]
    attended_got = across(attended, "tensor", 1)
    block_shapes = [out((slots // parts, width), bf16)] * parts
    hidden, *blocks = call(
        dispatch_kernel,
        "dispatch",
        [Near(out((block_rows, width), f32)), *block_shapes],
        [Near(x_rows), attended, Near(attended_got), gain_second, Near(table)],
    )
    received = trade(blocks)
    cots, back_active = call(
        functools.partial(cots_kernel, parts),
        "cots",
        [Near(out((2 * slots, width), bf16)), Near(out((2 * slots, w_down.shape[1]), f32))],
        [ids, Near(cots_own), Near(cots_other), w_down, Raw(blocks[0])],
        smem=1,
        scratch=[pltpu.VMEM((slots, width), f32)] if direct else [],
    )
    slots_own = jnp.concatenate(received)
    slots_other = across(slots_own, "core", 1)
    active, grad_upward, chosen, grad_kept, grad_sent, router_part, slots_all = call(
        expert_kernel,
        "expert",
        [
            Near(out((2 * slots, w_up.shape[1]), bf16)),
            Near(out((2 * slots, w_up.shape[1]), bf16)),
            Near(out((2 * slots, 1), f32)),
            out((slots, width), f32),
            out((slots, width), bf16),
            Near(out(w_router.shape[::-1], f32)),
            Near(out((2 * slots, width), bf16)),
        ],
        [ids, slots_own, Near(slots_other), Near(back_active), w_up, w_router.T],
        smem=1,
    )
    grad_blocks = call(
        join_kernel, "join_grad", block_shapes, [grad_kept, Near(across(grad_sent, "core", 1))]
    )
    grad_back = trade(grad_blocks)
    grad_normed_two = call(
        gather_kernel,
        "gather_grad",
        [out((block_rows, width), bf16)],
        [Near(back_table), *grad_back],
    )[0]
    grad_normed_two_got = across(grad_normed_two, "tensor", 1)

    out_kept, out_sent = call(
        expert_out_kernel,
        "expert_out",
        [out((slots, width), f32), out((slots, width), bf16)],
        [Near(active), Near(chosen), w_down, Raw(grad_blocks[-1])],
    )
    out_slots = call(
        functools.partial(join_natural_kernel, parts),
        "join_out",
        [out(natural, bf16)],
        [ids, out_kept, Near(across(out_sent, "core", 1))],
        smem=1,
    )[0]
    out_back = trade_natural(out_slots.reshape(slots, width)).reshape(slots, width)
    half_block = (own_rows, width)

    kept = [weights, wo_far, x_seq, qkv, mixed, *probs]
    weights, wo, x_seq, qkv, mixed, *probs = call(
        functools.partial(move_kernel, len(kept)),
        "unpark",
        [out(a.shape, a.dtype) for a in kept],
        [*(Far(a) for a in kept), Raw(out_slots)],
        scratch=[pltpu.SemaphoreType.DMA((len(kept),))],
    )
    grad_hidden, grad_attended, gain_two_part = call(
        hidden_back_kernel,
        "hidden_back",
        [Near(out(half_block, f32)), out((block_rows, width), bf16), Near(out((1, width), f32))],
        [
            ids,
            Near(hidden),
            grad_normed_two,
            Near(grad_normed_two_got),
            cotangent,
            gain_second,
            Raw(mixed),
        ],
        smem=1,
        scratch=[pltpu.VMEM((block_rows, width), f32)],
    )
    grad_attended_other = across(grad_attended, "core", 1)
    chunk = 3 * HD + cols
    other_chunk = 3 * (cols - HD)
    small_rows = -(-(2 + experts + heads) // 16) * 16
    if direct:
        first_shapes = [out((width // 2, chunk), t) for t in (f32, bf16)]
        second_shapes = [out((width // 2, other_chunk), t) for t in (f32, bf16)]
    else:
        first_shapes = [out((width, chunk), bf16)]
        second_shapes = [out((width, other_chunk), bf16)]
    grad_mixed, first_dqkv, diagonals, normed_seq, *first_chunk = call(
        functools.partial(first_back_kernel, heads, parts),
        "first_back",
        [
            out((seq, cols), bf16),
            out((seq, 3 * HD), bf16),
            out((8, 2 * seq), f32),
            out((seq, width), bf16),
            *first_shapes,
        ],
        [
            ids,
            grad_attended,
            Near(grad_attended_other),
            gain_first,
            *(wo, qkv, probs[0], x_seq, mixed),
        ],
        smem=1,
        flops=FLOPS1,
        scratch=[
            pltpu.VMEM((seq, width), bf16),
            pltpu.VMEM((seq, seq), bf16),
            pltpu.VMEM((width, chunk), f32),
        ],
    )
    grad_kept, grad_sent, small, *second_chunk = call(
        functools.partial(second_back_kernel, heads, parts),
        "second_back",
        [
            out((block_rows, width), f32),
            out((block_rows, width), bf16),
            out((small_rows, width), f32),
            *second_shapes,
        ],
        [
            ids,
            grad_mixed,
            first_dqkv,
            diagonals,
            bucket_hot,
            normed_seq,
            Near(gain_two_part),
            Near(router_part),
            *(qkv, *probs[1:], x_seq, weights),
        ],
        smem=1,
        flops=FLOPS2,
        scratch=[
            pltpu.VMEM((8, 2 * seq), f32),
            pltpu.VMEM((seq, other_chunk), bf16),
            pltpu.VMEM((seq, 3 * cols), bf16),
            pltpu.VMEM((seq, seq), bf16),
            pltpu.VMEM((width, other_chunk), f32),
        ],
    )

    shard_rows = w_query.shape[0]
    returned, returned_sent = call(
        returned_kernel,
        "returned",
        [out(half_block, bf16), out(half_block, bf16)],
        [ids, Near(plain_back_table), Near(out_back), Raw(grad_kept)],
        smem=1,
    )
    part = out((shard_rows, chunk), f32)
    if direct:
        tall = width // 2 + 2 * small_rows
        second_sent, grad_sent, returned_sent, small, own_one, *send_one = call(
            fold_kernel,
            "fold_first",
            [
                out((tall, chunk), bf16),
                out(grad_sent.shape, bf16),
                out(returned_sent.shape, bf16),
                out((2 * small_rows, chunk), f32),
                out((node_rows, chunk), f32),
                *([out((node_rows, chunk), bf16)] * 3),
            ],
            [
                first_chunk[0],
                across(first_chunk[1], "node", 1),
                small,
                across(small, "tensor", 1),
                second_chunk[1],
                grad_sent,
                returned_sent,
            ],
        )
        got_one = [across(b, "node", 2 * i + 2) for i, b in enumerate(send_one)]
        first_done = send_one[0]
    else:
        sums = [jnp.sum(trade_natural(c[0]).astype(f32), axis=0) for c in (first_chunk, second_chunk)]
        kept_one, kept_two = (
            lax.dynamic_slice_in_dim(s, core * shard_rows, shard_rows, 0) for s in sums
        )
        sent_one, sent_two = (
            lax.dynamic_slice_in_dim(s, (1 - core) * shard_rows, shard_rows, 0) for s in sums
        )
        first_done, second_done = kept_one, kept_two
    grad_normed, grad_normed_sent = call(
        normed_sum_kernel,
        "normed_sum",
        [Near(out(half_block, f32)), out(half_block, bf16)],
        [ids, grad_kept, Near(across(grad_sent, "core", 1)), Raw(first_done)],
        smem=1,
        scratch=[pltpu.VMEM((block_rows, width), f32)],
    )
    if direct:
        high = node_rows + 2 * small_rows
        grad_normed_sent, kept_one, sent_one, own_two, *send_two = call(
            fold_second_kernel,
            "fold_second",
            [out(half_block, bf16), part, part, out((high, chunk), f32), *([out((high, chunk), bf16)] * 3)],
            [
                ids,
                second_chunk[0],
                across(second_sent, "node", 1),
                small,
                grad_normed_sent,
                own_one,
                *got_one,
            ],
            smem=1,
        )
        got_two = [across(b, "node", 2 * i + 2) for i, b in enumerate(send_two)]
        second_done = send_two[0]
    grad_w_up_here, grad_w_down_here = call(
        expert_grads_kernel,
        "expert_grads",
        [out(w_up.shape, f32), out(w_down.shape, f32)],
        [
            *(Near(a) for a in (slots_all, cots, active, grad_upward, chosen)),
            Raw(second_done),
        ],
    )
    input_grad = call(
        input_kernel,
        "input_grad",
        [out(half_block, f32)],
        [
            Near(grad_normed),
            Near(across(grad_normed_sent, "tensor", 1)),
            Near(grad_hidden),
            tokens,
            gain_first,
        ],
    )[0]
    activations = call(
        activations_kernel,
        "activations",
        [out(half_block, bf16)],
        [ids, Near(hidden), Near(returned), Near(across(returned_sent, "tensor", 1))],
        smem=1,
    )[0]
    if direct:
        kept_two, sent_two = call(
            sum_nodes_kernel,
            "sum_nodes",
            [part, out((shard_rows + 2 * small_rows, chunk), f32)],
            [
                ids,
                own_two,
                *got_two,
                *(Far(a) for a in (grad_w_up_here, activations, input_grad)),
            ],
            smem=1,
        )
    got_one = across(sent_one, "core", 1)
    got_two = across(sent_two, "core", 1)
    small_outs = []
    if direct:
        small_outs = [
            out((1, width), f32),
            out((1, width), f32),
            out((experts, width), f32),
            out(bias_table.shape[::-1], f32),
        ]
    weight_grads = call(
        functools.partial(columns_kernel, heads),
        "columns",
        [out(w_query.shape, f32)] * 4 + small_outs,
        [ids, kept_one, got_one, kept_two, got_two] + ([sent_two] if direct else []),
        smem=1,
    )
    if direct:
        sum_one, sum_two, sum_router, sum_bias = weight_grads[4:]
    else:
        small = lax.psum(small, ("node", "core", "tensor"))
        sum_one, sum_two, sum_router = small[:1], small[1:2], small[2 : 2 + experts]
        sum_bias = small[2 + experts : 2 + experts + heads, : 4 * 128].reshape(heads, 4, 128)
        sum_bias = sum_bias[:, :, :bucket_count].transpose(1, 0, 2).reshape(bias_table.shape[::-1])
    return (
        activations,
        input_grad,
        sum_one[0],
        *weight_grads[:4],
        sum_bias.T,
        sum_two[0],
        sum_router.T,
        grad_w_up_here,
        grad_w_down_here,
    )


def solution(mesh):
    dp, tensor = mesh.shape["dp"], mesh.shape["tensor"]
    grid = Mesh(mesh.devices.reshape(dp // GROUP, GROUP, tensor), ("node", "core", "tensor"))
    dp = ("node", "core")
    every = ("node", "core", "tensor")
    in_specs = (
        P(every, None),
        P(),
        P(dp, "tensor"),
        P(dp, "tensor"),
        P(dp, "tensor"),
        P(dp, "tensor"),
        P(),
        P(),
        P(),
        P(None, every),
        P(None, every),
        P(dp, None),
        P(),
        P(),
        P(dp, None),
    )
    out_specs = (
        P(every, None),
        P(every, None),
        P(),
        P(dp, "tensor"),
        P(dp, "tensor"),
        P(dp, "tensor"),
        P(dp, "tensor"),
        P(),
        P(),
        P(),
        P(None, every),
        P(None, every),
    )
    return jax.shard_map(
        per_device, mesh=grid, in_specs=in_specs, out_specs=out_specs, check_vma=False
    )
```

```python
import functools

import jax
import jax.numpy as jnp
from jax import lax
from jax.experimental import pallas as pl
from jax.experimental.pallas import tpu as pltpu
from jax.sharding import Mesh, PartitionSpec as P

HD = 64
GROUP = 2
FLOPS1 = 0
FLOPS2 = 0
DIRECT = 8
FORWARD_TILE = 256
BACK_TILE = 512

norm_eps = 1e-06
masked_value = -1e30
exact = lax.Precision.HIGHEST
bf16 = jnp.bfloat16
f32 = jnp.float32

VMEM = pl.BlockSpec(memory_space=pltpu.VMEM)
SMEM = pl.BlockSpec(memory_space=pltpu.SMEM)
ANY = pl.BlockSpec(memory_space=pl.ANY)


def across(shard, axis, bits):
    return lax.ppermute(shard, axis, [(i, i ^ bits) for i in range(lax.axis_size(axis))])


class Near:
    def __init__(self, array):
        self.array = array


class Raw(Near):
    pass


class Far(Raw):
    pass


def call(body, name, outs, args, smem=0, scratch=(), flops=0):
    arrays = [a.array if isinstance(a, Near) else a for a in args]
    results = [o.array if isinstance(o, Near) else o for o in outs]
    kept = sum(padded_bytes(a) for a in [*arrays, *results, *scratch] if is_plain(a))
    space = {Near: pltpu.VMEM, Far: pltpu.HBM}
    given = [
        pltpu.with_memory_space_constraint(x, space[type(a)]) if type(a) in space else x
        for a, x in zip(args, arrays)
    ]
    return pl.pallas_call(
        body,
        name=name,
        out_shape=[
            space[type(o)](x.shape, x.dtype) if type(o) in space else x
            for o, x in zip(outs, results)
        ],
        in_specs=[SMEM] * smem + [ANY if isinstance(a, Raw) else VMEM for a in args[smem:]],
        out_specs=[ANY if isinstance(o, Raw) else VMEM for o in outs],
        scratch_shapes=scratch,
        compiler_params=pltpu.CompilerParams(vmem_limit_bytes=kept + 10 * 1024 * 1024),
        cost_estimate=pl.CostEstimate(flops=flops, bytes_accessed=0, transcendentals=0),
    )(*given)


def is_plain(array):
    return array.dtype in (bf16, f32, jnp.int32)


def padded_bytes(array):
    *lead, rows, cols = (1, 1, *array.shape)
    size = jnp.dtype(array.dtype).itemsize
    for extent in lead:
        size *= extent
    return size * (-(-rows // 16) * 16) * (-(-cols // 128) * 128)


def out(shape, dtype):
    return jax.ShapeDtypeStruct(shape, dtype)


def mm(a, b):
    return jnp.dot(a, b, preferred_element_type=f32)


def mm_bt(a, b):
    return lax.dot_general(a, b, (((1,), (1,)), ((), ())), preferred_element_type=f32)


def mm_at(a, b):
    return lax.dot_general(a, b, (((0,), (0,)), ((), ())), preferred_element_type=f32)


def shares_kernel(ids, *refs):
    weights, (keep_ref, send_ref, near_ref, sems) = refs[:4], refs[4:]
    copies = [
        pltpu.make_async_copy(w, near_ref.at[i], sems.at[i]) for i, w in enumerate(weights)
    ]
    for copy in copies:
        copy.start()
    for copy in copies:
        copy.wait()
    first = ids[0] == 0
    cols = keep_ref.shape[1] // 4
    for i in range(4):
        low, high = near_ref[i, :, :cols], near_ref[i, :, cols:]
        keep_ref[:, i * cols : (i + 1) * cols] = jnp.where(first, low, high)
        send_ref[:, i * cols : (i + 1) * cols] = jnp.where(first, high, low)


def rows_kernel(ids, own_ref, got_ref, held_ref, out_ref):
    rows = own_ref.shape[0]
    out_ref[pl.ds(pl.multiple_of(ids[2] * rows, rows), rows), :] = own_ref[...]
    out_ref[pl.ds(pl.multiple_of((1 - ids[2]) * rows, rows), rows), :] = got_ref[...]


def move_kernel(count, *refs):
    sources, targets, sems = refs[:count], refs[-count - 1 : -1], refs[-1]
    copies = [
        pltpu.make_async_copy(a, b, sems.at[i]) for i, (a, b) in enumerate(zip(sources, targets))
    ]
    for copy in copies:
        copy.start()
    for copy in copies:
        copy.wait()


def unit_rows(x):
    wide = x.astype(f32)
    return wide * lax.rsqrt(jnp.mean(wide * wide, axis=1, keepdims=True) + norm_eps)


def tables_kernel(experts, capacity, direct, ids, routes_ref, turned_ref, plain_ref):
    rows, slots = plain_ref.shape
    routes = routes_ref[...]
    picks = routes == lax.broadcasted_iota(jnp.int32, (rows, experts), 1)
    upto = lax.broadcasted_iota(jnp.int32, (rows, rows), 0) >= lax.broadcasted_iota(
        jnp.int32, (rows, rows), 1
    )
    counts = mm(upto.astype(f32).astype(bf16), picks.astype(f32).astype(bf16))
    slot = jnp.sum(jnp.where(picks, counts - 1.0, 0.0), axis=1, keepdims=True).astype(jnp.int32)
    codes = lax.broadcasted_iota(jnp.int32, (1, slots), 1)
    expert = jnp.zeros((1, slots), jnp.int32)
    for i in range(1, experts):
        expert = expert + jnp.where(codes >= i * capacity, 1, 0)
    place = codes - expert * capacity
    plain = (routes == expert) & (slot == place)
    plain_ref[...] = plain.astype(f32).astype(bf16)
    turned = (routes == (expert ^ ids[1])) & (slot == place) if direct else plain
    turned_ref[...] = turned.astype(f32).astype(bf16)


def slots_kernel(table_ref, rows_ref, held_ref, out_ref):
    out_ref[...] = mm_at(table_ref[...], rows_ref[...]).astype(bf16)


def cots_kernel(parts, ids, own_ref, other_ref, wdown_ref, held_ref, cots_ref, back_ref, near_ref, sems, *scratch):
    slots = cots_ref.shape[0] // 2
    copies = []
    me = ids[1]
    for at, source in ((0, own_ref), (slots, other_ref)):
        if parts == 1:
            near_ref[at : at + slots, :] = source[...]
        else:
            rows = slots // parts
            for i in range(parts):
                scratch[0][i * rows : (i + 1) * rows, :] = source[me ^ i].astype(f32)
            near_ref[at : at + slots, :] = scratch[0][...].astype(bf16)
        copies.append(
            pltpu.make_async_copy(near_ref.at[at : at + slots], cots_ref.at[at : at + slots], sems.at[len(copies)])
        )
        copies[-1].start()
        back_ref[at : at + slots, :] = mm(near_ref[at : at + slots, :], wdown_ref[...])
    for copy in copies:
        copy.wait()


def attend_kernel(heads, parts, ids, own_ref, other_ref, gain_ref, vec_ref, row_docs, col_docs, *refs):
    pieces = refs[:parts]
    w_ref, wo_ref, x_ref, qkv_ref, mixed_ref, keep_ref, send_ref, *probs_refs = refs[parts:-1]
    seq_ref = refs[-1]
    core = ids[0]
    me = ids[1]
    seq = x_ref.shape[0]
    width = heads * HD
    half = seq // GROUP
    span = seq + FORWARD_TILE
    rows = pieces[0].shape[0]
    for i, piece in enumerate(pieces):
        start = 0 if parts == 1 else pl.multiple_of((me ^ i) * rows, rows)
        w_ref[pl.ds(start, rows), :] = piece[...]
    for place, source in ((core, own_ref), (1 - core, other_ref)):
        at = pl.ds(pl.multiple_of(place * half, half), half)
        x = source[...]
        x_ref[at, :] = x
        seq_ref[at, :] = (unit_rows(x) * gain_ref[...]).astype(bf16)
    wo_ref[...] = w_ref[:, 3 * width :]
    for i in range(0, seq, 256):
        qkv_ref[i : i + 256, :] = mm(seq_ref[i : i + 256, :], w_ref[:, : 3 * width]).astype(bf16)
    for h in range(heads):
        at = h * HD
        key = qkv_ref[:, width + at : width + at + HD]
        value = qkv_ref[:, 2 * width + at : 2 * width + at + HD]
        for i in range(0, seq, FORWARD_TILE):
            base = seq - FORWARD_TILE - i
            seg = jnp.broadcast_to(vec_ref[h : h + 1, base : base + span], (FORWARD_TILE, span))
            bias = pltpu.roll(seg, span - FORWARD_TILE + 1, 1, stride=1, stride_axis=0)[:, :seq]
            scores = mm_bt(qkv_ref[i : i + FORWARD_TILE, at : at + HD], key) * HD**-0.5 + bias
            scores = jnp.where(row_docs[i : i + FORWARD_TILE, :] == col_docs[...], scores, masked_value)
            peak = jnp.max(scores, axis=1, keepdims=True)
            exp_scores = jnp.exp(scores - peak)
            probs = exp_scores / jnp.sum(exp_scores, axis=1, keepdims=True)
            probs_refs[h][i : i + FORWARD_TILE, :] = probs.astype(bf16)
            mixed_ref[i : i + FORWARD_TILE, at : at + HD] = mm(probs.astype(bf16), value).astype(bf16)
    keep_ref[...] = mixed_ref[pl.ds(pl.multiple_of(core * half, half), half), :]
    send_ref[...] = mixed_ref[pl.ds(pl.multiple_of((1 - core) * half, half), half), :]


def attended_kernel(keep_ref, got_ref, wo_ref, wo_other_ref, held_ref, out_ref):
    total = mm_bt(keep_ref[...], wo_ref[...]) + mm_bt(got_ref[...], wo_other_ref[...])
    out_ref[...] = total.astype(bf16)


def dispatch_kernel(hidden_ref, gain_ref, table_ref, *blocks):
    hidden = hidden_ref[...]
    scale = lax.rsqrt(jnp.mean(hidden * hidden, axis=1, keepdims=True) + norm_eps)
    normed = (hidden * scale * gain_ref[...]).astype(bf16)
    slots = mm_at(table_ref[...], normed)
    rows = blocks[0].shape[0]
    for i, block in enumerate(blocks):
        block[...] = slots[i * rows : (i + 1) * rows, :].astype(bf16)


def expert_kernel(ids, own_ref, other_ref, h_ref, wup_ref, wr_ref, *refs):
    active_ref, gup_ref, chosen_ref, keep_ref, send_ref, router_ref, all_ref = refs
    rows = own_ref.shape[0]
    step = rows // 2
    router = jnp.zeros(router_ref.shape, f32)
    root = 0.7978845608028654
    for i in range(0, 2 * rows, step):
        src = own_ref if i < rows else other_ref
        at = i % rows
        slots = src[at : at + step, :]
        all_ref[i : i + step, :] = slots
        logits = mm_bt(slots, wr_ref[...])
        peak = jnp.max(logits, axis=1, keepdims=True)
        exp_logits = jnp.exp(logits - peak)
        gates = exp_logits / jnp.sum(exp_logits, axis=1, keepdims=True)
        mine = lax.broadcasted_iota(jnp.int32, gates.shape, 1) == ids[1]
        chosen = jnp.sum(jnp.where(mine, gates, 0.0), axis=1, keepdims=True)
        chosen_ref[i : i + step, :] = chosen
        up = mm(slots, wup_ref[...])
        square = up * up
        bent = jnp.tanh(root * (up + 0.044715 * up * square))
        low = (0.5 * up * (1.0 + bent)).astype(bf16)
        active_ref[i : i + step, :] = low
        slope = 0.5 * (1.0 + bent) + 0.5 * up * (1.0 - bent * bent) * root * (
            1.0 + 3.0 * 0.044715 * square
        )
        back = h_ref[i : i + step, :]
        gup = (chosen * back * slope).astype(bf16)
        gup_ref[i : i + step, :] = gup
        grad_chosen = jnp.sum(low.astype(f32) * back, axis=1, keepdims=True)
        grad_logits = gates * (jnp.where(mine, 1.0, 0.0) - chosen) * grad_chosen
        grad_logits = grad_logits.astype(bf16)
        router = router + mm_at(grad_logits, slots)
        grad = mm_bt(gup, wup_ref[...]) + mm(grad_logits, wr_ref[...])
        if i < rows:
            keep_ref[at : at + step, :] = grad
        else:
            send_ref[at : at + step, :] = grad.astype(bf16)
    router_ref[...] = router


def expert_out_kernel(active_ref, chosen_ref, wdown_ref, held_ref, keep_ref, send_ref):
    rows = keep_ref.shape[0]
    result = mm_bt(active_ref[...], wdown_ref[...]) * chosen_ref[...]
    keep_ref[...] = result[:rows, :]
    send_ref[...] = result[rows:, :].astype(bf16)


def expert_grads_kernel(slots_ref, cots_ref, active_ref, gup_ref, chosen_ref, held_ref, gwup_ref, gwdown_ref):
    gwup_ref[...] = mm_at(slots_ref[...], gup_ref[...])
    grads = (chosen_ref[...] * cots_ref[...].astype(f32)).astype(bf16)
    gwdown_ref[...] = mm_at(grads, active_ref[...])


def join_kernel(keep_ref, got_ref, *blocks):
    total = keep_ref[...] + got_ref[...].astype(f32)
    rows = blocks[0].shape[0]
    for i, block in enumerate(blocks):
        block[...] = total[i * rows : (i + 1) * rows, :].astype(bf16)


def join_natural_kernel(parts, ids, keep_ref, got_ref, out_ref):
    total = keep_ref[...] + got_ref[...].astype(f32)
    if parts == 1:
        out_ref[...] = total.astype(bf16)
        return
    rows = out_ref.shape[1]
    for i in range(parts):
        out_ref[ids[1] ^ i] = total[i * rows : (i + 1) * rows, :].astype(bf16)


def gather_kernel(back_table_ref, *refs):
    blocks = refs[:-1]
    slots = jnp.concatenate([b[...].astype(f32) for b in blocks], axis=0).astype(bf16)
    refs[-1][...] = mm(back_table_ref[...], slots).astype(bf16)


def hidden_back_kernel(ids, hidden_ref, own_ref, got_ref, cot_ref, gain_ref, held_ref, grad_ref, low_ref, dgain_ref, all_ref):
    hidden = hidden_ref[...]
    grad_normed = own_ref[...].astype(f32) + got_ref[...].astype(f32)
    scale = lax.rsqrt(jnp.mean(hidden * hidden, axis=1, keepdims=True) + norm_eps)
    dgain_ref[...] = jnp.sum(grad_normed * hidden * scale, axis=0, keepdims=True)
    pulled = gain_ref[...] * grad_normed
    inner = jnp.mean(pulled * hidden, axis=1, keepdims=True)
    grad = cot_ref[...].astype(f32) + scale * pulled - hidden * (scale * scale * scale) * inner
    low_ref[...] = grad.astype(bf16)
    all_ref[...] = grad
    rows = grad_ref.shape[0]
    grad_ref[...] = all_ref[pl.ds(pl.multiple_of(ids[2] * rows, rows), rows), :]


def returned_kernel(ids, table_ref, slots_ref, held_ref, keep_ref, send_ref):
    rows = keep_ref.shape[0]
    mine = table_ref[pl.ds(pl.multiple_of(ids[2] * rows, rows), rows), :]
    keep_ref[...] = mm(mine, slots_ref[...]).astype(bf16)
    theirs = table_ref[pl.ds(pl.multiple_of((1 - ids[2]) * rows, rows), rows), :]
    send_ref[...] = mm(theirs, slots_ref[...]).astype(bf16)


def activations_kernel(ids, hidden_ref, own_ref, got_ref, out_ref):
    rows = out_ref.shape[0]
    hidden = hidden_ref[pl.ds(pl.multiple_of(ids[2] * rows, rows), rows), :]
    out_ref[...] = (hidden + (own_ref[...].astype(f32) + got_ref[...].astype(f32))).astype(bf16)


def normed_sum_kernel(ids, keep_ref, got_ref, held_ref, own_ref, send_ref, all_ref):
    all_ref[...] = keep_ref[...] + got_ref[...].astype(f32)
    rows = own_ref.shape[0]
    own_ref[...] = all_ref[pl.ds(pl.multiple_of(ids[2] * rows, rows), rows), :]
    theirs = pl.ds(pl.multiple_of((1 - ids[2]) * rows, rows), rows)
    send_ref[...] = all_ref[theirs, :].astype(bf16)


def heads_back(heads, first, qkv_ref, gm_ref, probs, dqkv_ref, diag_ref, ds_ref):
    seq = qkv_ref.shape[0]
    width = heads * HD
    here = len(probs) * HD
    span = seq + BACK_TILE
    flip = (
        lax.broadcasted_iota(jnp.int32, (BACK_TILE, BACK_TILE), 0)
        + lax.broadcasted_iota(jnp.int32, (BACK_TILE, BACK_TILE), 1)
        == BACK_TILE - 1
    ).astype(bf16)
    for h, probs_ref in enumerate(probs):
        at = (first + h) * HD
        to = h * HD
        key = qkv_ref[:, width + at : width + at + HD]
        value = qkv_ref[:, 2 * width + at : 2 * width + at + HD]
        for i in range(0, seq, BACK_TILE):
            probs_rows = probs_ref[i : i + BACK_TILE, :].astype(f32)
            grad_probs = mm_bt(gm_ref[i : i + BACK_TILE, at : at + HD], value)
            inner = jnp.sum(probs_rows * grad_probs, axis=1, keepdims=True)
            grad_scores = (probs_rows * (grad_probs - inner)).astype(bf16)
            ds_ref[i : i + BACK_TILE, :] = grad_scores
            dqkv_ref[i : i + BACK_TILE, to : to + HD] = (mm(grad_scores, key) * HD**-0.5).astype(bf16)
            flipped = mm(flip, grad_scores)
            padded = jnp.concatenate([flipped, jnp.zeros((BACK_TILE, BACK_TILE), f32)], axis=1)
            skewed = pltpu.roll(padded, 0, 1, stride=1, stride_axis=0)
            base = seq - BACK_TILE - i
            row = first + h
            diag_ref[row : row + 1, base : base + span] += jnp.sum(skewed, axis=0, keepdims=True)
        dqkv_ref[:, here + to : here + to + HD] = (
            mm_at(ds_ref[...], qkv_ref[:, at : at + HD]) * HD**-0.5
        ).astype(bf16)
        dqkv_ref[:, 2 * here + to : 2 * here + to + HD] = mm_at(
            probs_ref[...], gm_ref[:, at : at + HD]
        ).astype(bf16)


def send_rows(parts, me, gw_ref, outs):
    if parts == 1:
        outs[0][...] = gw_ref[...].astype(bf16)
        return
    rows = gw_ref.shape[0] // parts
    for i in range(parts // 2):
        at = slice(i * rows, (i + 1) * rows)
        outs[0][at, :] = gw_ref[pl.ds(pl.multiple_of((me ^ 2 * i) * rows, rows), rows), :]
        there = pl.ds(pl.multiple_of((me ^ 2 * i ^ 1) * rows, rows), rows)
        outs[1][at, :] = gw_ref[there, :].astype(bf16)


def first_back_kernel(heads, parts, ids, own_ref, other_ref, gain_ref, *refs):
    wo_ref, qkv_ref, probs_ref, x_ref, mixed_ref = refs[:5]
    gm_ref, dqkv_ref, diag_ref, seq_ref, *outs = refs[5:-3]
    ga_ref, ds_ref, gw_ref = refs[-3:]
    core = ids[0]
    half = own_ref.shape[0]
    ga_ref[pl.ds(pl.multiple_of(core * half, half), half), :] = own_ref[...]
    ga_ref[pl.ds(pl.multiple_of((1 - core) * half, half), half), :] = other_ref[...]
    gm_ref[...] = mm(ga_ref[...], wo_ref[...]).astype(bf16)
    diag_ref[...] = jnp.zeros_like(diag_ref)
    heads_back(heads, 0, qkv_ref, gm_ref, [probs_ref], dqkv_ref, diag_ref, ds_ref)
    cut = dqkv_ref.shape[1]
    seq_ref[...] = (unit_rows(x_ref[...]) * gain_ref[...]).astype(bf16)
    gw_ref[:, :cut] = mm_at(seq_ref[...], dqkv_ref[...])
    gw_ref[:, cut:] = mm_at(ga_ref[...], mixed_ref[...])
    send_rows(parts, ids[1], gw_ref, outs)


def second_back_kernel(
    heads, parts, ids, gm_ref, first_ref, diag_in_ref, hot_ref, seq_ref, gain_ref, router_ref, *refs
):
    count = heads + 2
    qkv_ref, *probs, x_ref, w_ref = refs[:count]
    refs = refs[count:]
    keep_ref, send_ref, small_ref, *outs = refs[:-5]
    diag_ref, dqkv_ref, all_ref, ds_ref, gw_ref = refs[-5:]
    core, me, side = ids[0], ids[1], ids[2]
    half = keep_ref.shape[0]
    diag_ref[...] = diag_in_ref[...]
    heads_back(heads, 1, qkv_ref, gm_ref, probs, dqkv_ref, diag_ref, ds_ref)
    gw_ref[...] = mm_at(seq_ref[...], dqkv_ref[...])
    send_rows(parts, me, gw_ref, outs)
    rest = (heads - 1) * HD
    for i in range(3):
        at = i * heads * HD
        all_ref[:, at : at + HD] = first_ref[:, i * HD : (i + 1) * HD]
        all_ref[:, at + HD : at + heads * HD] = dqkv_ref[:, i * rest : (i + 1) * rest]
    gain = jnp.zeros((1, x_ref.shape[1]), f32)
    for place, mine in ((core, True), (1 - core, False)):
        rows = pl.ds(pl.multiple_of(place * half, half), half)
        grad = mm_bt(all_ref[rows, :], w_ref[:, : all_ref.shape[1]])
        gain = gain + jnp.sum(grad * unit_rows(x_ref[rows, :]), axis=0, keepdims=True)
        if mine:
            keep_ref[...] = grad
        else:
            send_ref[...] = grad.astype(bf16)
    small_ref[...] = jnp.zeros_like(small_ref)
    small_ref[0:1, :] = gain
    small_ref[1:2, :] = jnp.where(side == 0, gain_ref[...], 0.0)
    experts = router_ref.shape[0]
    small_ref[2 : 2 + experts, :] = router_ref[...]
    bias = jnp.dot(diag_ref[...], hot_ref[...], precision=exact, preferred_element_type=f32)
    lanes = bias.shape[1]
    for i in range(2 * GROUP):
        small_ref[2 + experts : 2 + experts + heads, i * lanes : (i + 1) * lanes] = jnp.where(
            side * GROUP + core == i, bias[:heads, :], 0.0
        )


def fold_kernel(
    keep_ref, got_ref, small_ref, small_got_ref, second_ref, returned_ref,
    second_out, returned_out, small_out, own_ref, *sends
):
    returned_out[...] = returned_ref[...]
    end, cols = second_ref.shape
    high = small_ref.shape[0]
    second_out[:end, :] = second_ref[...]
    for i in range(2):
        at = slice(i * cols, (i + 1) * cols)
        low = (small_ref[:, at] + small_got_ref[:, at]).astype(bf16)
        second_out[end + i * high : end + (i + 1) * high, :] = low
        small_out[i * high : (i + 1) * high, :] = low.astype(f32)
    total = keep_ref[...] + got_ref[...].astype(f32)
    rows = own_ref.shape[0]
    own_ref[...] = total[:rows, :]
    for i, send in enumerate(sends):
        send[...] = total[(i + 1) * rows : (i + 2) * rows, :].astype(bf16)


def quarters(refs, at):
    a, b, c, d = (r[at, :].astype(f32) for r in refs)
    return (a + b) + (c + d)


def split_cores(core, refs, keep_ref, send_ref):
    rows = keep_ref.shape[0]
    keep_ref[...] = quarters(refs, pl.ds(pl.multiple_of(core * rows, rows), rows))
    send_ref[:rows, :] = quarters(refs, pl.ds(pl.multiple_of((1 - core) * rows, rows), rows))


def fold_second_kernel(ids, keep_ref, got_ref, small_ref, grad_ref, *refs):
    first = refs[:4]
    grad_out, keep_one_ref, send_one_ref, own_ref, *sends = refs[4:]
    grad_out[...] = grad_ref[...]
    end = keep_ref.shape[0]
    total = keep_ref[...] + got_ref[:end, :].astype(f32)
    small = (small_ref[...] + got_ref[end:, :].astype(f32)).astype(bf16)
    rows = keep_one_ref.shape[0] * 2
    for i, block in enumerate((own_ref, *sends)):
        block[:rows, :] = total[i * rows : (i + 1) * rows, :].astype(block.dtype)
        block[rows:, :] = small.astype(block.dtype)
    split_cores(ids[0], first, keep_one_ref, send_one_ref)


def sum_nodes_kernel(ids, *refs):
    second = refs[:4]
    keep_ref, send_ref = refs[-2:]
    split_cores(ids[0], second, keep_ref, send_ref)
    rows = keep_ref.shape[0]
    send_ref[rows:, :] = quarters(second, slice(2 * rows, second[0].shape[0]))


def columns_kernel(heads, ids, keep_one, got_one, keep_two, got_two, *refs):
    outs = refs[:4] if len(refs) == 4 else refs[1:5]
    core = ids[0]
    rows = keep_one.shape[0]
    cols = heads * HD
    rest = cols - HD
    for c in range(2):
        at = c * cols
        mine = core == c
        one = jnp.where(mine, keep_one[...], got_one[...])
        two = jnp.where(mine, keep_two[...], got_two[:rows, :])
        for i in range(3):
            outs[i][:, at : at + HD] = one[:, i * HD : (i + 1) * HD]
            outs[i][:, at + HD : at + cols] = two[:, i * rest : (i + 1) * rest]
        outs[3][:, at : at + cols] = one[:, 3 * HD : 3 * HD + cols]
    if len(refs) == 4:
        return
    gain_one_ref, gain_two_ref, router_ref, bias_ref = refs[5:]
    small = refs[0][rows:, :] + got_two[rows:, :]
    high = small.shape[0] // 2
    wide = jnp.concatenate([small[:high, :], small[high:, :]], axis=1)
    experts = router_ref.shape[0]
    gain_one_ref[...] = wide[0:1, :]
    gain_two_ref[...] = wide[1:2, :]
    router_ref[...] = wide[2 : 2 + experts, :]
    for i in range(2 * GROUP):
        for h in range(heads):
            row = 2 + experts + h
            bias_ref[i * heads + h : i * heads + h + 1, :] = wide[
                row : row + 1, i * 128 : i * 128 + bias_ref.shape[1]
            ]


def input_kernel(keep_ref, got_ref, grad_ref, x_ref, gain_ref, out_ref):
    grad_normed = keep_ref[...] + got_ref[...].astype(f32)
    wide = x_ref[...].astype(f32)
    scale = lax.rsqrt(jnp.mean(wide * wide, axis=1, keepdims=True) + norm_eps)
    pulled = gain_ref[...] * grad_normed
    inner = jnp.mean(pulled * wide, axis=1, keepdims=True)
    out_ref[...] = grad_ref[...] + scale * pulled - wide * (scale * scale * scale) * inner


def in_order(first, mine, other):
    return jnp.where(first, jnp.concatenate([mine, other]), jnp.concatenate([other, mine]))


def per_device(
    tokens,
    gain_one,
    w_query,
    w_key,
    w_value,
    w_out,
    bias_table,
    gain_two,
    w_router,
    w_up,
    w_down,
    routes,
    doc_lengths,
    buckets,
    cotangent,
):
    own_rows, width = tokens.shape
    block_rows = routes.shape[0]
    seq = block_rows * GROUP
    cols = w_query.shape[1] // GROUP
    heads = cols // HD
    experts = w_router.shape[1]
    capacity = max(2, (5 * block_rows + 4 * experts - 1) // (4 * experts))
    slots = experts * capacity
    nodes = lax.axis_size("node")
    core = lax.axis_index("core")
    side = lax.axis_index("tensor")
    me = lax.axis_index("node")
    direct = nodes == DIRECT
    parts = nodes if direct else 1
    ids = jnp.stack([core, me, side]).astype(jnp.int32)
    node_rows = width // nodes

    def trade(blocks):
        if direct:
            return [blocks[0]] + [across(blocks[i], "node", i) for i in range(1, nodes)]
        stacked = blocks[0].reshape(nodes, -1, blocks[0].shape[1])
        back = lax.all_to_all(stacked, "node", split_axis=0, concat_axis=0, tiled=True)
        return [back.reshape(blocks[0].shape)]

    def trade_natural(rows):
        stacked = rows.reshape(nodes, -1, rows.shape[-1])
        return lax.all_to_all(stacked, "node", split_axis=0, concat_axis=0, tiled=True)

    share = out((w_query.shape[0], 4 * cols), bf16)
    share_kept, share_sent = call(
        shares_kernel,
        "shares",
        [share, share],
        [ids, *(Far(w) for w in (w_query, w_key, w_value, w_out))],
        smem=1,
        scratch=[pltpu.VMEM((4, *w_query.shape), bf16), pltpu.SemaphoreType.DMA((4,))],
    )
    piece = in_order(core == 0, share_kept, across(share_sent, "core", 1))
    if direct:
        pieces = {0: piece}
        for i in (4, 6, 2):
            pieces[i] = across(piece, "node", i)
        for i in (0, 2, 4, 6):
            pieces[i + 1] = across(pieces[i], "node", 1)
        pieces = [pieces[i] for i in range(nodes)]
    else:
        pieces = [lax.all_gather(piece, "node", axis=0, tiled=True)]

    x_rows = call(
        rows_kernel,
        "rows",
        [out((block_rows, width), bf16)],
        [ids, tokens, across(tokens, "tensor", 1), Raw(pieces[min(1, parts - 1)])],
        smem=1,
    )[0]
    x_other = across(x_rows, "core", 1)
    gain_first = gain_one.astype(f32)[None, :]
    gain_second = gain_two.astype(f32)[None, :]

    back_table, plain_back_table = call(
        functools.partial(tables_kernel, experts, capacity, direct),
        "tables",
        [out((block_rows, slots), bf16)] * 2,
        [ids, routes],
        smem=1,
    )

    lengths_row = lax.dynamic_slice_in_dim(doc_lengths, me, 1, 0)[0]
    ends = jnp.cumsum(lengths_row)
    places = jnp.arange(seq, dtype=jnp.int32)
    docs = jnp.sum((ends[None, :] <= places[:, None]).astype(jnp.int32), axis=1)
    bucket_count = bias_table.shape[0]
    bucket_hot = (
        jnp.pad(buckets, (0, 1))[:, None] == jnp.arange(128, dtype=jnp.int32)[None, :]
    ).astype(f32)
    head_start = (side * GROUP + core) * heads
    bias_here = lax.dynamic_slice_in_dim(bias_table, head_start, heads, 1)
    bias_here = jnp.pad(bias_here, ((0, 128 - bucket_count), (0, 0)))
    bias_vectors = lax.dot_general(
        bias_here, bucket_hot, (((0,), (1,)), ((), ())), precision=exact, preferred_element_type=f32
    )

    weights, wo, x_seq, qkv, mixed, mixed_kept, mixed_sent, *probs = call(
        functools.partial(attend_kernel, heads, parts),
        "attend",
        [
            out((width, 4 * cols), bf16),
            out((width, cols), bf16),
            out((seq, width), bf16),
            out((seq, 3 * cols), bf16),
            out((seq, cols), bf16),
            out((block_rows, cols), bf16),
            out((block_rows, cols), bf16),
            *([out((seq, seq), bf16)] * heads),
        ],
        [
            ids,
            x_rows,
            Near(x_other),
            gain_first,
            bias_vectors,
            docs[:, None],
            docs[None, :],
            *(Near(p) for p in pieces),
        ],
        smem=1,
        scratch=[pltpu.VMEM((seq, width), bf16)],
    )
    kept = [weights, wo, x_seq, qkv, mixed, *probs]
    weights, wo_far, x_seq, qkv, mixed, *probs = call(
        functools.partial(move_kernel, len(kept)),
        "park",
        [Far(out(a.shape, a.dtype)) for a in kept],
        [*(Near(a) for a in kept)],
        scratch=[pltpu.SemaphoreType.DMA((len(kept),))],
    )

    natural = (nodes, slots // nodes, width) if direct else (slots, width)
    cot_slots = call(
        slots_kernel,
        "cot_slots",
        [out((slots, width), bf16)],
        [plain_back_table, cotangent, Raw(pieces[min(3, parts - 1)])],
    )[0]
    cots_own = trade_natural(cot_slots).reshape(natural)
    cots_other = across(cots_own, "core", 1)

    mixed_got = across(mixed_sent, "core", 1)
    attended = call(
        attended_kernel,
        "attended",
        [out((block_rows, width), bf16)],
        [mixed_kept, mixed_got, wo, across(wo, "core", 1), Far(mixed)],
    )[0]
    attended_got = across(attended, "tensor", 1)
    block_shapes = [out((slots // parts, width), bf16)] * parts
    hidden = x_rows.astype(f32) + (attended.astype(f32) + attended_got.astype(f32))
    blocks = call(
        dispatch_kernel,
        "dispatch",
        block_shapes,
        [hidden, gain_second, back_table],
    )
    received = trade(blocks)
    cots, back_active = call(
        functools.partial(cots_kernel, parts),
        "cots",
        [Far(out((2 * slots, width), bf16)), Near(out((2 * slots, w_down.shape[1]), f32))],
        [ids, Near(cots_own), Near(cots_other), w_down, Raw(blocks[0])],
        smem=1,
        scratch=[
            pltpu.VMEM((2 * slots, width), bf16),
            pltpu.SemaphoreType.DMA((2,)),
            *([pltpu.VMEM((slots, width), f32)] if direct else []),
        ],
    )
    slots_own = jnp.concatenate(received)
    slots_other = across(slots_own, "core", 1)
    active, grad_upward, chosen, grad_kept, grad_sent, router_part, slots_all = call(
        expert_kernel,
        "expert",
        [
            Near(out((2 * slots, w_up.shape[1]), bf16)),
            Near(out((2 * slots, w_up.shape[1]), bf16)),
            Near(out((2 * slots, 1), f32)),
            out((slots, width), f32),
            out((slots, width), bf16),
            Near(out(w_router.shape[::-1], f32)),
            Near(out((2 * slots, width), bf16)),
        ],
        [ids, slots_own, Near(slots_other), Near(back_active), w_up, w_router.T],
        smem=1,
    )
    grad_blocks = call(
        join_kernel, "join_grad", block_shapes, [grad_kept, Near(across(grad_sent, "core", 1))]
    )
    grad_back = trade(grad_blocks)
    grad_normed_two = call(
        gather_kernel,
        "gather_grad",
        [out((block_rows, width), bf16)],
        [back_table, *grad_back],
    )[0]
    grad_normed_two_got = across(grad_normed_two, "tensor", 1)

    out_kept, out_sent = call(
        expert_out_kernel,
        "expert_out",
        [out((slots, width), f32), out((slots, width), bf16)],
        [Near(active), Near(chosen), w_down, Raw(grad_blocks[-1])],
    )
    out_slots = call(
        functools.partial(join_natural_kernel, parts),
        "join_out",
        [out(natural, bf16)],
        [ids, out_kept, Near(across(out_sent, "core", 1))],
        smem=1,
    )[0]
    out_back = trade_natural(out_slots.reshape(slots, width)).reshape(slots, width)
    half_block = (own_rows, width)

    kept = [weights, wo_far, x_seq, qkv, mixed, *probs]
    weights, wo, x_seq, qkv, mixed, *probs = call(
        functools.partial(move_kernel, len(kept)),
        "unpark",
        [out(a.shape, a.dtype) for a in kept],
        [*(Far(a) for a in kept), Raw(out_slots)],
        scratch=[pltpu.SemaphoreType.DMA((len(kept),))],
    )
    grad_hidden, grad_attended, gain_two_part = call(
        hidden_back_kernel,
        "hidden_back",
        [Near(out(half_block, f32)), out((block_rows, width), bf16), Near(out((1, width), f32))],
        [
            ids,
            Near(hidden),
            grad_normed_two,
            Near(grad_normed_two_got),
            cotangent,
            gain_second,
            Raw(mixed),
        ],
        smem=1,
        scratch=[pltpu.VMEM((block_rows, width), f32)],
    )
    grad_attended_other = across(grad_attended, "core", 1)
    chunk = 3 * HD + cols
    other_chunk = 3 * (cols - HD)
    small_rows = -(-(2 + experts + heads) // 16) * 16
    if direct:
        first_shapes = [out((width // 2, chunk), t) for t in (f32, bf16)]
        second_shapes = [out((width // 2, other_chunk), t) for t in (f32, bf16)]
    else:
        first_shapes = [out((width, chunk), bf16)]
        second_shapes = [out((width, other_chunk), bf16)]
    grad_mixed, first_dqkv, diagonals, normed_seq, *first_chunk = call(
        functools.partial(first_back_kernel, heads, parts),
        "first_back",
        [
            out((seq, cols), bf16),
            out((seq, 3 * HD), bf16),
            out((8, 2 * seq), f32),
            out((seq, width), bf16),
            *first_shapes,
        ],
        [
            ids,
            grad_attended,
            Near(grad_attended_other),
            gain_first,
            *(wo, qkv, probs[0], x_seq, mixed),
        ],
        smem=1,
        flops=FLOPS1,
        scratch=[
            pltpu.VMEM((seq, width), bf16),
            pltpu.VMEM((seq, seq), bf16),
            pltpu.VMEM((width, chunk), f32),
        ],
    )
    grad_kept, grad_sent, small, *second_chunk = call(
        functools.partial(second_back_kernel, heads, parts),
        "second_back",
        [
            out((block_rows, width), f32),
            out((block_rows, width), bf16),
            out((small_rows, width), f32),
            *second_shapes,
        ],
        [
            ids,
            grad_mixed,
            first_dqkv,
            diagonals,
            bucket_hot,
            normed_seq,
            Near(gain_two_part),
            Near(router_part),
            *(qkv, *probs[1:], x_seq, weights),
        ],
        smem=1,
        flops=FLOPS2,
        scratch=[
            pltpu.VMEM((8, 2 * seq), f32),
            pltpu.VMEM((seq, other_chunk), bf16),
            pltpu.VMEM((seq, 3 * cols), bf16),
            pltpu.VMEM((seq, seq), bf16),
            pltpu.VMEM((width, other_chunk), f32),
        ],
    )

    shard_rows = w_query.shape[0]
    returned, returned_sent = call(
        returned_kernel,
        "returned",
        [out(half_block, bf16), out(half_block, bf16)],
        [ids, plain_back_table, Near(out_back), Raw(grad_kept)],
        smem=1,
    )
    part = out((shard_rows, chunk), f32)
    if direct:
        tall = width // 2 + 2 * small_rows
        second_sent, returned_sent, small, own_one, *send_one = call(
            fold_kernel,
            "fold_first",
            [
                out((tall, chunk), bf16),
                out(returned_sent.shape, bf16),
                out((2 * small_rows, chunk), f32),
                out((node_rows, chunk), f32),
                *([out((node_rows, chunk), bf16)] * 3),
            ],
            [
                first_chunk[0],
                across(first_chunk[1], "node", 1),
                small,
                across(small, "tensor", 1),
                second_chunk[1],
                returned_sent,
            ],
        )
        got_one = [across(b, "node", 2 * i + 2) for i, b in enumerate(send_one)]
        first_done = send_one[0]
    else:
        sums = [jnp.sum(trade_natural(c[0]).astype(f32), axis=0) for c in (first_chunk, second_chunk)]
        kept_one, kept_two = (
            lax.dynamic_slice_in_dim(s, core * shard_rows, shard_rows, 0) for s in sums
        )
        sent_one, sent_two = (
            lax.dynamic_slice_in_dim(s, (1 - core) * shard_rows, shard_rows, 0) for s in sums
        )
        first_done, second_done = kept_one, kept_two
    grad_normed, grad_normed_sent = call(
        normed_sum_kernel,
        "normed_sum",
        [Near(out(half_block, f32)), out(half_block, bf16)],
        [ids, grad_kept, Near(across(grad_sent, "core", 1)), Raw(first_done)],
        smem=1,
        scratch=[pltpu.VMEM((block_rows, width), f32)],
    )
    if direct:
        high = node_rows + 2 * small_rows
        grad_normed_sent, kept_one, sent_one, own_two, *send_two = call(
            fold_second_kernel,
            "fold_second",
            [out(half_block, bf16), part, part, out((high, chunk), f32), *([out((high, chunk), bf16)] * 3)],
            [
                ids,
                second_chunk[0],
                across(second_sent, "node", 1),
                small,
                grad_normed_sent,
                own_one,
                *got_one,
            ],
            smem=1,
        )
        got_two = [across(b, "node", 2 * i + 2) for i, b in enumerate(send_two)]
        second_done = send_two[0]
    grad_w_up_here, grad_w_down_here = call(
        expert_grads_kernel,
        "expert_grads",
        [out(w_up.shape, f32), out(w_down.shape, f32)],
        [
            Near(slots_all),
            cots,
            *(Near(a) for a in (active, grad_upward, chosen)),
            Raw(second_done),
        ],
    )
    input_grad = call(
        input_kernel,
        "input_grad",
        [out(half_block, f32)],
        [
            Near(grad_normed),
            Near(across(grad_normed_sent, "tensor", 1)),
            Near(grad_hidden),
            tokens,
            gain_first,
        ],
    )[0]
    activations = call(
        activations_kernel,
        "activations",
        [out(half_block, bf16)],
        [ids, Near(hidden), Near(returned), Near(across(returned_sent, "tensor", 1))],
        smem=1,
    )[0]
    if direct:
        kept_two, sent_two = call(
            sum_nodes_kernel,
            "sum_nodes",
            [part, out((shard_rows + 2 * small_rows, chunk), f32)],
            [
                ids,
                own_two,
                *got_two,
                *(Far(a) for a in (grad_w_up_here, activations, input_grad)),
            ],
            smem=1,
        )
    got_one = across(sent_one, "core", 1)
    got_two = across(sent_two, "core", 1)
    small_outs = []
    if direct:
        small_outs = [
            out((1, width), f32),
            out((1, width), f32),
            out((experts, width), f32),
            out(bias_table.shape[::-1], f32),
        ]
    weight_grads = call(
        functools.partial(columns_kernel, heads),
        "columns",
        [out(w_query.shape, f32)] * 4 + small_outs,
        [ids, kept_one, got_one, kept_two, got_two] + ([sent_two] if direct else []),
        smem=1,
    )
    if direct:
        sum_one, sum_two, sum_router, sum_bias = weight_grads[4:]
    else:
        small = lax.psum(small, ("node", "core", "tensor"))
        sum_one, sum_two, sum_router = small[:1], small[1:2], small[2 : 2 + experts]
        sum_bias = small[2 + experts : 2 + experts + heads, : 4 * 128].reshape(heads, 4, 128)
        sum_bias = sum_bias[:, :, :bucket_count].transpose(1, 0, 2).reshape(bias_table.shape[::-1])
    return (
        activations,
        input_grad,
        sum_one[0],
        *weight_grads[:4],
        sum_bias.T,
        sum_two[0],
        sum_router.T,
        grad_w_up_here,
        grad_w_down_here,
    )


def solution(mesh):
    dp, tensor = mesh.shape["dp"], mesh.shape["tensor"]
    grid = Mesh(mesh.devices.reshape(dp // GROUP, GROUP, tensor), ("node", "core", "tensor"))
    dp = ("node", "core")
    every = ("node", "core", "tensor")
    in_specs = (
        P(every, None),
        P(),
        P(dp, "tensor"),
        P(dp, "tensor"),
        P(dp, "tensor"),
        P(dp, "tensor"),
        P(),
        P(),
        P(),
        P(None, every),
        P(None, every),
        P(dp, None),
        P(),
        P(),
        P(dp, None),
    )
    out_specs = (
        P(every, None),
        P(every, None),
        P(),
        P(dp, "tensor"),
        P(dp, "tensor"),
        P(dp, "tensor"),
        P(dp, "tensor"),
        P(),
        P(),
        P(),
        P(None, every),
        P(None, every),
    )
    return jax.shard_map(
        per_device, mesh=grid, in_specs=in_specs, out_specs=out_specs, check_vma=False
    )
```

```python
import functools

import jax
import jax.numpy as jnp
from jax import lax
from jax.experimental import pallas as pl
from jax.experimental.pallas import tpu as pltpu
from jax.sharding import Mesh, PartitionSpec as P

HD = 64
GROUP = 2
FLOPS1 = 0
FLOPS2 = 0
DIRECT = 8
FORWARD_TILE = 256
BACK_TILE = 512

norm_eps = 1e-06
masked_value = -1e30
exact = lax.Precision.HIGHEST
bf16 = jnp.bfloat16
f32 = jnp.float32

VMEM = pl.BlockSpec(memory_space=pltpu.VMEM)
SMEM = pl.BlockSpec(memory_space=pltpu.SMEM)
ANY = pl.BlockSpec(memory_space=pl.ANY)


def across(shard, axis, bits):
    return lax.ppermute(shard, axis, [(i, i ^ bits) for i in range(lax.axis_size(axis))])


class Near:
    def __init__(self, array):
        self.array = array


class Raw(Near):
    pass


class Far(Raw):
    pass


def call(body, name, outs, args, smem=0, scratch=(), flops=0):
    arrays = [a.array if isinstance(a, Near) else a for a in args]
    results = [o.array if isinstance(o, Near) else o for o in outs]
    kept = sum(padded_bytes(a) for a in [*arrays, *results, *scratch] if is_plain(a))
    space = {Near: pltpu.VMEM, Far: pltpu.HBM}
    given = [
        pltpu.with_memory_space_constraint(x, space[type(a)]) if type(a) in space else x
        for a, x in zip(args, arrays)
    ]
    return pl.pallas_call(
        body,
        name=name,
        out_shape=[
            space[type(o)](x.shape, x.dtype) if type(o) in space else x
            for o, x in zip(outs, results)
        ],
        in_specs=[SMEM] * smem + [ANY if isinstance(a, Raw) else VMEM for a in args[smem:]],
        out_specs=[ANY if isinstance(o, Raw) else VMEM for o in outs],
        scratch_shapes=scratch,
        compiler_params=pltpu.CompilerParams(vmem_limit_bytes=kept + 10 * 1024 * 1024),
        cost_estimate=pl.CostEstimate(flops=flops, bytes_accessed=0, transcendentals=0),
    )(*given)


def is_plain(array):
    return array.dtype in (bf16, f32, jnp.int32)


def padded_bytes(array):
    *lead, rows, cols = (1, 1, *array.shape)
    size = jnp.dtype(array.dtype).itemsize
    for extent in lead:
        size *= extent
    return size * (-(-rows // 16) * 16) * (-(-cols // 128) * 128)


def out(shape, dtype):
    return jax.ShapeDtypeStruct(shape, dtype)


def mm(a, b):
    return jnp.dot(a, b, preferred_element_type=f32)


def mm_bt(a, b):
    return lax.dot_general(a, b, (((1,), (1,)), ((), ())), preferred_element_type=f32)


def mm_at(a, b):
    return lax.dot_general(a, b, (((0,), (0,)), ((), ())), preferred_element_type=f32)


def shares_kernel(ids, *refs):
    weights, (keep_ref, send_ref, near_ref, sems) = refs[:4], refs[4:]
    copies = [
        pltpu.make_async_copy(w, near_ref.at[i], sems.at[i]) for i, w in enumerate(weights)
    ]
    for copy in copies:
        copy.start()
    for copy in copies:
        copy.wait()
    first = ids[0] == 0
    cols = keep_ref.shape[1] // 4
    for i in range(4):
        low, high = near_ref[i, :, :cols], near_ref[i, :, cols:]
        keep_ref[:, i * cols : (i + 1) * cols] = jnp.where(first, low, high)
        send_ref[:, i * cols : (i + 1) * cols] = jnp.where(first, high, low)


def rows_kernel(ids, own_ref, got_ref, held_ref, out_ref):
    rows = own_ref.shape[0]
    out_ref[pl.ds(pl.multiple_of(ids[2] * rows, rows), rows), :] = own_ref[...]
    out_ref[pl.ds(pl.multiple_of((1 - ids[2]) * rows, rows), rows), :] = got_ref[...]


def move_kernel(count, *refs):
    sources, targets, sems = refs[:count], refs[-count - 1 : -1], refs[-1]
    copies = [
        pltpu.make_async_copy(a, b, sems.at[i]) for i, (a, b) in enumerate(zip(sources, targets))
    ]
    for copy in copies:
        copy.start()
    for copy in copies:
        copy.wait()


def unit_rows(x):
    wide = x.astype(f32)
    return wide * lax.rsqrt(jnp.mean(wide * wide, axis=1, keepdims=True) + norm_eps)


def tables_kernel(experts, capacity, direct, ids, routes_ref, turned_ref, plain_ref):
    rows, slots = plain_ref.shape
    routes = routes_ref[...]
    picks = routes == lax.broadcasted_iota(jnp.int32, (rows, experts), 1)
    upto = lax.broadcasted_iota(jnp.int32, (rows, rows), 0) >= lax.broadcasted_iota(
        jnp.int32, (rows, rows), 1
    )
    counts = mm(upto.astype(f32).astype(bf16), picks.astype(f32).astype(bf16))
    slot = jnp.sum(jnp.where(picks, counts - 1.0, 0.0), axis=1, keepdims=True).astype(jnp.int32)
    codes = lax.broadcasted_iota(jnp.int32, (1, slots), 1)
    expert = jnp.zeros((1, slots), jnp.int32)
    for i in range(1, experts):
        expert = expert + jnp.where(codes >= i * capacity, 1, 0)
    place = codes - expert * capacity
    plain = (routes == expert) & (slot == place)
    plain_ref[...] = plain.astype(f32).astype(bf16)
    turned = (routes == (expert ^ ids[1])) & (slot == place) if direct else plain
    turned_ref[...] = turned.astype(f32).astype(bf16)


def slots_kernel(table_ref, rows_ref, held_ref, out_ref):
    out_ref[...] = mm_at(table_ref[...], rows_ref[...]).astype(bf16)


def cots_kernel(parts, ids, own_ref, other_ref, wdown_ref, held_ref, cots_ref, back_ref, near_ref, sems, *scratch):
    slots = cots_ref.shape[0] // 2
    copies = []
    me = ids[1]
    for at, source in ((0, own_ref), (slots, other_ref)):
        if parts == 1:
            near_ref[at : at + slots, :] = source[...]
        else:
            rows = slots // parts
            for i in range(parts):
                scratch[0][i * rows : (i + 1) * rows, :] = source[me ^ i].astype(f32)
            near_ref[at : at + slots, :] = scratch[0][...].astype(bf16)
        copies.append(
            pltpu.make_async_copy(near_ref.at[at : at + slots], cots_ref.at[at : at + slots], sems.at[len(copies)])
        )
        copies[-1].start()
        back_ref[at : at + slots, :] = mm(near_ref[at : at + slots, :], wdown_ref[...])
    for copy in copies:
        copy.wait()


def attend_kernel(heads, parts, ids, own_ref, other_ref, gain_ref, vec_ref, row_docs, col_docs, *refs):
    pieces = refs[:parts]
    w_ref, wo_ref, x_ref, qkv_ref, mixed_ref, keep_ref, send_ref, *probs_refs = refs[parts:-1]
    seq_ref = refs[-1]
    core = ids[0]
    me = ids[1]
    seq = x_ref.shape[0]
    width = heads * HD
    half = seq // GROUP
    span = seq + FORWARD_TILE
    rows = pieces[0].shape[0]
    for i, piece in enumerate(pieces):
        start = 0 if parts == 1 else pl.multiple_of((me ^ i) * rows, rows)
        w_ref[pl.ds(start, rows), :] = piece[...]
    for place, source in ((core, own_ref), (1 - core, other_ref)):
        at = pl.ds(pl.multiple_of(place * half, half), half)
        x = source[...]
        x_ref[at, :] = x
        seq_ref[at, :] = (unit_rows(x) * gain_ref[...]).astype(bf16)
    wo_ref[...] = w_ref[:, 3 * width :]
    for i in range(0, seq, 256):
        qkv_ref[i : i + 256, :] = mm(seq_ref[i : i + 256, :], w_ref[:, : 3 * width]).astype(bf16)
    for h in range(heads):
        at = h * HD
        key = qkv_ref[:, width + at : width + at + HD]
        value = qkv_ref[:, 2 * width + at : 2 * width + at + HD]
        for i in range(0, seq, FORWARD_TILE):
            base = seq - FORWARD_TILE - i
            seg = jnp.broadcast_to(vec_ref[h : h + 1, base : base + span], (FORWARD_TILE, span))
            bias = pltpu.roll(seg, span - FORWARD_TILE + 1, 1, stride=1, stride_axis=0)[:, :seq]
            scores = mm_bt(qkv_ref[i : i + FORWARD_TILE, at : at + HD], key) * HD**-0.5 + bias
            scores = jnp.where(row_docs[i : i + FORWARD_TILE, :] == col_docs[...], scores, masked_value)
            peak = jnp.max(scores, axis=1, keepdims=True)
            exp_scores = jnp.exp(scores - peak)
            probs = exp_scores / jnp.sum(exp_scores, axis=1, keepdims=True)
            probs_refs[h][i : i + FORWARD_TILE, :] = probs.astype(bf16)
            mixed_ref[i : i + FORWARD_TILE, at : at + HD] = mm(probs.astype(bf16), value).astype(bf16)
    keep_ref[...] = mixed_ref[pl.ds(pl.multiple_of(core * half, half), half), :]
    send_ref[...] = mixed_ref[pl.ds(pl.multiple_of((1 - core) * half, half), half), :]


def attended_kernel(keep_ref, got_ref, wo_ref, wo_other_ref, held_ref, out_ref):
    total = mm_bt(keep_ref[...], wo_ref[...]) + mm_bt(got_ref[...], wo_other_ref[...])
    out_ref[...] = total.astype(bf16)


def dispatch_kernel(hidden_ref, gain_ref, table_ref, *blocks):
    hidden = hidden_ref[...]
    scale = lax.rsqrt(jnp.mean(hidden * hidden, axis=1, keepdims=True) + norm_eps)
    normed = (hidden * scale * gain_ref[...]).astype(bf16)
    slots = mm_at(table_ref[...], normed)
    rows = blocks[0].shape[0]
    for i, block in enumerate(blocks):
        block[...] = slots[i * rows : (i + 1) * rows, :].astype(bf16)


def expert_kernel(ids, own_ref, other_ref, h_ref, wup_ref, wr_ref, *refs):
    active_ref, gup_ref, chosen_ref, keep_ref, send_ref, router_ref, all_ref = refs
    rows = own_ref.shape[0]
    step = rows
    router = jnp.zeros(router_ref.shape, f32)
    root = 0.7978845608028654
    for i in range(0, 2 * rows, step):
        src = own_ref if i < rows else other_ref
        at = i % rows
        slots = src[at : at + step, :]
        all_ref[i : i + step, :] = slots
        logits = mm_bt(slots, wr_ref[...])
        peak = jnp.max(logits, axis=1, keepdims=True)
        exp_logits = jnp.exp(logits - peak)
        gates = exp_logits / jnp.sum(exp_logits, axis=1, keepdims=True)
        mine = lax.broadcasted_iota(jnp.int32, gates.shape, 1) == ids[1]
        chosen = jnp.sum(jnp.where(mine, gates, 0.0), axis=1, keepdims=True)
        chosen_ref[i : i + step, :] = chosen
        up = mm(slots, wup_ref[...])
        square = up * up
        bent = jnp.tanh(root * (up + 0.044715 * up * square))
        low = (0.5 * up * (1.0 + bent)).astype(bf16)
        active_ref[i : i + step, :] = low
        slope = 0.5 * (1.0 + bent) + 0.5 * up * (1.0 - bent * bent) * root * (
            1.0 + 3.0 * 0.044715 * square
        )
        back = h_ref[i : i + step, :]
        gup = (chosen * back * slope).astype(bf16)
        gup_ref[i : i + step, :] = gup
        grad_chosen = jnp.sum(low.astype(f32) * back, axis=1, keepdims=True)
        grad_logits = gates * (jnp.where(mine, 1.0, 0.0) - chosen) * grad_chosen
        grad_logits = grad_logits.astype(bf16)
        router = router + mm_at(grad_logits, slots)
        grad = mm_bt(gup, wup_ref[...]) + mm(grad_logits, wr_ref[...])
        if i < rows:
            keep_ref[at : at + step, :] = grad
        else:
            send_ref[at : at + step, :] = grad.astype(bf16)
    router_ref[...] = router


def expert_out_kernel(active_ref, chosen_ref, wdown_ref, held_ref, keep_ref, send_ref):
    rows = keep_ref.shape[0]
    result = mm_bt(active_ref[...], wdown_ref[...]) * chosen_ref[...]
    keep_ref[...] = result[:rows, :]
    send_ref[...] = result[rows:, :].astype(bf16)


def expert_grads_kernel(slots_ref, cots_ref, active_ref, gup_ref, chosen_ref, held_ref, gwup_ref, gwdown_ref):
    gwup_ref[...] = mm_at(slots_ref[...], gup_ref[...])
    grads = (chosen_ref[...] * cots_ref[...].astype(f32)).astype(bf16)
    gwdown_ref[...] = mm_at(grads, active_ref[...])


def join_kernel(keep_ref, got_ref, *blocks):
    total = keep_ref[...] + got_ref[...].astype(f32)
    rows = blocks[0].shape[0]
    for i, block in enumerate(blocks):
        block[...] = total[i * rows : (i + 1) * rows, :].astype(bf16)


def join_natural_kernel(parts, ids, keep_ref, got_ref, out_ref):
    total = keep_ref[...] + got_ref[...].astype(f32)
    if parts == 1:
        out_ref[...] = total.astype(bf16)
        return
    rows = out_ref.shape[1]
    for i in range(parts):
        out_ref[ids[1] ^ i] = total[i * rows : (i + 1) * rows, :].astype(bf16)


def gather_kernel(back_table_ref, *refs):
    blocks = refs[:-1]
    slots = jnp.concatenate([b[...].astype(f32) for b in blocks], axis=0).astype(bf16)
    refs[-1][...] = mm(back_table_ref[...], slots).astype(bf16)


def hidden_back_kernel(ids, hidden_ref, own_ref, got_ref, cot_ref, gain_ref, held_ref, grad_ref, low_ref, dgain_ref, all_ref):
    hidden = hidden_ref[...]
    grad_normed = own_ref[...].astype(f32) + got_ref[...].astype(f32)
    scale = lax.rsqrt(jnp.mean(hidden * hidden, axis=1, keepdims=True) + norm_eps)
    dgain_ref[...] = jnp.sum(grad_normed * hidden * scale, axis=0, keepdims=True)
    pulled = gain_ref[...] * grad_normed
    inner = jnp.mean(pulled * hidden, axis=1, keepdims=True)
    grad = cot_ref[...].astype(f32) + scale * pulled - hidden * (scale * scale * scale) * inner
    low_ref[...] = grad.astype(bf16)
    all_ref[...] = grad
    rows = grad_ref.shape[0]
    grad_ref[...] = all_ref[pl.ds(pl.multiple_of(ids[2] * rows, rows), rows), :]


def returned_kernel(ids, table_ref, slots_ref, held_ref, keep_ref, send_ref):
    rows = keep_ref.shape[0]
    mine = table_ref[pl.ds(pl.multiple_of(ids[2] * rows, rows), rows), :]
    keep_ref[...] = mm(mine, slots_ref[...]).astype(bf16)
    theirs = table_ref[pl.ds(pl.multiple_of((1 - ids[2]) * rows, rows), rows), :]
    send_ref[...] = mm(theirs, slots_ref[...]).astype(bf16)


def activations_kernel(ids, hidden_ref, own_ref, got_ref, out_ref):
    rows = out_ref.shape[0]
    hidden = hidden_ref[pl.ds(pl.multiple_of(ids[2] * rows, rows), rows), :]
    out_ref[...] = (hidden + (own_ref[...].astype(f32) + got_ref[...].astype(f32))).astype(bf16)


def normed_sum_kernel(ids, keep_ref, got_ref, held_ref, own_ref, send_ref, all_ref):
    all_ref[...] = keep_ref[...] + got_ref[...].astype(f32)
    rows = own_ref.shape[0]
    own_ref[...] = all_ref[pl.ds(pl.multiple_of(ids[2] * rows, rows), rows), :]
    theirs = pl.ds(pl.multiple_of((1 - ids[2]) * rows, rows), rows)
    send_ref[...] = all_ref[theirs, :].astype(bf16)


def heads_back(heads, first, qkv_ref, gm_ref, probs, dqkv_ref, diag_ref, ds_ref):
    seq = qkv_ref.shape[0]
    width = heads * HD
    here = len(probs) * HD
    span = seq + BACK_TILE
    flip = (
        lax.broadcasted_iota(jnp.int32, (BACK_TILE, BACK_TILE), 0)
        + lax.broadcasted_iota(jnp.int32, (BACK_TILE, BACK_TILE), 1)
        == BACK_TILE - 1
    ).astype(bf16)
    for h, probs_ref in enumerate(probs):
        at = (first + h) * HD
        to = h * HD
        key = qkv_ref[:, width + at : width + at + HD]
        value = qkv_ref[:, 2 * width + at : 2 * width + at + HD]
        for i in range(0, seq, BACK_TILE):
            probs_rows = probs_ref[i : i + BACK_TILE, :].astype(f32)
            grad_probs = mm_bt(gm_ref[i : i + BACK_TILE, at : at + HD], value)
            inner = jnp.sum(probs_rows * grad_probs, axis=1, keepdims=True)
            grad_scores = (probs_rows * (grad_probs - inner)).astype(bf16)
            ds_ref[i : i + BACK_TILE, :] = grad_scores
            dqkv_ref[i : i + BACK_TILE, to : to + HD] = (mm(grad_scores, key) * HD**-0.5).astype(bf16)
            flipped = mm(flip, grad_scores)
            padded = jnp.concatenate([flipped, jnp.zeros((BACK_TILE, BACK_TILE), f32)], axis=1)
            skewed = pltpu.roll(padded, 0, 1, stride=1, stride_axis=0)
            base = seq - BACK_TILE - i
            row = first + h
            diag_ref[row : row + 1, base : base + span] += jnp.sum(skewed, axis=0, keepdims=True)
        dqkv_ref[:, here + to : here + to + HD] = (
            mm_at(ds_ref[...], qkv_ref[:, at : at + HD]) * HD**-0.5
        ).astype(bf16)
        dqkv_ref[:, 2 * here + to : 2 * here + to + HD] = mm_at(
            probs_ref[...], gm_ref[:, at : at + HD]
        ).astype(bf16)


def send_rows(parts, me, gw_ref, outs):
    if parts == 1:
        outs[0][...] = gw_ref[...].astype(bf16)
        return
    rows = gw_ref.shape[0] // parts
    for i in range(parts // 2):
        at = slice(i * rows, (i + 1) * rows)
        outs[0][at, :] = gw_ref[pl.ds(pl.multiple_of((me ^ 2 * i) * rows, rows), rows), :]
        there = pl.ds(pl.multiple_of((me ^ 2 * i ^ 1) * rows, rows), rows)
        outs[1][at, :] = gw_ref[there, :].astype(bf16)


def first_back_kernel(heads, parts, ids, own_ref, other_ref, gain_ref, *refs):
    wo_ref, qkv_ref, probs_ref, x_ref, mixed_ref = refs[:5]
    gm_ref, dqkv_ref, diag_ref, seq_ref, *outs = refs[5:-3]
    ga_ref, ds_ref, gw_ref = refs[-3:]
    core = ids[0]
    half = own_ref.shape[0]
    ga_ref[pl.ds(pl.multiple_of(core * half, half), half), :] = own_ref[...]
    ga_ref[pl.ds(pl.multiple_of((1 - core) * half, half), half), :] = other_ref[...]
    gm_ref[...] = mm(ga_ref[...], wo_ref[...]).astype(bf16)
    diag_ref[...] = jnp.zeros_like(diag_ref)
    heads_back(heads, 0, qkv_ref, gm_ref, [probs_ref], dqkv_ref, diag_ref, ds_ref)
    cut = dqkv_ref.shape[1]
    seq_ref[...] = (unit_rows(x_ref[...]) * gain_ref[...]).astype(bf16)
    gw_ref[:, :cut] = mm_at(seq_ref[...], dqkv_ref[...])
    gw_ref[:, cut:] = mm_at(ga_ref[...], mixed_ref[...])
    send_rows(parts, ids[1], gw_ref, outs)


def second_back_kernel(
    heads, parts, ids, gm_ref, first_ref, diag_in_ref, hot_ref, seq_ref, gain_ref, router_ref, *refs
):
    count = heads + 2
    qkv_ref, *probs, x_ref, w_ref = refs[:count]
    refs = refs[count:]
    keep_ref, send_ref, small_ref, *outs = refs[:-5]
    diag_ref, dqkv_ref, all_ref, ds_ref, gw_ref = refs[-5:]
    core, me, side = ids[0], ids[1], ids[2]
    half = keep_ref.shape[0]
    diag_ref[...] = diag_in_ref[...]
    heads_back(heads, 1, qkv_ref, gm_ref, probs, dqkv_ref, diag_ref, ds_ref)
    gw_ref[...] = mm_at(seq_ref[...], dqkv_ref[...])
    send_rows(parts, me, gw_ref, outs)
    rest = (heads - 1) * HD
    for i in range(3):
        at = i * heads * HD
        all_ref[:, at : at + HD] = first_ref[:, i * HD : (i + 1) * HD]
        all_ref[:, at + HD : at + heads * HD] = dqkv_ref[:, i * rest : (i + 1) * rest]
    gain = jnp.zeros((1, x_ref.shape[1]), f32)
    for place, mine in ((core, True), (1 - core, False)):
        rows = pl.ds(pl.multiple_of(place * half, half), half)
        grad = mm_bt(all_ref[rows, :], w_ref[:, : all_ref.shape[1]])
        gain = gain + jnp.sum(grad * unit_rows(x_ref[rows, :]), axis=0, keepdims=True)
        if mine:
            keep_ref[...] = grad
        else:
            send_ref[...] = grad.astype(bf16)
    small_ref[...] = jnp.zeros_like(small_ref)
    small_ref[0:1, :] = gain
    small_ref[1:2, :] = jnp.where(side == 0, gain_ref[...], 0.0)
    experts = router_ref.shape[0]
    small_ref[2 : 2 + experts, :] = router_ref[...]
    bias = jnp.dot(diag_ref[...], hot_ref[...], precision=exact, preferred_element_type=f32)
    lanes = bias.shape[1]
    for i in range(2 * GROUP):
        small_ref[2 + experts : 2 + experts + heads, i * lanes : (i + 1) * lanes] = jnp.where(
            side * GROUP + core == i, bias[:heads, :], 0.0
        )


def fold_kernel(
    keep_ref, got_ref, small_ref, small_got_ref, second_ref, returned_ref,
    second_out, returned_out, small_out, own_ref, *sends
):
    returned_out[...] = returned_ref[...]
    end, cols = second_ref.shape
    high = small_ref.shape[0]
    second_out[:end, :] = second_ref[...]
    for i in range(2):
        at = slice(i * cols, (i + 1) * cols)
        low = (small_ref[:, at] + small_got_ref[:, at]).astype(bf16)
        second_out[end + i * high : end + (i + 1) * high, :] = low
        small_out[i * high : (i + 1) * high, :] = low.astype(f32)
    total = keep_ref[...] + got_ref[...].astype(f32)
    rows = own_ref.shape[0]
    own_ref[...] = total[:rows, :]
    for i, send in enumerate(sends):
        send[...] = total[(i + 1) * rows : (i + 2) * rows, :].astype(bf16)


def quarters(refs, at):
    a, b, c, d = (r[at, :].astype(f32) for r in refs)
    return (a + b) + (c + d)


def split_cores(core, refs, keep_ref, send_ref):
    rows = keep_ref.shape[0]
    keep_ref[...] = quarters(refs, pl.ds(pl.multiple_of(core * rows, rows), rows))
    send_ref[:rows, :] = quarters(refs, pl.ds(pl.multiple_of((1 - core) * rows, rows), rows))


def fold_second_kernel(ids, keep_ref, got_ref, small_ref, grad_ref, *refs):
    first = refs[:4]
    grad_out, keep_one_ref, send_one_ref, own_ref, *sends = refs[4:]
    grad_out[...] = grad_ref[...]
    end = keep_ref.shape[0]
    total = keep_ref[...] + got_ref[:end, :].astype(f32)
    small = (small_ref[...] + got_ref[end:, :].astype(f32)).astype(bf16)
    rows = keep_one_ref.shape[0] * 2
    for i, block in enumerate((own_ref, *sends)):
        block[:rows, :] = total[i * rows : (i + 1) * rows, :].astype(block.dtype)
        block[rows:, :] = small.astype(block.dtype)
    split_cores(ids[0], first, keep_one_ref, send_one_ref)


def sum_nodes_kernel(ids, *refs):
    second = refs[:4]
    keep_ref, send_ref = refs[-2:]
    split_cores(ids[0], second, keep_ref, send_ref)
    rows = keep_ref.shape[0]
    send_ref[rows:, :] = quarters(second, slice(2 * rows, second[0].shape[0]))


def columns_kernel(heads, ids, keep_one, got_one, keep_two, got_two, *refs):
    outs = refs[:4] if len(refs) == 4 else refs[1:5]
    core = ids[0]
    rows = keep_one.shape[0]
    cols = heads * HD
    rest = cols - HD
    for c in range(2):
        at = c * cols
        mine = core == c
        one = jnp.where(mine, keep_one[...], got_one[...])
        two = jnp.where(mine, keep_two[...], got_two[:rows, :])
        for i in range(3):
            outs[i][:, at : at + HD] = one[:, i * HD : (i + 1) * HD]
            outs[i][:, at + HD : at + cols] = two[:, i * rest : (i + 1) * rest]
        outs[3][:, at : at + cols] = one[:, 3 * HD : 3 * HD + cols]
    if len(refs) == 4:
        return
    gain_one_ref, gain_two_ref, router_ref, bias_ref = refs[5:]
    small = refs[0][rows:, :] + got_two[rows:, :]
    high = small.shape[0] // 2
    wide = jnp.concatenate([small[:high, :], small[high:, :]], axis=1)
    experts = router_ref.shape[0]
    gain_one_ref[...] = wide[0:1, :]
    gain_two_ref[...] = wide[1:2, :]
    router_ref[...] = wide[2 : 2 + experts, :]
    for i in range(2 * GROUP):
        for h in range(heads):
            row = 2 + experts + h
            bias_ref[i * heads + h : i * heads + h + 1, :] = wide[
                row : row + 1, i * 128 : i * 128 + bias_ref.shape[1]
            ]


def input_kernel(keep_ref, got_ref, grad_ref, x_ref, gain_ref, out_ref):
    grad_normed = keep_ref[...] + got_ref[...].astype(f32)
    wide = x_ref[...].astype(f32)
    scale = lax.rsqrt(jnp.mean(wide * wide, axis=1, keepdims=True) + norm_eps)
    pulled = gain_ref[...] * grad_normed
    inner = jnp.mean(pulled * wide, axis=1, keepdims=True)
    out_ref[...] = grad_ref[...] + scale * pulled - wide * (scale * scale * scale) * inner


def in_order(first, mine, other):
    return jnp.where(first, jnp.concatenate([mine, other]), jnp.concatenate([other, mine]))


def per_device(
    tokens,
    gain_one,
    w_query,
    w_key,
    w_value,
    w_out,
    bias_table,
    gain_two,
    w_router,
    w_up,
    w_down,
    routes,
    doc_lengths,
    buckets,
    cotangent,
):
    own_rows, width = tokens.shape
    block_rows = routes.shape[0]
    seq = block_rows * GROUP
    cols = w_query.shape[1] // GROUP
    heads = cols // HD
    experts = w_router.shape[1]
    capacity = max(2, (5 * block_rows + 4 * experts - 1) // (4 * experts))
    slots = experts * capacity
    nodes = lax.axis_size("node")
    core = lax.axis_index("core")
    side = lax.axis_index("tensor")
    me = lax.axis_index("node")
    direct = nodes == DIRECT
    parts = nodes if direct else 1
    ids = jnp.stack([core, me, side]).astype(jnp.int32)
    node_rows = width // nodes

    def trade(blocks):
        if direct:
            return [blocks[0]] + [across(blocks[i], "node", i) for i in range(1, nodes)]
        stacked = blocks[0].reshape(nodes, -1, blocks[0].shape[1])
        back = lax.all_to_all(stacked, "node", split_axis=0, concat_axis=0, tiled=True)
        return [back.reshape(blocks[0].shape)]

    def trade_natural(rows):
        stacked = rows.reshape(nodes, -1, rows.shape[-1])
        return lax.all_to_all(stacked, "node", split_axis=0, concat_axis=0, tiled=True)

    share = out((w_query.shape[0], 4 * cols), bf16)
    share_kept, share_sent = call(
        shares_kernel,
        "shares",
        [share, share],
        [ids, *(Far(w) for w in (w_query, w_key, w_value, w_out))],
        smem=1,
        scratch=[pltpu.VMEM((4, *w_query.shape), bf16), pltpu.SemaphoreType.DMA((4,))],
    )
    piece = in_order(core == 0, share_kept, across(share_sent, "core", 1))
    if direct:
        pieces = {0: piece}
        for i in (4, 6, 2):
            pieces[i] = across(piece, "node", i)
        for i in (0, 2, 4, 6):
            pieces[i + 1] = across(pieces[i], "node", 1)
        pieces = [pieces[i] for i in range(nodes)]
    else:
        pieces = [lax.all_gather(piece, "node", axis=0, tiled=True)]

    x_rows = call(
        rows_kernel,
        "rows",
        [out((block_rows, width), bf16)],
        [ids, tokens, across(tokens, "tensor", 1), Raw(pieces[min(1, parts - 1)])],
        smem=1,
    )[0]
    x_other = across(x_rows, "core", 1)
    gain_first = gain_one.astype(f32)[None, :]
    gain_second = gain_two.astype(f32)[None, :]

    back_table, plain_back_table = call(
        functools.partial(tables_kernel, experts, capacity, direct),
        "tables",
        [out((block_rows, slots), bf16)] * 2,
        [ids, routes],
        smem=1,
    )

    lengths_row = lax.dynamic_slice_in_dim(doc_lengths, me, 1, 0)[0]
    ends = jnp.cumsum(lengths_row)
    places = jnp.arange(seq, dtype=jnp.int32)
    docs = jnp.sum((ends[None, :] <= places[:, None]).astype(jnp.int32), axis=1)
    bucket_count = bias_table.shape[0]
    bucket_hot = (
        jnp.pad(buckets, (0, 1))[:, None] == jnp.arange(128, dtype=jnp.int32)[None, :]
    ).astype(f32)
    head_start = (side * GROUP + core) * heads
    bias_here = lax.dynamic_slice_in_dim(bias_table, head_start, heads, 1)
    bias_here = jnp.pad(bias_here, ((0, 128 - bucket_count), (0, 0)))
    bias_vectors = lax.dot_general(
        bias_here, bucket_hot, (((0,), (1,)), ((), ())), precision=exact, preferred_element_type=f32
    )

    weights, wo, x_seq, qkv, mixed, mixed_kept, mixed_sent, *probs = call(
        functools.partial(attend_kernel, heads, parts),
        "attend",
        [
            out((width, 4 * cols), bf16),
            out((width, cols), bf16),
            out((seq, width), bf16),
            out((seq, 3 * cols), bf16),
            out((seq, cols), bf16),
            out((block_rows, cols), bf16),
            out((block_rows, cols), bf16),
            *([out((seq, seq), bf16)] * heads),
        ],
        [
            ids,
            x_rows,
            Near(x_other),
            gain_first,
            bias_vectors,
            docs[:, None],
            docs[None, :],
            *(Near(p) for p in pieces),
        ],
        smem=1,
        scratch=[pltpu.VMEM((seq, width), bf16)],
    )
    kept = [weights, wo, x_seq, qkv, mixed, *probs]
    weights, wo_far, x_seq, qkv, mixed, *probs = call(
        functools.partial(move_kernel, len(kept)),
        "park",
        [Far(out(a.shape, a.dtype)) for a in kept],
        [*(Near(a) for a in kept)],
        scratch=[pltpu.SemaphoreType.DMA((len(kept),))],
    )

    natural = (nodes, slots // nodes, width) if direct else (slots, width)
    cot_slots = call(
        slots_kernel,
        "cot_slots",
        [out((slots, width), bf16)],
        [plain_back_table, cotangent, Raw(pieces[min(3, parts - 1)])],
    )[0]
    cots_own = trade_natural(cot_slots).reshape(natural)
    cots_other = across(cots_own, "core", 1)

    mixed_got = across(mixed_sent, "core", 1)
    attended = call(
        attended_kernel,
        "attended",
        [out((block_rows, width), bf16)],
        [mixed_kept, mixed_got, wo, across(wo, "core", 1), Far(mixed)],
    )[0]
    attended_got = across(attended, "tensor", 1)
    block_shapes = [out((slots // parts, width), bf16)] * parts
    hidden = x_rows.astype(f32) + (attended.astype(f32) + attended_got.astype(f32))
    blocks = call(
        dispatch_kernel,
        "dispatch",
        block_shapes,
        [hidden, gain_second, back_table],
    )
    received = trade(blocks)
    cots, back_active = call(
        functools.partial(cots_kernel, parts),
        "cots",
        [Far(out((2 * slots, width), bf16)), Near(out((2 * slots, w_down.shape[1]), f32))],
        [ids, Near(cots_own), Near(cots_other), w_down, Raw(blocks[0])],
        smem=1,
        scratch=[
            pltpu.VMEM((2 * slots, width), bf16),
            pltpu.SemaphoreType.DMA((2,)),
            *([pltpu.VMEM((slots, width), f32)] if direct else []),
        ],
    )
    slots_own = jnp.concatenate(received)
    slots_other = across(slots_own, "core", 1)
    active, grad_upward, chosen, grad_kept, grad_sent, router_part, slots_all = call(
        expert_kernel,
        "expert",
        [
            Near(out((2 * slots, w_up.shape[1]), bf16)),
            Near(out((2 * slots, w_up.shape[1]), bf16)),
            Near(out((2 * slots, 1), f32)),
            out((slots, width), f32),
            out((slots, width), bf16),
            Near(out(w_router.shape[::-1], f32)),
            Near(out((2 * slots, width), bf16)),
        ],
        [ids, slots_own, Near(slots_other), Near(back_active), w_up, w_router.T],
        smem=1,
    )
    grad_blocks = call(
        join_kernel, "join_grad", block_shapes, [grad_kept, Near(across(grad_sent, "core", 1))]
    )
    grad_back = trade(grad_blocks)
    grad_normed_two = call(
        gather_kernel,
        "gather_grad",
        [out((block_rows, width), bf16)],
        [back_table, *grad_back],
    )[0]
    grad_normed_two_got = across(grad_normed_two, "tensor", 1)

    out_kept, out_sent = call(
        expert_out_kernel,
        "expert_out",
        [out((slots, width), f32), out((slots, width), bf16)],
        [Near(active), Near(chosen), w_down, Raw(grad_blocks[-1])],
    )
    out_slots = call(
        functools.partial(join_natural_kernel, parts),
        "join_out",
        [out(natural, bf16)],
        [ids, out_kept, Near(across(out_sent, "core", 1))],
        smem=1,
    )[0]
    out_back = trade_natural(out_slots.reshape(slots, width)).reshape(slots, width)
    half_block = (own_rows, width)

    kept = [weights, wo_far, x_seq, qkv, mixed, *probs]
    weights, wo, x_seq, qkv, mixed, *probs = call(
        functools.partial(move_kernel, len(kept)),
        "unpark",
        [out(a.shape, a.dtype) for a in kept],
        [*(Far(a) for a in kept), Raw(out_slots)],
        scratch=[pltpu.SemaphoreType.DMA((len(kept),))],
    )
    grad_hidden, grad_attended, gain_two_part = call(
        hidden_back_kernel,
        "hidden_back",
        [Near(out(half_block, f32)), out((block_rows, width), bf16), Near(out((1, width), f32))],
        [
            ids,
            Near(hidden),
            grad_normed_two,
            Near(grad_normed_two_got),
            cotangent,
            gain_second,
            Raw(mixed),
        ],
        smem=1,
        scratch=[pltpu.VMEM((block_rows, width), f32)],
    )
    grad_attended_other = across(grad_attended, "core", 1)
    chunk = 3 * HD + cols
    other_chunk = 3 * (cols - HD)
    small_rows = -(-(2 + experts + heads) // 16) * 16
    if direct:
        first_shapes = [out((width // 2, chunk), t) for t in (f32, bf16)]
        second_shapes = [out((width // 2, other_chunk), t) for t in (f32, bf16)]
    else:
        first_shapes = [out((width, chunk), bf16)]
        second_shapes = [out((width, other_chunk), bf16)]
    grad_mixed, first_dqkv, diagonals, normed_seq, *first_chunk = call(
        functools.partial(first_back_kernel, heads, parts),
        "first_back",
        [
            out((seq, cols), bf16),
            out((seq, 3 * HD), bf16),
            out((8, 2 * seq), f32),
            out((seq, width), bf16),
            *first_shapes,
        ],
        [
            ids,
            grad_attended,
            Near(grad_attended_other),
            gain_first,
            *(wo, qkv, probs[0], x_seq, mixed),
        ],
        smem=1,
        flops=FLOPS1,
        scratch=[
            pltpu.VMEM((seq, width), bf16),
            pltpu.VMEM((seq, seq), bf16),
            pltpu.VMEM((width, chunk), f32),
        ],
    )
    grad_kept, grad_sent, small, *second_chunk = call(
        functools.partial(second_back_kernel, heads, parts),
        "second_back",
        [
            out((block_rows, width), f32),
            out((block_rows, width), bf16),
            out((small_rows, width), f32),
            *second_shapes,
        ],
        [
            ids,
            grad_mixed,
            first_dqkv,
            diagonals,
            bucket_hot,
            normed_seq,
            Near(gain_two_part),
            Near(router_part),
            *(qkv, *probs[1:], x_seq, weights),
        ],
        smem=1,
        flops=FLOPS2,
        scratch=[
            pltpu.VMEM((8, 2 * seq), f32),
            pltpu.VMEM((seq, other_chunk), bf16),
            pltpu.VMEM((seq, 3 * cols), bf16),
            pltpu.VMEM((seq, seq), bf16),
            pltpu.VMEM((width, other_chunk), f32),
        ],
    )

    shard_rows = w_query.shape[0]
    returned, returned_sent = call(
        returned_kernel,
        "returned",
        [out(half_block, bf16), out(half_block, bf16)],
        [ids, plain_back_table, Near(out_back), Raw(grad_kept)],
        smem=1,
    )
    part = out((shard_rows, chunk), f32)
    if direct:
        tall = width // 2 + 2 * small_rows
        second_sent, returned_sent, small, own_one, *send_one = call(
            fold_kernel,
            "fold_first",
            [
                out((tall, chunk), bf16),
                out(returned_sent.shape, bf16),
                out((2 * small_rows, chunk), f32),
                out((node_rows, chunk), f32),
                *([out((node_rows, chunk), bf16)] * 3),
            ],
            [
                first_chunk[0],
                across(first_chunk[1], "node", 1),
                small,
                across(small, "tensor", 1),
                second_chunk[1],
                returned_sent,
            ],
        )
        got_one = [across(b, "node", 2 * i + 2) for i, b in enumerate(send_one)]
        first_done = send_one[0]
    else:
        sums = [jnp.sum(trade_natural(c[0]).astype(f32), axis=0) for c in (first_chunk, second_chunk)]
        kept_one, kept_two = (
            lax.dynamic_slice_in_dim(s, core * shard_rows, shard_rows, 0) for s in sums
        )
        sent_one, sent_two = (
            lax.dynamic_slice_in_dim(s, (1 - core) * shard_rows, shard_rows, 0) for s in sums
        )
        first_done, second_done = kept_one, kept_two
    grad_normed, grad_normed_sent = call(
        normed_sum_kernel,
        "normed_sum",
        [Near(out(half_block, f32)), out(half_block, bf16)],
        [ids, grad_kept, Near(across(grad_sent, "core", 1)), Raw(first_done)],
        smem=1,
        scratch=[pltpu.VMEM((block_rows, width), f32)],
    )
    if direct:
        high = node_rows + 2 * small_rows
        grad_normed_sent, kept_one, sent_one, own_two, *send_two = call(
            fold_second_kernel,
            "fold_second",
            [out(half_block, bf16), part, part, out((high, chunk), f32), *([out((high, chunk), bf16)] * 3)],
            [
                ids,
                second_chunk[0],
                across(second_sent, "node", 1),
                small,
                grad_normed_sent,
                own_one,
                *got_one,
            ],
            smem=1,
        )
        got_two = [across(b, "node", 2 * i + 2) for i, b in enumerate(send_two)]
        second_done = send_two[0]
    grad_w_up_here, grad_w_down_here = call(
        expert_grads_kernel,
        "expert_grads",
        [out(w_up.shape, f32), out(w_down.shape, f32)],
        [
            Near(slots_all),
            cots,
            *(Near(a) for a in (active, grad_upward, chosen)),
            Raw(second_done),
        ],
    )
    input_grad = call(
        input_kernel,
        "input_grad",
        [out(half_block, f32)],
        [
            Near(grad_normed),
            Near(across(grad_normed_sent, "tensor", 1)),
            Near(grad_hidden),
            tokens,
            gain_first,
        ],
    )[0]
    activations = call(
        activations_kernel,
        "activations",
        [out(half_block, bf16)],
        [ids, Near(hidden), Near(returned), Near(across(returned_sent, "tensor", 1))],
        smem=1,
    )[0]
    if direct:
        kept_two, sent_two = call(
            sum_nodes_kernel,
            "sum_nodes",
            [part, out((shard_rows + 2 * small_rows, chunk), f32)],
            [
                ids,
                own_two,
                *got_two,
                *(Far(a) for a in (grad_w_up_here, activations, input_grad)),
            ],
            smem=1,
        )
    got_one = across(sent_one, "core", 1)
    got_two = across(sent_two, "core", 1)
    small_outs = []
    if direct:
        small_outs = [
            out((1, width), f32),
            out((1, width), f32),
            out((experts, width), f32),
            out(bias_table.shape[::-1], f32),
        ]
    weight_grads = call(
        functools.partial(columns_kernel, heads),
        "columns",
        [out(w_query.shape, f32)] * 4 + small_outs,
        [ids, kept_one, got_one, kept_two, got_two] + ([sent_two] if direct else []),
        smem=1,
    )
    if direct:
        sum_one, sum_two, sum_router, sum_bias = weight_grads[4:]
    else:
        small = lax.psum(small, ("node", "core", "tensor"))
        sum_one, sum_two, sum_router = small[:1], small[1:2], small[2 : 2 + experts]
        sum_bias = small[2 + experts : 2 + experts + heads, : 4 * 128].reshape(heads, 4, 128)
        sum_bias = sum_bias[:, :, :bucket_count].transpose(1, 0, 2).reshape(bias_table.shape[::-1])
    return (
        activations,
        input_grad,
        sum_one[0],
        *weight_grads[:4],
        sum_bias.T,
        sum_two[0],
        sum_router.T,
        grad_w_up_here,
        grad_w_down_here,
    )


def solution(mesh):
    dp, tensor = mesh.shape["dp"], mesh.shape["tensor"]
    grid = Mesh(mesh.devices.reshape(dp // GROUP, GROUP, tensor), ("node", "core", "tensor"))
    dp = ("node", "core")
    every = ("node", "core", "tensor")
    in_specs = (
        P(every, None),
        P(),
        P(dp, "tensor"),
        P(dp, "tensor"),
        P(dp, "tensor"),
        P(dp, "tensor"),
        P(),
        P(),
        P(),
        P(None, every),
        P(None, every),
        P(dp, None),
        P(),
        P(),
        P(dp, None),
    )
    out_specs = (
        P(every, None),
        P(every, None),
        P(),
        P(dp, "tensor"),
        P(dp, "tensor"),
        P(dp, "tensor"),
        P(dp, "tensor"),
        P(),
        P(),
        P(),
        P(None, every),
        P(None, every),
    )
    return jax.shard_map(
        per_device, mesh=grid, in_specs=in_specs, out_specs=out_specs, check_vma=False
    )
```

```python
import functools

import jax
import jax.numpy as jnp
from jax import lax
from jax.experimental import pallas as pl
from jax.experimental.pallas import tpu as pltpu
from jax.sharding import Mesh, PartitionSpec as P

HD = 64
GROUP = 2
FLOPS1 = 0
FLOPS2 = 0
DIRECT = 8
FORWARD_TILE = 256
BACK_TILE = 512

norm_eps = 1e-06
masked_value = -1e30
exact = lax.Precision.HIGHEST
bf16 = jnp.bfloat16
f32 = jnp.float32

VMEM = pl.BlockSpec(memory_space=pltpu.VMEM)
SMEM = pl.BlockSpec(memory_space=pltpu.SMEM)
ANY = pl.BlockSpec(memory_space=pl.ANY)


def across(shard, axis, bits):
    return lax.ppermute(shard, axis, [(i, i ^ bits) for i in range(lax.axis_size(axis))])


class Near:
    def __init__(self, array):
        self.array = array


class Raw(Near):
    pass


class Far(Raw):
    pass


def call(body, name, outs, args, smem=0, scratch=(), flops=0):
    arrays = [a.array if isinstance(a, Near) else a for a in args]
    results = [o.array if isinstance(o, Near) else o for o in outs]
    kept = sum(padded_bytes(a) for a in [*arrays, *results, *scratch] if is_plain(a))
    space = {Near: pltpu.VMEM, Far: pltpu.HBM}
    given = [
        pltpu.with_memory_space_constraint(x, space[type(a)]) if type(a) in space else x
        for a, x in zip(args, arrays)
    ]
    return pl.pallas_call(
        body,
        name=name,
        out_shape=[
            space[type(o)](x.shape, x.dtype) if type(o) in space else x
            for o, x in zip(outs, results)
        ],
        in_specs=[SMEM] * smem + [ANY if isinstance(a, Raw) else VMEM for a in args[smem:]],
        out_specs=[ANY if isinstance(o, Raw) else VMEM for o in outs],
        scratch_shapes=scratch,
        compiler_params=pltpu.CompilerParams(vmem_limit_bytes=kept + 10 * 1024 * 1024),
        cost_estimate=pl.CostEstimate(flops=flops, bytes_accessed=0, transcendentals=0),
    )(*given)


def is_plain(array):
    return getattr(array, "dtype", None) in (bf16, f32, jnp.int32)


def padded_bytes(array):
    *lead, rows, cols = (1, 1, *array.shape)
    size = jnp.dtype(array.dtype).itemsize
    for extent in lead:
        size *= extent
    return size * (-(-rows // 16) * 16) * (-(-cols // 128) * 128)


def out(shape, dtype):
    return jax.ShapeDtypeStruct(shape, dtype)


def mm(a, b):
    return jnp.dot(a, b, preferred_element_type=f32)


def mm_bt(a, b):
    return lax.dot_general(a, b, (((1,), (1,)), ((), ())), preferred_element_type=f32)


def mm_at(a, b):
    return lax.dot_general(a, b, (((0,), (0,)), ((), ())), preferred_element_type=f32)


def shares_kernel(ids, *refs):
    weights, (keep_ref, send_ref, near_ref, sems) = refs[:4], refs[4:]
    copies = [
        pltpu.make_async_copy(w, near_ref.at[i], sems.at[i]) for i, w in enumerate(weights)
    ]
    for copy in copies:
        copy.start()
    for copy in copies:
        copy.wait()
    first = ids[0] == 0
    cols = keep_ref.shape[1] // 4
    for i in range(4):
        low, high = near_ref[i, :, :cols], near_ref[i, :, cols:]
        keep_ref[:, i * cols : (i + 1) * cols] = jnp.where(first, low, high)
        send_ref[:, i * cols : (i + 1) * cols] = jnp.where(first, high, low)


def rows_kernel(ids, own_ref, got_ref, held_ref, out_ref):
    rows = own_ref.shape[0]
    out_ref[pl.ds(pl.multiple_of(ids[2] * rows, rows), rows), :] = own_ref[...]
    out_ref[pl.ds(pl.multiple_of((1 - ids[2]) * rows, rows), rows), :] = got_ref[...]


def move_kernel(count, *refs):
    sources, targets, sems = refs[:count], refs[-count - 1 : -1], refs[-1]
    copies = [
        pltpu.make_async_copy(a, b, sems.at[i]) for i, (a, b) in enumerate(zip(sources, targets))
    ]
    for copy in copies:
        copy.start()
    for copy in copies:
        copy.wait()


def unit_rows(x):
    wide = x.astype(f32)
    return wide * lax.rsqrt(jnp.mean(wide * wide, axis=1, keepdims=True) + norm_eps)


def tables_kernel(experts, capacity, direct, ids, routes_ref, turned_ref, plain_ref):
    rows, slots = plain_ref.shape
    routes = routes_ref[...]
    picks = routes == lax.broadcasted_iota(jnp.int32, (rows, experts), 1)
    upto = lax.broadcasted_iota(jnp.int32, (rows, rows), 0) >= lax.broadcasted_iota(
        jnp.int32, (rows, rows), 1
    )
    counts = mm(upto.astype(f32).astype(bf16), picks.astype(f32).astype(bf16))
    slot = jnp.sum(jnp.where(picks, counts - 1.0, 0.0), axis=1, keepdims=True).astype(jnp.int32)
    codes = lax.broadcasted_iota(jnp.int32, (1, slots), 1)
    expert = jnp.zeros((1, slots), jnp.int32)
    for i in range(1, experts):
        expert = expert + jnp.where(codes >= i * capacity, 1, 0)
    place = codes - expert * capacity
    plain = (routes == expert) & (slot == place)
    plain_ref[...] = plain.astype(f32).astype(bf16)
    turned = (routes == (expert ^ ids[1])) & (slot == place) if direct else plain
    turned_ref[...] = turned.astype(f32).astype(bf16)


def slots_kernel(table_ref, rows_ref, held_ref, out_ref):
    out_ref[...] = mm_at(table_ref[...], rows_ref[...]).astype(bf16)


def cots_kernel(parts, ids, own_ref, other_ref, wdown_ref, held_ref, cots_ref, back_ref, near_ref, sems, *scratch):
    slots = cots_ref.shape[0] // 2
    copies = []
    me = ids[1]
    for at, source in ((0, own_ref), (slots, other_ref)):
        if parts == 1:
            near_ref[at : at + slots, :] = source[...]
        else:
            rows = slots // parts
            for i in range(parts):
                scratch[0][i * rows : (i + 1) * rows, :] = source[me ^ i].astype(f32)
            near_ref[at : at + slots, :] = scratch[0][...].astype(bf16)
        copies.append(
            pltpu.make_async_copy(near_ref.at[at : at + slots], cots_ref.at[at : at + slots], sems.at[len(copies)])
        )
        copies[-1].start()
        back_ref[at : at + slots, :] = mm(near_ref[at : at + slots, :], wdown_ref[...])
    for copy in copies:
        copy.wait()


def attend_kernel(heads, parts, ids, own_ref, other_ref, gain_ref, vec_ref, row_docs, col_docs, *refs):
    pieces = refs[:parts]
    w_ref, wo_ref, x_ref, qkv_ref, mixed_ref, keep_ref, send_ref, *probs_refs = refs[parts:-1]
    seq_ref = refs[-1]
    core = ids[0]
    me = ids[1]
    seq = x_ref.shape[0]
    width = heads * HD
    half = seq // GROUP
    span = seq + FORWARD_TILE
    rows = pieces[0].shape[0]
    for i, piece in enumerate(pieces):
        start = 0 if parts == 1 else pl.multiple_of((me ^ i) * rows, rows)
        w_ref[pl.ds(start, rows), :] = piece[...]
    for place, source in ((core, own_ref), (1 - core, other_ref)):
        at = pl.ds(pl.multiple_of(place * half, half), half)
        x = source[...]
        x_ref[at, :] = x
        seq_ref[at, :] = (unit_rows(x) * gain_ref[...]).astype(bf16)
    wo_ref[...] = w_ref[:, 3 * width :]
    for i in range(0, seq, 256):
        qkv_ref[i : i + 256, :] = mm(seq_ref[i : i + 256, :], w_ref[:, : 3 * width]).astype(bf16)
    for h in range(heads):
        at = h * HD
        key = qkv_ref[:, width + at : width + at + HD]
        value = qkv_ref[:, 2 * width + at : 2 * width + at + HD]
        for i in range(0, seq, FORWARD_TILE):
            base = seq - FORWARD_TILE - i
            seg = jnp.broadcast_to(vec_ref[h : h + 1, base : base + span], (FORWARD_TILE, span))
            bias = pltpu.roll(seg, span - FORWARD_TILE + 1, 1, stride=1, stride_axis=0)[:, :seq]
            scores = mm_bt(qkv_ref[i : i + FORWARD_TILE, at : at + HD], key) * HD**-0.5 + bias
            scores = jnp.where(row_docs[i : i + FORWARD_TILE, :] == col_docs[...], scores, masked_value)
            peak = jnp.max(scores, axis=1, keepdims=True)
            exp_scores = jnp.exp(scores - peak)
            probs = exp_scores / jnp.sum(exp_scores, axis=1, keepdims=True)
            probs_refs[h][i : i + FORWARD_TILE, :] = probs.astype(bf16)
            mixed_ref[i : i + FORWARD_TILE, at : at + HD] = mm(probs.astype(bf16), value).astype(bf16)
    keep_ref[...] = mixed_ref[pl.ds(pl.multiple_of(core * half, half), half), :]
    send_ref[...] = mixed_ref[pl.ds(pl.multiple_of((1 - core) * half, half), half), :]


def attended_kernel(keep_ref, got_ref, wo_ref, wo_other_ref, held_ref, out_ref):
    total = mm_bt(keep_ref[...], wo_ref[...]) + mm_bt(got_ref[...], wo_other_ref[...])
    out_ref[...] = total.astype(bf16)


def dispatch_kernel(hidden_ref, gain_ref, table_ref, *blocks):
    hidden = hidden_ref[...]
    scale = lax.rsqrt(jnp.mean(hidden * hidden, axis=1, keepdims=True) + norm_eps)
    normed = (hidden * scale * gain_ref[...]).astype(bf16)
    slots = mm_at(table_ref[...], normed)
    rows = blocks[0].shape[0]
    for i, block in enumerate(blocks):
        block[...] = slots[i * rows : (i + 1) * rows, :].astype(bf16)


def expert_kernel(ids, own_ref, other_ref, h_ref, wup_ref, wr_ref, *refs):
    active_ref, gup_ref, chosen_ref, keep_ref, send_ref, router_ref, all_ref = refs
    rows = own_ref.shape[0]
    step = rows
    router = jnp.zeros(router_ref.shape, f32)
    root = 0.7978845608028654
    for i in range(0, 2 * rows, step):
        src = own_ref if i < rows else other_ref
        at = i % rows
        slots = src[at : at + step, :]
        all_ref[i : i + step, :] = slots
        logits = mm_bt(slots, wr_ref[...])
        peak = jnp.max(logits, axis=1, keepdims=True)
        exp_logits = jnp.exp(logits - peak)
        gates = exp_logits / jnp.sum(exp_logits, axis=1, keepdims=True)
        mine = lax.broadcasted_iota(jnp.int32, gates.shape, 1) == ids[1]
        chosen = jnp.sum(jnp.where(mine, gates, 0.0), axis=1, keepdims=True)
        chosen_ref[i : i + step, :] = chosen
        up = mm(slots, wup_ref[...])
        square = up * up
        bent = jnp.tanh(root * (up + 0.044715 * up * square))
        low = (0.5 * up * (1.0 + bent)).astype(bf16)
        active_ref[i : i + step, :] = low
        slope = 0.5 * (1.0 + bent) + 0.5 * up * (1.0 - bent * bent) * root * (
            1.0 + 3.0 * 0.044715 * square
        )
        back = h_ref[i : i + step, :]
        gup = (chosen * back * slope).astype(bf16)
        gup_ref[i : i + step, :] = gup
        grad_chosen = jnp.sum(low.astype(f32) * back, axis=1, keepdims=True)
        grad_logits = gates * (jnp.where(mine, 1.0, 0.0) - chosen) * grad_chosen
        grad_logits = grad_logits.astype(bf16)
        router = router + mm_at(grad_logits, slots)
        grad = mm_bt(gup, wup_ref[...]) + mm(grad_logits, wr_ref[...])
        if i < rows:
            keep_ref[at : at + step, :] = grad
        else:
            send_ref[at : at + step, :] = grad.astype(bf16)
    router_ref[...] = router


def expert_out_kernel(active_ref, chosen_ref, wdown_ref, held_ref, keep_ref, send_ref):
    rows = keep_ref.shape[0]
    result = mm_bt(active_ref[...], wdown_ref[...]) * chosen_ref[...]
    keep_ref[...] = result[:rows, :]
    send_ref[...] = result[rows:, :].astype(bf16)


def expert_grads_kernel(slots_ref, cots_ref, active_ref, gup_ref, chosen_ref, held_ref, gwup_ref, gwdown_ref):
    gwup_ref[...] = mm_at(slots_ref[...], gup_ref[...])
    grads = (chosen_ref[...] * cots_ref[...].astype(f32)).astype(bf16)
    gwdown_ref[...] = mm_at(grads, active_ref[...])


def join_kernel(keep_ref, got_ref, *blocks):
    total = keep_ref[...] + got_ref[...].astype(f32)
    rows = blocks[0].shape[0]
    for i, block in enumerate(blocks):
        block[...] = total[i * rows : (i + 1) * rows, :].astype(bf16)


def join_natural_kernel(parts, ids, keep_ref, got_ref, out_ref):
    total = keep_ref[...] + got_ref[...].astype(f32)
    if parts == 1:
        out_ref[...] = total.astype(bf16)
        return
    rows = out_ref.shape[1]
    for i in range(parts):
        out_ref[ids[1] ^ i] = total[i * rows : (i + 1) * rows, :].astype(bf16)


def gather_kernel(back_table_ref, *refs):
    blocks = refs[:-1]
    slots = jnp.concatenate([b[...].astype(f32) for b in blocks], axis=0).astype(bf16)
    refs[-1][...] = mm(back_table_ref[...], slots).astype(bf16)


def hidden_back_kernel(ids, hidden_ref, own_ref, got_ref, cot_ref, gain_ref, held_ref, grad_ref, low_ref, dgain_ref, all_ref):
    hidden = hidden_ref[...]
    grad_normed = own_ref[...].astype(f32) + got_ref[...].astype(f32)
    scale = lax.rsqrt(jnp.mean(hidden * hidden, axis=1, keepdims=True) + norm_eps)
    dgain_ref[...] = jnp.sum(grad_normed * hidden * scale, axis=0, keepdims=True)
    pulled = gain_ref[...] * grad_normed
    inner = jnp.mean(pulled * hidden, axis=1, keepdims=True)
    grad = cot_ref[...].astype(f32) + scale * pulled - hidden * (scale * scale * scale) * inner
    low_ref[...] = grad.astype(bf16)
    all_ref[...] = grad
    rows = grad_ref.shape[0]
    grad_ref[...] = all_ref[pl.ds(pl.multiple_of(ids[2] * rows, rows), rows), :]


def returned_kernel(ids, table_ref, slots_ref, held_ref, keep_ref, send_ref):
    rows = keep_ref.shape[0]
    mine = table_ref[pl.ds(pl.multiple_of(ids[2] * rows, rows), rows), :]
    keep_ref[...] = mm(mine, slots_ref[...]).astype(bf16)
    theirs = table_ref[pl.ds(pl.multiple_of((1 - ids[2]) * rows, rows), rows), :]
    send_ref[...] = mm(theirs, slots_ref[...]).astype(bf16)


def activations_kernel(ids, hidden_ref, own_ref, got_ref, out_ref):
    rows = out_ref.shape[0]
    hidden = hidden_ref[pl.ds(pl.multiple_of(ids[2] * rows, rows), rows), :]
    out_ref[...] = (hidden + (own_ref[...].astype(f32) + got_ref[...].astype(f32))).astype(bf16)


def normed_sum_kernel(ids, keep_ref, got_ref, held_ref, own_ref, send_ref, all_ref):
    all_ref[...] = keep_ref[...] + got_ref[...].astype(f32)
    rows = own_ref.shape[0]
    own_ref[...] = all_ref[pl.ds(pl.multiple_of(ids[2] * rows, rows), rows), :]
    theirs = pl.ds(pl.multiple_of((1 - ids[2]) * rows, rows), rows)
    send_ref[...] = all_ref[theirs, :].astype(bf16)


def heads_back(heads, first, qkv_ref, gm_ref, probs, dqkv_ref, diag_ref, ds_ref):
    seq = qkv_ref.shape[0]
    width = heads * HD
    here = len(probs) * HD
    span = seq + BACK_TILE
    flip = (
        lax.broadcasted_iota(jnp.int32, (BACK_TILE, BACK_TILE), 0)
        + lax.broadcasted_iota(jnp.int32, (BACK_TILE, BACK_TILE), 1)
        == BACK_TILE - 1
    ).astype(bf16)
    for h, probs_ref in enumerate(probs):
        at = (first + h) * HD
        to = h * HD
        key = qkv_ref[:, width + at : width + at + HD]
        value = qkv_ref[:, 2 * width + at : 2 * width + at + HD]
        for i in range(0, seq, BACK_TILE):
            probs_rows = probs_ref[i : i + BACK_TILE, :].astype(f32)
            grad_probs = mm_bt(gm_ref[i : i + BACK_TILE, at : at + HD], value)
            inner = jnp.sum(probs_rows * grad_probs, axis=1, keepdims=True)
            grad_scores = (probs_rows * (grad_probs - inner)).astype(bf16)
            ds_ref[i : i + BACK_TILE, :] = grad_scores
            dqkv_ref[i : i + BACK_TILE, to : to + HD] = (mm(grad_scores, key) * HD**-0.5).astype(bf16)
            flipped = mm(flip, grad_scores)
            padded = jnp.concatenate([flipped, jnp.zeros((BACK_TILE, BACK_TILE), f32)], axis=1)
            skewed = pltpu.roll(padded, 0, 1, stride=1, stride_axis=0)
            base = seq - BACK_TILE - i
            row = first + h
            diag_ref[row : row + 1, base : base + span] += jnp.sum(skewed, axis=0, keepdims=True)
        dqkv_ref[:, here + to : here + to + HD] = (
            mm_at(ds_ref[...], qkv_ref[:, at : at + HD]) * HD**-0.5
        ).astype(bf16)
        dqkv_ref[:, 2 * here + to : 2 * here + to + HD] = mm_at(
            probs_ref[...], gm_ref[:, at : at + HD]
        ).astype(bf16)


def send_rows(parts, me, gw_ref, outs, keep_ref):
    if parts == 1:
        outs[0][...] = gw_ref[...].astype(bf16)
        return
    rows = gw_ref.shape[0] // parts
    for i in range(parts // 2):
        at = slice(i * rows, (i + 1) * rows)
        keep_ref[at, :] = gw_ref[pl.ds(pl.multiple_of((me ^ 2 * i) * rows, rows), rows), :]
        there = pl.ds(pl.multiple_of((me ^ 2 * i ^ 1) * rows, rows), rows)
        outs[1][at, :] = gw_ref[there, :].astype(bf16)


def first_back_kernel(heads, parts, ids, own_ref, other_ref, gain_ref, *refs):
    wo_ref, qkv_ref, probs_ref, x_ref, mixed_ref = refs[:5]
    gm_ref, dqkv_ref, diag_ref, seq_ref, *outs = refs[5:-3]
    ga_ref, ds_ref, gw_ref = refs[-3:]
    core = ids[0]
    half = own_ref.shape[0]
    ga_ref[pl.ds(pl.multiple_of(core * half, half), half), :] = own_ref[...]
    ga_ref[pl.ds(pl.multiple_of((1 - core) * half, half), half), :] = other_ref[...]
    gm_ref[...] = mm(ga_ref[...], wo_ref[...]).astype(bf16)
    diag_ref[...] = jnp.zeros_like(diag_ref)
    heads_back(heads, 0, qkv_ref, gm_ref, [probs_ref], dqkv_ref, diag_ref, ds_ref)
    cut = dqkv_ref.shape[1]
    seq_ref[...] = (unit_rows(x_ref[...]) * gain_ref[...]).astype(bf16)
    gw_ref[:, :cut] = mm_at(seq_ref[...], dqkv_ref[...])
    gw_ref[:, cut:] = mm_at(ga_ref[...], mixed_ref[...])
    send_rows(parts, ids[1], gw_ref, outs, outs[0])


def second_back_kernel(
    heads, parts, ids, gm_ref, first_ref, diag_in_ref, hot_ref, seq_ref, gain_ref, router_ref, *refs
):
    count = heads + 2
    qkv_ref, *probs, x_ref, w_ref = refs[:count]
    refs = refs[count:]
    keep_ref, send_ref, small_ref, *outs = refs[:-7]
    diag_ref, dqkv_ref, all_ref, ds_ref, gw_ref, near_ref, sem = refs[-7:]
    core, me, side = ids[0], ids[1], ids[2]
    half = keep_ref.shape[0]
    diag_ref[...] = diag_in_ref[...]
    heads_back(heads, 1, qkv_ref, gm_ref, probs, dqkv_ref, diag_ref, ds_ref)
    gw_ref[...] = mm_at(seq_ref[...], dqkv_ref[...])
    send_rows(parts, me, gw_ref, outs, near_ref)
    copy = None
    if parts > 1:
        copy = pltpu.make_async_copy(near_ref, outs[0], sem)
        copy.start()
    rest = (heads - 1) * HD
    for i in range(3):
        at = i * heads * HD
        all_ref[:, at : at + HD] = first_ref[:, i * HD : (i + 1) * HD]
        all_ref[:, at + HD : at + heads * HD] = dqkv_ref[:, i * rest : (i + 1) * rest]
    gain = jnp.zeros((1, x_ref.shape[1]), f32)
    for place, mine in ((core, True), (1 - core, False)):
        rows = pl.ds(pl.multiple_of(place * half, half), half)
        grad = mm_bt(all_ref[rows, :], w_ref[:, : all_ref.shape[1]])
        gain = gain + jnp.sum(grad * unit_rows(x_ref[rows, :]), axis=0, keepdims=True)
        if mine:
            keep_ref[...] = grad
        else:
            send_ref[...] = grad.astype(bf16)
    small_ref[...] = jnp.zeros_like(small_ref)
    small_ref[0:1, :] = gain
    small_ref[1:2, :] = jnp.where(side == 0, gain_ref[...], 0.0)
    experts = router_ref.shape[0]
    small_ref[2 : 2 + experts, :] = router_ref[...]
    bias = jnp.dot(diag_ref[...], hot_ref[...], precision=exact, preferred_element_type=f32)
    lanes = bias.shape[1]
    for i in range(2 * GROUP):
        small_ref[2 + experts : 2 + experts + heads, i * lanes : (i + 1) * lanes] = jnp.where(
            side * GROUP + core == i, bias[:heads, :], 0.0
        )
    if copy is not None:
        copy.wait()


def fold_kernel(
    keep_ref, got_ref, small_ref, small_got_ref, second_ref, returned_ref,
    second_out, returned_out, small_out, own_ref, *sends
):
    returned_out[...] = returned_ref[...]
    end, cols = second_ref.shape
    high = small_ref.shape[0]
    second_out[:end, :] = second_ref[...]
    for i in range(2):
        at = slice(i * cols, (i + 1) * cols)
        low = (small_ref[:, at] + small_got_ref[:, at]).astype(bf16)
        second_out[end + i * high : end + (i + 1) * high, :] = low
        small_out[i * high : (i + 1) * high, :] = low.astype(f32)
    total = keep_ref[...] + got_ref[...].astype(f32)
    rows = own_ref.shape[0]
    own_ref[...] = total[:rows, :]
    for i, send in enumerate(sends):
        send[...] = total[(i + 1) * rows : (i + 2) * rows, :].astype(bf16)


def quarters(refs, at):
    a, b, c, d = (r[at, :].astype(f32) for r in refs)
    return (a + b) + (c + d)


def split_cores(core, refs, keep_ref, send_ref):
    rows = keep_ref.shape[0]
    keep_ref[...] = quarters(refs, pl.ds(pl.multiple_of(core * rows, rows), rows))
    send_ref[:rows, :] = quarters(refs, pl.ds(pl.multiple_of((1 - core) * rows, rows), rows))


def fold_second_kernel(ids, keep_ref, got_ref, small_ref, grad_ref, *refs):
    first = refs[:4]
    grad_out, keep_one_ref, send_one_ref, own_ref, *sends = refs[4:]
    grad_out[...] = grad_ref[...]
    end = keep_ref.shape[0]
    total = keep_ref[...] + got_ref[:end, :].astype(f32)
    small = (small_ref[...] + got_ref[end:, :].astype(f32)).astype(bf16)
    rows = keep_one_ref.shape[0] * 2
    for i, block in enumerate((own_ref, *sends)):
        block[:rows, :] = total[i * rows : (i + 1) * rows, :].astype(block.dtype)
        block[rows:, :] = small.astype(block.dtype)
    split_cores(ids[0], first, keep_one_ref, send_one_ref)


def sum_nodes_kernel(ids, *refs):
    second = refs[:4]
    keep_ref, send_ref = refs[-2:]
    split_cores(ids[0], second, keep_ref, send_ref)
    rows = keep_ref.shape[0]
    send_ref[rows:, :] = quarters(second, slice(2 * rows, second[0].shape[0]))


def columns_kernel(heads, ids, keep_one, got_one, keep_two, got_two, *refs):
    outs = refs[:4] if len(refs) == 4 else refs[1:5]
    core = ids[0]
    rows = keep_one.shape[0]
    cols = heads * HD
    rest = cols - HD
    for c in range(2):
        at = c * cols
        mine = core == c
        one = jnp.where(mine, keep_one[...], got_one[...])
        two = jnp.where(mine, keep_two[...], got_two[:rows, :])
        for i in range(3):
            outs[i][:, at : at + HD] = one[:, i * HD : (i + 1) * HD]
            outs[i][:, at + HD : at + cols] = two[:, i * rest : (i + 1) * rest]
        outs[3][:, at : at + cols] = one[:, 3 * HD : 3 * HD + cols]
    if len(refs) == 4:
        return
    gain_one_ref, gain_two_ref, router_ref, bias_ref = refs[5:]
    small = refs[0][rows:, :] + got_two[rows:, :]
    high = small.shape[0] // 2
    wide = jnp.concatenate([small[:high, :], small[high:, :]], axis=1)
    experts = router_ref.shape[0]
    gain_one_ref[...] = wide[0:1, :]
    gain_two_ref[...] = wide[1:2, :]
    router_ref[...] = wide[2 : 2 + experts, :]
    for i in range(2 * GROUP):
        for h in range(heads):
            row = 2 + experts + h
            bias_ref[i * heads + h : i * heads + h + 1, :] = wide[
                row : row + 1, i * 128 : i * 128 + bias_ref.shape[1]
            ]


def input_kernel(keep_ref, got_ref, grad_ref, x_ref, gain_ref, out_ref):
    grad_normed = keep_ref[...] + got_ref[...].astype(f32)
    wide = x_ref[...].astype(f32)
    scale = lax.rsqrt(jnp.mean(wide * wide, axis=1, keepdims=True) + norm_eps)
    pulled = gain_ref[...] * grad_normed
    inner = jnp.mean(pulled * wide, axis=1, keepdims=True)
    out_ref[...] = grad_ref[...] + scale * pulled - wide * (scale * scale * scale) * inner


def in_order(first, mine, other):
    return jnp.where(first, jnp.concatenate([mine, other]), jnp.concatenate([other, mine]))


def per_device(
    tokens,
    gain_one,
    w_query,
    w_key,
    w_value,
    w_out,
    bias_table,
    gain_two,
    w_router,
    w_up,
    w_down,
    routes,
    doc_lengths,
    buckets,
    cotangent,
):
    own_rows, width = tokens.shape
    block_rows = routes.shape[0]
    seq = block_rows * GROUP
    cols = w_query.shape[1] // GROUP
    heads = cols // HD
    experts = w_router.shape[1]
    capacity = max(2, (5 * block_rows + 4 * experts - 1) // (4 * experts))
    slots = experts * capacity
    nodes = lax.axis_size("node")
    core = lax.axis_index("core")
    side = lax.axis_index("tensor")
    me = lax.axis_index("node")
    direct = nodes == DIRECT
    parts = nodes if direct else 1
    ids = jnp.stack([core, me, side]).astype(jnp.int32)
    node_rows = width // nodes

    def trade(blocks):
        if direct:
            return [blocks[0]] + [across(blocks[i], "node", i) for i in range(1, nodes)]
        stacked = blocks[0].reshape(nodes, -1, blocks[0].shape[1])
        back = lax.all_to_all(stacked, "node", split_axis=0, concat_axis=0, tiled=True)
        return [back.reshape(blocks[0].shape)]

    def trade_natural(rows):
        stacked = rows.reshape(nodes, -1, rows.shape[-1])
        return lax.all_to_all(stacked, "node", split_axis=0, concat_axis=0, tiled=True)

    share = out((w_query.shape[0], 4 * cols), bf16)
    share_kept, share_sent = call(
        shares_kernel,
        "shares",
        [share, share],
        [ids, *(Far(w) for w in (w_query, w_key, w_value, w_out))],
        smem=1,
        scratch=[pltpu.VMEM((4, *w_query.shape), bf16), pltpu.SemaphoreType.DMA((4,))],
    )
    piece = in_order(core == 0, share_kept, across(share_sent, "core", 1))
    if direct:
        pieces = {0: piece}
        for i in (4, 6, 2):
            pieces[i] = across(piece, "node", i)
        for i in (0, 2, 4, 6):
            pieces[i + 1] = across(pieces[i], "node", 1)
        pieces = [pieces[i] for i in range(nodes)]
    else:
        pieces = [lax.all_gather(piece, "node", axis=0, tiled=True)]

    x_rows = call(
        rows_kernel,
        "rows",
        [out((block_rows, width), bf16)],
        [ids, tokens, across(tokens, "tensor", 1), Raw(pieces[min(1, parts - 1)])],
        smem=1,
    )[0]
    x_other = across(x_rows, "core", 1)
    gain_first = gain_one.astype(f32)[None, :]
    gain_second = gain_two.astype(f32)[None, :]

    back_table, plain_back_table = call(
        functools.partial(tables_kernel, experts, capacity, direct),
        "tables",
        [out((block_rows, slots), bf16)] * 2,
        [ids, routes],
        smem=1,
    )

    lengths_row = lax.dynamic_slice_in_dim(doc_lengths, me, 1, 0)[0]
    ends = jnp.cumsum(lengths_row)
    places = jnp.arange(seq, dtype=jnp.int32)
    docs = jnp.sum((ends[None, :] <= places[:, None]).astype(jnp.int32), axis=1)
    bucket_count = bias_table.shape[0]
    bucket_hot = (
        jnp.pad(buckets, (0, 1))[:, None] == jnp.arange(128, dtype=jnp.int32)[None, :]
    ).astype(f32)
    head_start = (side * GROUP + core) * heads
    bias_here = lax.dynamic_slice_in_dim(bias_table, head_start, heads, 1)
    bias_here = jnp.pad(bias_here, ((0, 128 - bucket_count), (0, 0)))
    bias_vectors = lax.dot_general(
        bias_here, bucket_hot, (((0,), (1,)), ((), ())), precision=exact, preferred_element_type=f32
    )

    weights, wo, x_seq, qkv, mixed, mixed_kept, mixed_sent, *probs = call(
        functools.partial(attend_kernel, heads, parts),
        "attend",
        [
            out((width, 4 * cols), bf16),
            out((width, cols), bf16),
            out((seq, width), bf16),
            out((seq, 3 * cols), bf16),
            out((seq, cols), bf16),
            out((block_rows, cols), bf16),
            out((block_rows, cols), bf16),
            *([out((seq, seq), bf16)] * heads),
        ],
        [
            ids,
            x_rows,
            Near(x_other),
            gain_first,
            bias_vectors,
            docs[:, None],
            docs[None, :],
            *(Near(p) for p in pieces),
        ],
        smem=1,
        scratch=[pltpu.VMEM((seq, width), bf16)],
    )
    kept = [weights, wo, x_seq, qkv, mixed, *probs]
    weights, wo_far, x_seq, qkv, mixed, *probs = call(
        functools.partial(move_kernel, len(kept)),
        "park",
        [Far(out(a.shape, a.dtype)) for a in kept],
        [*(Near(a) for a in kept)],
        scratch=[pltpu.SemaphoreType.DMA((len(kept),))],
    )

    natural = (nodes, slots // nodes, width) if direct else (slots, width)
    cot_slots = call(
        slots_kernel,
        "cot_slots",
        [out((slots, width), bf16)],
        [plain_back_table, cotangent, Raw(pieces[min(3, parts - 1)])],
    )[0]
    cots_own = trade_natural(cot_slots).reshape(natural)
    cots_other = across(cots_own, "core", 1)

    mixed_got = across(mixed_sent, "core", 1)
    attended = call(
        attended_kernel,
        "attended",
        [out((block_rows, width), bf16)],
        [mixed_kept, mixed_got, wo, across(wo, "core", 1), Far(mixed)],
    )[0]
    attended_got = across(attended, "tensor", 1)
    block_shapes = [out((slots // parts, width), bf16)] * parts
    hidden = x_rows.astype(f32) + (attended.astype(f32) + attended_got.astype(f32))
    blocks = call(
        dispatch_kernel,
        "dispatch",
        block_shapes,
        [hidden, gain_second, back_table],
    )
    received = trade(blocks)
    cots, back_active = call(
        functools.partial(cots_kernel, parts),
        "cots",
        [Far(out((2 * slots, width), bf16)), Near(out((2 * slots, w_down.shape[1]), f32))],
        [ids, Near(cots_own), Near(cots_other), w_down, Raw(blocks[0])],
        smem=1,
        scratch=[
            pltpu.VMEM((2 * slots, width), bf16),
            pltpu.SemaphoreType.DMA((2,)),
            *([pltpu.VMEM((slots, width), f32)] if direct else []),
        ],
    )
    slots_own = jnp.concatenate(received)
    slots_other = across(slots_own, "core", 1)
    active, grad_upward, chosen, grad_kept, grad_sent, router_part, slots_all = call(
        expert_kernel,
        "expert",
        [
            Near(out((2 * slots, w_up.shape[1]), bf16)),
            Near(out((2 * slots, w_up.shape[1]), bf16)),
            Near(out((2 * slots, 1), f32)),
            out((slots, width), f32),
            out((slots, width), bf16),
            Near(out(w_router.shape[::-1], f32)),
            Near(out((2 * slots, width), bf16)),
        ],
        [ids, slots_own, Near(slots_other), Near(back_active), w_up, w_router.T],
        smem=1,
    )
    grad_blocks = call(
        join_kernel, "join_grad", block_shapes, [grad_kept, Near(across(grad_sent, "core", 1))]
    )
    grad_back = trade(grad_blocks)
    grad_normed_two = call(
        gather_kernel,
        "gather_grad",
        [out((block_rows, width), bf16)],
        [back_table, *grad_back],
    )[0]
    grad_normed_two_got = across(grad_normed_two, "tensor", 1)

    out_kept, out_sent = call(
        expert_out_kernel,
        "expert_out",
        [out((slots, width), f32), out((slots, width), bf16)],
        [Near(active), Near(chosen), w_down, Raw(grad_blocks[-1])],
    )
    out_slots = call(
        functools.partial(join_natural_kernel, parts),
        "join_out",
        [out(natural, bf16)],
        [ids, out_kept, Near(across(out_sent, "core", 1))],
        smem=1,
    )[0]
    out_back = trade_natural(out_slots.reshape(slots, width)).reshape(slots, width)
    half_block = (own_rows, width)

    kept = [weights, wo_far, x_seq, qkv, mixed, *probs]
    weights, wo, x_seq, qkv, mixed, *probs = call(
        functools.partial(move_kernel, len(kept)),
        "unpark",
        [out(a.shape, a.dtype) for a in kept],
        [*(Far(a) for a in kept), Raw(out_slots)],
        scratch=[pltpu.SemaphoreType.DMA((len(kept),))],
    )
    grad_hidden, grad_attended, gain_two_part = call(
        hidden_back_kernel,
        "hidden_back",
        [Near(out(half_block, f32)), out((block_rows, width), bf16), Near(out((1, width), f32))],
        [
            ids,
            Near(hidden),
            grad_normed_two,
            Near(grad_normed_two_got),
            cotangent,
            gain_second,
            Raw(mixed),
        ],
        smem=1,
        scratch=[pltpu.VMEM((block_rows, width), f32)],
    )
    grad_attended_other = across(grad_attended, "core", 1)
    chunk = 3 * HD + cols
    other_chunk = 3 * (cols - HD)
    small_rows = -(-(2 + experts + heads) // 16) * 16
    if direct:
        first_shapes = [out((width // 2, chunk), t) for t in (f32, bf16)]
        second_shapes = [Far(out((width // 2, other_chunk), f32)), out((width // 2, other_chunk), bf16)]
    else:
        first_shapes = [out((width, chunk), bf16)]
        second_shapes = [out((width, other_chunk), bf16)]
    grad_mixed, first_dqkv, diagonals, normed_seq, *first_chunk = call(
        functools.partial(first_back_kernel, heads, parts),
        "first_back",
        [
            out((seq, cols), bf16),
            out((seq, 3 * HD), bf16),
            out((8, 2 * seq), f32),
            out((seq, width), bf16),
            *first_shapes,
        ],
        [
            ids,
            grad_attended,
            Near(grad_attended_other),
            gain_first,
            *(wo, qkv, probs[0], x_seq, mixed),
        ],
        smem=1,
        flops=FLOPS1,
        scratch=[
            pltpu.VMEM((seq, width), bf16),
            pltpu.VMEM((seq, seq), bf16),
            pltpu.VMEM((width, chunk), f32),
        ],
    )
    grad_kept, grad_sent, small, *second_chunk = call(
        functools.partial(second_back_kernel, heads, parts),
        "second_back",
        [
            out((block_rows, width), f32),
            out((block_rows, width), bf16),
            out((small_rows, width), f32),
            *second_shapes,
        ],
        [
            ids,
            grad_mixed,
            first_dqkv,
            diagonals,
            bucket_hot,
            normed_seq,
            Near(gain_two_part),
            Near(router_part),
            *(qkv, *probs[1:], x_seq, weights),
        ],
        smem=1,
        flops=FLOPS2,
        scratch=[
            pltpu.VMEM((8, 2 * seq), f32),
            pltpu.VMEM((seq, other_chunk), bf16),
            pltpu.VMEM((seq, 3 * cols), bf16),
            pltpu.VMEM((seq, seq), bf16),
            pltpu.VMEM((width, other_chunk), f32),
            pltpu.VMEM((width // 2, other_chunk), f32),
            pltpu.SemaphoreType.DMA,
        ],
    )

    shard_rows = w_query.shape[0]
    returned, returned_sent = call(
        returned_kernel,
        "returned",
        [out(half_block, bf16), out(half_block, bf16)],
        [ids, plain_back_table, Near(out_back), Raw(grad_kept)],
        smem=1,
    )
    part = out((shard_rows, chunk), f32)
    if direct:
        tall = width // 2 + 2 * small_rows
        second_sent, returned_sent, small, own_one, *send_one = call(
            fold_kernel,
            "fold_first",
            [
                out((tall, chunk), bf16),
                out(returned_sent.shape, bf16),
                out((2 * small_rows, chunk), f32),
                out((node_rows, chunk), f32),
                *([out((node_rows, chunk), bf16)] * 3),
            ],
            [
                first_chunk[0],
                across(first_chunk[1], "node", 1),
                small,
                across(small, "tensor", 1),
                second_chunk[1],
                returned_sent,
            ],
        )
        got_one = [across(b, "node", 2 * i + 2) for i, b in enumerate(send_one)]
        first_done = send_one[0]
    else:
        sums = [jnp.sum(trade_natural(c[0]).astype(f32), axis=0) for c in (first_chunk, second_chunk)]
        kept_one, kept_two = (
            lax.dynamic_slice_in_dim(s, core * shard_rows, shard_rows, 0) for s in sums
        )
        sent_one, sent_two = (
            lax.dynamic_slice_in_dim(s, (1 - core) * shard_rows, shard_rows, 0) for s in sums
        )
        first_done, second_done = kept_one, kept_two
    grad_normed, grad_normed_sent = call(
        normed_sum_kernel,
        "normed_sum",
        [Near(out(half_block, f32)), out(half_block, bf16)],
        [ids, grad_kept, Near(across(grad_sent, "core", 1)), Raw(first_done)],
        smem=1,
        scratch=[pltpu.VMEM((block_rows, width), f32)],
    )
    if direct:
        high = node_rows + 2 * small_rows
        grad_normed_sent, kept_one, sent_one, own_two, *send_two = call(
            fold_second_kernel,
            "fold_second",
            [out(half_block, bf16), part, part, out((high, chunk), f32), *([out((high, chunk), bf16)] * 3)],
            [
                ids,
                second_chunk[0],
                across(second_sent, "node", 1),
                small,
                grad_normed_sent,
                own_one,
                *got_one,
            ],
            smem=1,
        )
        got_two = [across(b, "node", 2 * i + 2) for i, b in enumerate(send_two)]
        second_done = send_two[0]
    grad_w_up_here, grad_w_down_here = call(
        expert_grads_kernel,
        "expert_grads",
        [out(w_up.shape, f32), out(w_down.shape, f32)],
        [
            Near(slots_all),
            cots,
            *(Near(a) for a in (active, grad_upward, chosen)),
            Raw(second_done),
        ],
    )
    input_grad = call(
        input_kernel,
        "input_grad",
        [out(half_block, f32)],
        [
            Near(grad_normed),
            Near(across(grad_normed_sent, "tensor", 1)),
            Near(grad_hidden),
            tokens,
            gain_first,
        ],
    )[0]
    activations = call(
        activations_kernel,
        "activations",
        [out(half_block, bf16)],
        [ids, Near(hidden), Near(returned), Near(across(returned_sent, "tensor", 1))],
        smem=1,
    )[0]
    if direct:
        kept_two, sent_two = call(
            sum_nodes_kernel,
            "sum_nodes",
            [part, out((shard_rows + 2 * small_rows, chunk), f32)],
            [
                ids,
                own_two,
                *got_two,
                *(Far(a) for a in (grad_w_up_here, activations, input_grad)),
            ],
            smem=1,
        )
    got_one = across(sent_one, "core", 1)
    got_two = across(sent_two, "core", 1)
    small_outs = []
    if direct:
        small_outs = [
            out((1, width), f32),
            out((1, width), f32),
            out((experts, width), f32),
            out(bias_table.shape[::-1], f32),
        ]
    weight_grads = call(
        functools.partial(columns_kernel, heads),
        "columns",
        [out(w_query.shape, f32)] * 4 + small_outs,
        [ids, kept_one, got_one, kept_two, got_two] + ([sent_two] if direct else []),
        smem=1,
    )
    if direct:
        sum_one, sum_two, sum_router, sum_bias = weight_grads[4:]
    else:
        small = lax.psum(small, ("node", "core", "tensor"))
        sum_one, sum_two, sum_router = small[:1], small[1:2], small[2 : 2 + experts]
        sum_bias = small[2 + experts : 2 + experts + heads, : 4 * 128].reshape(heads, 4, 128)
        sum_bias = sum_bias[:, :, :bucket_count].transpose(1, 0, 2).reshape(bias_table.shape[::-1])
    return (
        activations,
        input_grad,
        sum_one[0],
        *weight_grads[:4],
        sum_bias.T,
        sum_two[0],
        sum_router.T,
        grad_w_up_here,
        grad_w_down_here,
    )


def solution(mesh):
    dp, tensor = mesh.shape["dp"], mesh.shape["tensor"]
    grid = Mesh(mesh.devices.reshape(dp // GROUP, GROUP, tensor), ("node", "core", "tensor"))
    dp = ("node", "core")
    every = ("node", "core", "tensor")
    in_specs = (
        P(every, None),
        P(),
        P(dp, "tensor"),
        P(dp, "tensor"),
        P(dp, "tensor"),
        P(dp, "tensor"),
        P(),
        P(),
        P(),
        P(None, every),
        P(None, every),
        P(dp, None),
        P(),
        P(),
        P(dp, None),
    )
    out_specs = (
        P(every, None),
        P(every, None),
        P(),
        P(dp, "tensor"),
        P(dp, "tensor"),
        P(dp, "tensor"),
        P(dp, "tensor"),
        P(),
        P(),
        P(),
        P(None, every),
        P(None, every),
    )
    return jax.shard_map(
        per_device, mesh=grid, in_specs=in_specs, out_specs=out_specs, check_vma=False
    )
```

```python
import functools

import jax
import jax.numpy as jnp
from jax import lax
from jax.experimental import pallas as pl
from jax.experimental.pallas import tpu as pltpu
from jax.sharding import Mesh, PartitionSpec as P

HD = 64
GROUP = 2
FLOPS1 = 0
FLOPS2 = 0
DIRECT = 8
FORWARD_TILE = 256
BACK_TILE = 512

norm_eps = 1e-06
masked_value = -1e30
exact = lax.Precision.HIGHEST
bf16 = jnp.bfloat16
f32 = jnp.float32

VMEM = pl.BlockSpec(memory_space=pltpu.VMEM)
SMEM = pl.BlockSpec(memory_space=pltpu.SMEM)
ANY = pl.BlockSpec(memory_space=pl.ANY)


def across(shard, axis, bits):
    return lax.ppermute(shard, axis, [(i, i ^ bits) for i in range(lax.axis_size(axis))])


class Near:
    def __init__(self, array):
        self.array = array


class Raw(Near):
    pass


class Far(Raw):
    pass


def call(body, name, outs, args, smem=0, scratch=(), flops=0):
    arrays = [a.array if isinstance(a, Near) else a for a in args]
    results = [o.array if isinstance(o, Near) else o for o in outs]
    kept = sum(padded_bytes(a) for a in [*arrays, *results, *scratch] if is_plain(a))
    space = {Near: pltpu.VMEM, Far: pltpu.HBM}
    given = [
        pltpu.with_memory_space_constraint(x, space[type(a)]) if type(a) in space else x
        for a, x in zip(args, arrays)
    ]
    return pl.pallas_call(
        body,
        name=name,
        out_shape=[
            space[type(o)](x.shape, x.dtype) if type(o) in space else x
            for o, x in zip(outs, results)
        ],
        in_specs=[SMEM] * smem + [ANY if isinstance(a, Raw) else VMEM for a in args[smem:]],
        out_specs=[ANY if isinstance(o, Raw) else VMEM for o in outs],
        scratch_shapes=scratch,
        compiler_params=pltpu.CompilerParams(vmem_limit_bytes=kept + 10 * 1024 * 1024),
        cost_estimate=pl.CostEstimate(flops=flops, bytes_accessed=0, transcendentals=0),
    )(*given)


def is_plain(array):
    return getattr(array, "dtype", None) in (bf16, f32, jnp.int32)


def padded_bytes(array):
    *lead, rows, cols = (1, 1, *array.shape)
    size = jnp.dtype(array.dtype).itemsize
    for extent in lead:
        size *= extent
    return size * (-(-rows // 16) * 16) * (-(-cols // 128) * 128)


def out(shape, dtype):
    return jax.ShapeDtypeStruct(shape, dtype)


def mm(a, b):
    return jnp.dot(a, b, preferred_element_type=f32)


def mm_bt(a, b):
    return lax.dot_general(a, b, (((1,), (1,)), ((), ())), preferred_element_type=f32)


def mm_at(a, b):
    return lax.dot_general(a, b, (((0,), (0,)), ((), ())), preferred_element_type=f32)


def shares_kernel(ids, *refs):
    weights, (keep_ref, send_ref, near_ref, sems) = refs[:4], refs[4:]
    copies = [
        pltpu.make_async_copy(w, near_ref.at[i], sems.at[i]) for i, w in enumerate(weights)
    ]
    for copy in copies:
        copy.start()
    for copy in copies:
        copy.wait()
    first = ids[0] == 0
    cols = keep_ref.shape[1] // 4
    for i in range(4):
        low, high = near_ref[i, :, :cols], near_ref[i, :, cols:]
        keep_ref[:, i * cols : (i + 1) * cols] = jnp.where(first, low, high)
        send_ref[:, i * cols : (i + 1) * cols] = jnp.where(first, high, low)


def rows_kernel(ids, own_ref, got_ref, held_ref, out_ref):
    rows = own_ref.shape[0]
    out_ref[pl.ds(pl.multiple_of(ids[2] * rows, rows), rows), :] = own_ref[...]
    out_ref[pl.ds(pl.multiple_of((1 - ids[2]) * rows, rows), rows), :] = got_ref[...]


def move_kernel(count, *refs):
    sources, targets, sems = refs[:count], refs[-count - 1 : -1], refs[-1]
    copies = [
        pltpu.make_async_copy(a, b, sems.at[i]) for i, (a, b) in enumerate(zip(sources, targets))
    ]
    for copy in copies:
        copy.start()
    for copy in copies:
        copy.wait()


def unit_rows(x):
    wide = x.astype(f32)
    return wide * lax.rsqrt(jnp.mean(wide * wide, axis=1, keepdims=True) + norm_eps)


def tables_kernel(experts, capacity, direct, ids, routes_ref, turned_ref, plain_ref):
    rows, slots = plain_ref.shape
    routes = routes_ref[...]
    picks = routes == lax.broadcasted_iota(jnp.int32, (rows, experts), 1)
    upto = lax.broadcasted_iota(jnp.int32, (rows, rows), 0) >= lax.broadcasted_iota(
        jnp.int32, (rows, rows), 1
    )
    counts = mm(upto.astype(f32).astype(bf16), picks.astype(f32).astype(bf16))
    slot = jnp.sum(jnp.where(picks, counts - 1.0, 0.0), axis=1, keepdims=True).astype(jnp.int32)
    codes = lax.broadcasted_iota(jnp.int32, (1, slots), 1)
    expert = jnp.zeros((1, slots), jnp.int32)
    for i in range(1, experts):
        expert = expert + jnp.where(codes >= i * capacity, 1, 0)
    place = codes - expert * capacity
    plain = (routes == expert) & (slot == place)
    plain_ref[...] = plain.astype(f32).astype(bf16)
    turned = (routes == (expert ^ ids[1])) & (slot == place) if direct else plain
    turned_ref[...] = turned.astype(f32).astype(bf16)


def slots_kernel(table_ref, rows_ref, held_ref, out_ref):
    out_ref[...] = mm_at(table_ref[...], rows_ref[...]).astype(bf16)


def cots_kernel(parts, ids, own_ref, other_ref, wdown_ref, held_ref, cots_ref, back_ref, near_ref, sems, *scratch):
    slots = cots_ref.shape[0] // 2
    copies = []
    me = ids[1]
    for at, source in ((0, own_ref), (slots, other_ref)):
        if parts == 1:
            near_ref[at : at + slots, :] = source[...]
        else:
            rows = slots // parts
            for i in range(parts):
                scratch[0][i * rows : (i + 1) * rows, :] = source[me ^ i].astype(f32)
            near_ref[at : at + slots, :] = scratch[0][...].astype(bf16)
        copies.append(
            pltpu.make_async_copy(near_ref.at[at : at + slots], cots_ref.at[at : at + slots], sems.at[len(copies)])
        )
        copies[-1].start()
        back_ref[at : at + slots, :] = mm(near_ref[at : at + slots, :], wdown_ref[...])
    for copy in copies:
        copy.wait()


def attend_kernel(heads, parts, ids, own_ref, other_ref, gain_ref, vec_ref, row_docs, col_docs, *refs):
    pieces = refs[:parts]
    w_ref, wo_ref, x_ref, qkv_ref, mixed_ref, keep_ref, send_ref, *probs_refs = refs[parts:-1]
    seq_ref = refs[-1]
    core = ids[0]
    me = ids[1]
    seq = x_ref.shape[0]
    width = heads * HD
    half = seq // GROUP
    span = seq + FORWARD_TILE
    rows = pieces[0].shape[0]
    for i, piece in enumerate(pieces):
        start = 0 if parts == 1 else pl.multiple_of((me ^ i) * rows, rows)
        w_ref[pl.ds(start, rows), :] = piece[...]
    for place, source in ((core, own_ref), (1 - core, other_ref)):
        at = pl.ds(pl.multiple_of(place * half, half), half)
        x = source[...]
        x_ref[at, :] = x
        seq_ref[at, :] = (unit_rows(x) * gain_ref[...]).astype(bf16)
    wo_ref[...] = w_ref[:, 3 * width :]
    for i in range(0, seq, 256):
        qkv_ref[i : i + 256, :] = mm(seq_ref[i : i + 256, :], w_ref[:, : 3 * width]).astype(bf16)
    for h in range(heads):
        at = h * HD
        key = qkv_ref[:, width + at : width + at + HD]
        value = qkv_ref[:, 2 * width + at : 2 * width + at + HD]
        for i in range(0, seq, FORWARD_TILE):
            base = seq - FORWARD_TILE - i
            seg = jnp.broadcast_to(vec_ref[h : h + 1, base : base + span], (FORWARD_TILE, span))
            bias = pltpu.roll(seg, span - FORWARD_TILE + 1, 1, stride=1, stride_axis=0)[:, :seq]
            scores = mm_bt(qkv_ref[i : i + FORWARD_TILE, at : at + HD], key) * HD**-0.5 + bias
            scores = jnp.where(row_docs[i : i + FORWARD_TILE, :] == col_docs[...], scores, masked_value)
            peak = jnp.max(scores, axis=1, keepdims=True)
            exp_scores = jnp.exp(scores - peak)
            probs = exp_scores / jnp.sum(exp_scores, axis=1, keepdims=True)
            probs_refs[h][i : i + FORWARD_TILE, :] = probs.astype(bf16)
            mixed_ref[i : i + FORWARD_TILE, at : at + HD] = mm(probs.astype(bf16), value).astype(bf16)
    keep_ref[...] = mixed_ref[pl.ds(pl.multiple_of(core * half, half), half), :]
    send_ref[...] = mixed_ref[pl.ds(pl.multiple_of((1 - core) * half, half), half), :]


def attended_kernel(keep_ref, got_ref, wo_ref, wo_other_ref, held_ref, out_ref):
    total = mm_bt(keep_ref[...], wo_ref[...]) + mm_bt(got_ref[...], wo_other_ref[...])
    out_ref[...] = total.astype(bf16)


def dispatch_kernel(hidden_ref, gain_ref, table_ref, *blocks):
    hidden = hidden_ref[...]
    scale = lax.rsqrt(jnp.mean(hidden * hidden, axis=1, keepdims=True) + norm_eps)
    normed = (hidden * scale * gain_ref[...]).astype(bf16)
    slots = mm_at(table_ref[...], normed)
    rows = blocks[0].shape[0]
    for i, block in enumerate(blocks):
        block[...] = slots[i * rows : (i + 1) * rows, :].astype(bf16)


def expert_kernel(ids, own_ref, other_ref, h_ref, wup_ref, wr_ref, *refs):
    active_ref, gup_ref, chosen_ref, keep_ref, send_ref, router_ref, all_ref = refs
    rows = own_ref.shape[0]
    step = rows
    router = jnp.zeros(router_ref.shape, f32)
    root = 0.7978845608028654
    for i in range(0, 2 * rows, step):
        src = own_ref if i < rows else other_ref
        at = i % rows
        slots = src[at : at + step, :]
        all_ref[i : i + step, :] = slots
        logits = mm_bt(slots, wr_ref[...])
        peak = jnp.max(logits, axis=1, keepdims=True)
        exp_logits = jnp.exp(logits - peak)
        gates = exp_logits / jnp.sum(exp_logits, axis=1, keepdims=True)
        mine = lax.broadcasted_iota(jnp.int32, gates.shape, 1) == ids[1]
        chosen = jnp.sum(jnp.where(mine, gates, 0.0), axis=1, keepdims=True)
        chosen_ref[i : i + step, :] = chosen
        up = mm(slots, wup_ref[...])
        square = up * up
        bent = jnp.tanh(root * (up + 0.044715 * up * square))
        low = (0.5 * up * (1.0 + bent)).astype(bf16)
        active_ref[i : i + step, :] = low
        slope = 0.5 * (1.0 + bent) + 0.5 * up * (1.0 - bent * bent) * root * (
            1.0 + 3.0 * 0.044715 * square
        )
        back = h_ref[i : i + step, :]
        gup = (chosen * back * slope).astype(bf16)
        gup_ref[i : i + step, :] = gup
        grad_chosen = jnp.sum(low.astype(f32) * back, axis=1, keepdims=True)
        grad_logits = gates * (jnp.where(mine, 1.0, 0.0) - chosen) * grad_chosen
        grad_logits = grad_logits.astype(bf16)
        router = router + mm_at(grad_logits, slots)
        grad = mm_bt(gup, wup_ref[...]) + mm(grad_logits, wr_ref[...])
        if i < rows:
            keep_ref[at : at + step, :] = grad
        else:
            send_ref[at : at + step, :] = grad.astype(bf16)
    router_ref[...] = router


def expert_out_kernel(active_ref, chosen_ref, wdown_ref, held_ref, keep_ref, send_ref):
    rows = keep_ref.shape[0]
    result = mm_bt(active_ref[...], wdown_ref[...]) * chosen_ref[...]
    keep_ref[...] = result[:rows, :]
    send_ref[...] = result[rows:, :].astype(bf16)


def expert_grads_kernel(slots_ref, cots_ref, active_ref, gup_ref, chosen_ref, held_ref, gwup_ref, gwdown_ref):
    gwup_ref[...] = mm_at(slots_ref[...], gup_ref[...])
    grads = (chosen_ref[...] * cots_ref[...].astype(f32)).astype(bf16)
    gwdown_ref[...] = mm_at(grads, active_ref[...])


def join_kernel(keep_ref, got_ref, *blocks):
    total = keep_ref[...] + got_ref[...].astype(f32)
    rows = blocks[0].shape[0]
    for i, block in enumerate(blocks):
        block[...] = total[i * rows : (i + 1) * rows, :].astype(bf16)


def join_natural_kernel(parts, ids, keep_ref, got_ref, out_ref):
    total = keep_ref[...] + got_ref[...].astype(f32)
    if parts == 1:
        out_ref[...] = total.astype(bf16)
        return
    rows = out_ref.shape[1]
    for i in range(parts):
        out_ref[ids[1] ^ i] = total[i * rows : (i + 1) * rows, :].astype(bf16)


def gather_kernel(back_table_ref, *refs):
    blocks = refs[:-1]
    slots = jnp.concatenate([b[...].astype(f32) for b in blocks], axis=0).astype(bf16)
    refs[-1][...] = mm(back_table_ref[...], slots).astype(bf16)


def hidden_back_kernel(ids, hidden_ref, own_ref, got_ref, cot_ref, gain_ref, held_ref, grad_ref, low_ref, dgain_ref, all_ref, sem):
    hidden = hidden_ref[...]
    grad_normed = own_ref[...].astype(f32) + got_ref[...].astype(f32)
    scale = lax.rsqrt(jnp.mean(hidden * hidden, axis=1, keepdims=True) + norm_eps)
    pulled = gain_ref[...] * grad_normed
    inner = jnp.mean(pulled * hidden, axis=1, keepdims=True)
    grad = cot_ref[...].astype(f32) + scale * pulled - hidden * (scale * scale * scale) * inner
    all_ref[...] = grad
    rows = grad_ref.shape[0]
    mine = all_ref.at[pl.ds(pl.multiple_of(ids[2] * rows, rows), rows)]
    copy = pltpu.make_async_copy(mine, grad_ref, sem)
    copy.start()
    low_ref[...] = grad.astype(bf16)
    dgain_ref[...] = jnp.sum(grad_normed * hidden * scale, axis=0, keepdims=True)
    copy.wait()


def returned_kernel(ids, table_ref, slots_ref, held_ref, keep_ref, send_ref):
    rows = keep_ref.shape[0]
    mine = table_ref[pl.ds(pl.multiple_of(ids[2] * rows, rows), rows), :]
    keep_ref[...] = mm(mine, slots_ref[...]).astype(bf16)
    theirs = table_ref[pl.ds(pl.multiple_of((1 - ids[2]) * rows, rows), rows), :]
    send_ref[...] = mm(theirs, slots_ref[...]).astype(bf16)


def activations_kernel(ids, hidden_ref, own_ref, got_ref, out_ref):
    rows = out_ref.shape[0]
    hidden = hidden_ref[pl.ds(pl.multiple_of(ids[2] * rows, rows), rows), :]
    out_ref[...] = (hidden + (own_ref[...].astype(f32) + got_ref[...].astype(f32))).astype(bf16)


def normed_sum_kernel(ids, keep_ref, got_ref, held_ref, own_ref, send_ref, all_ref):
    all_ref[...] = keep_ref[...] + got_ref[...].astype(f32)
    rows = own_ref.shape[0]
    own_ref[...] = all_ref[pl.ds(pl.multiple_of(ids[2] * rows, rows), rows), :]
    theirs = pl.ds(pl.multiple_of((1 - ids[2]) * rows, rows), rows)
    send_ref[...] = all_ref[theirs, :].astype(bf16)


def heads_back(heads, first, qkv_ref, gm_ref, probs, dqkv_ref, diag_ref, ds_ref):
    seq = qkv_ref.shape[0]
    width = heads * HD
    here = len(probs) * HD
    span = seq + BACK_TILE
    flip = (
        lax.broadcasted_iota(jnp.int32, (BACK_TILE, BACK_TILE), 0)
        + lax.broadcasted_iota(jnp.int32, (BACK_TILE, BACK_TILE), 1)
        == BACK_TILE - 1
    ).astype(bf16)
    for h, probs_ref in enumerate(probs):
        at = (first + h) * HD
        to = h * HD
        key = qkv_ref[:, width + at : width + at + HD]
        value = qkv_ref[:, 2 * width + at : 2 * width + at + HD]
        for i in range(0, seq, BACK_TILE):
            probs_rows = probs_ref[i : i + BACK_TILE, :].astype(f32)
            grad_probs = mm_bt(gm_ref[i : i + BACK_TILE, at : at + HD], value)
            inner = jnp.sum(probs_rows * grad_probs, axis=1, keepdims=True)
            grad_scores = (probs_rows * (grad_probs - inner)).astype(bf16)
            ds_ref[i : i + BACK_TILE, :] = grad_scores
            dqkv_ref[i : i + BACK_TILE, to : to + HD] = (mm(grad_scores, key) * HD**-0.5).astype(bf16)
            flipped = mm(flip, grad_scores)
            padded = jnp.concatenate([flipped, jnp.zeros((BACK_TILE, BACK_TILE), f32)], axis=1)
            skewed = pltpu.roll(padded, 0, 1, stride=1, stride_axis=0)
            base = seq - BACK_TILE - i
            row = first + h
            diag_ref[row : row + 1, base : base + span] += jnp.sum(skewed, axis=0, keepdims=True)
        dqkv_ref[:, here + to : here + to + HD] = (
            mm_at(ds_ref[...], qkv_ref[:, at : at + HD]) * HD**-0.5
        ).astype(bf16)
        dqkv_ref[:, 2 * here + to : 2 * here + to + HD] = mm_at(
            probs_ref[...], gm_ref[:, at : at + HD]
        ).astype(bf16)


def send_rows(parts, me, gw_ref, outs, keep_ref):
    if parts == 1:
        outs[0][...] = gw_ref[...].astype(bf16)
        return
    rows = gw_ref.shape[0] // parts
    for i in range(parts // 2):
        at = slice(i * rows, (i + 1) * rows)
        keep_ref[at, :] = gw_ref[pl.ds(pl.multiple_of((me ^ 2 * i) * rows, rows), rows), :]
        there = pl.ds(pl.multiple_of((me ^ 2 * i ^ 1) * rows, rows), rows)
        outs[1][at, :] = gw_ref[there, :].astype(bf16)


def first_back_kernel(heads, parts, ids, own_ref, other_ref, gain_ref, *refs):
    wo_ref, qkv_ref, probs_ref, x_ref, mixed_ref = refs[:5]
    gm_ref, dqkv_ref, diag_ref, seq_ref, *outs = refs[5:-3]
    ga_ref, ds_ref, gw_ref = refs[-3:]
    core = ids[0]
    half = own_ref.shape[0]
    ga_ref[pl.ds(pl.multiple_of(core * half, half), half), :] = own_ref[...]
    ga_ref[pl.ds(pl.multiple_of((1 - core) * half, half), half), :] = other_ref[...]
    gm_ref[...] = mm(ga_ref[...], wo_ref[...]).astype(bf16)
    diag_ref[...] = jnp.zeros_like(diag_ref)
    heads_back(heads, 0, qkv_ref, gm_ref, [probs_ref], dqkv_ref, diag_ref, ds_ref)
    cut = dqkv_ref.shape[1]
    seq_ref[...] = (unit_rows(x_ref[...]) * gain_ref[...]).astype(bf16)
    gw_ref[:, :cut] = mm_at(seq_ref[...], dqkv_ref[...])
    gw_ref[:, cut:] = mm_at(ga_ref[...], mixed_ref[...])
    send_rows(parts, ids[1], gw_ref, outs, outs[0])


def second_back_kernel(
    heads, parts, ids, gm_ref, first_ref, diag_in_ref, hot_ref, seq_ref, gain_ref, router_ref, *refs
):
    count = heads + 2
    qkv_ref, *probs, x_ref, w_ref = refs[:count]
    refs = refs[count:]
    keep_ref, send_ref, small_ref, *outs = refs[:-7]
    diag_ref, dqkv_ref, all_ref, ds_ref, gw_ref, near_ref, sem = refs[-7:]
    core, me, side = ids[0], ids[1], ids[2]
    half = keep_ref.shape[0]
    diag_ref[...] = diag_in_ref[...]
    heads_back(heads, 1, qkv_ref, gm_ref, probs, dqkv_ref, diag_ref, ds_ref)
    gw_ref[...] = mm_at(seq_ref[...], dqkv_ref[...])
    send_rows(parts, me, gw_ref, outs, near_ref)
    copy = None
    if parts > 1:
        copy = pltpu.make_async_copy(near_ref, outs[0], sem)
        copy.start()
    rest = (heads - 1) * HD
    for i in range(3):
        at = i * heads * HD
        all_ref[:, at : at + HD] = first_ref[:, i * HD : (i + 1) * HD]
        all_ref[:, at + HD : at + heads * HD] = dqkv_ref[:, i * rest : (i + 1) * rest]
    gain = jnp.zeros((1, x_ref.shape[1]), f32)
    for place, mine in ((core, True), (1 - core, False)):
        rows = pl.ds(pl.multiple_of(place * half, half), half)
        grad = mm_bt(all_ref[rows, :], w_ref[:, : all_ref.shape[1]])
        gain = gain + jnp.sum(grad * unit_rows(x_ref[rows, :]), axis=0, keepdims=True)
        if mine:
            keep_ref[...] = grad
        else:
            send_ref[...] = grad.astype(bf16)
    small_ref[...] = jnp.zeros_like(small_ref)
    small_ref[0:1, :] = gain
    small_ref[1:2, :] = jnp.where(side == 0, gain_ref[...], 0.0)
    experts = router_ref.shape[0]
    small_ref[2 : 2 + experts, :] = router_ref[...]
    bias = jnp.dot(diag_ref[...], hot_ref[...], precision=exact, preferred_element_type=f32)
    lanes = bias.shape[1]
    for i in range(2 * GROUP):
        small_ref[2 + experts : 2 + experts + heads, i * lanes : (i + 1) * lanes] = jnp.where(
            side * GROUP + core == i, bias[:heads, :], 0.0
        )
    if copy is not None:
        copy.wait()


def fold_kernel(
    keep_ref, got_ref, small_ref, small_got_ref, second_ref, returned_ref,
    second_out, returned_out, small_out, own_ref, *sends
):
    returned_out[...] = returned_ref[...]
    end, cols = second_ref.shape
    high = small_ref.shape[0]
    second_out[:end, :] = second_ref[...]
    for i in range(2):
        at = slice(i * cols, (i + 1) * cols)
        low = (small_ref[:, at] + small_got_ref[:, at]).astype(bf16)
        second_out[end + i * high : end + (i + 1) * high, :] = low
        small_out[i * high : (i + 1) * high, :] = low.astype(f32)
    total = keep_ref[...] + got_ref[...].astype(f32)
    rows = own_ref.shape[0]
    own_ref[...] = total[:rows, :]
    for i, send in enumerate(sends):
        send[...] = total[(i + 1) * rows : (i + 2) * rows, :].astype(bf16)


def quarters(refs, at):
    a, b, c, d = (r[at, :].astype(f32) for r in refs)
    return (a + b) + (c + d)


def split_cores(core, refs, keep_ref, send_ref):
    rows = keep_ref.shape[0]
    keep_ref[...] = quarters(refs, pl.ds(pl.multiple_of(core * rows, rows), rows))
    send_ref[:rows, :] = quarters(refs, pl.ds(pl.multiple_of((1 - core) * rows, rows), rows))


def fold_second_kernel(ids, keep_ref, got_ref, small_ref, grad_ref, *refs):
    first = refs[:4]
    grad_out, keep_one_ref, send_one_ref, own_ref, *sends = refs[4:]
    grad_out[...] = grad_ref[...]
    end = keep_ref.shape[0]
    total = keep_ref[...] + got_ref[:end, :].astype(f32)
    small = (small_ref[...] + got_ref[end:, :].astype(f32)).astype(bf16)
    rows = keep_one_ref.shape[0] * 2
    for i, block in enumerate((own_ref, *sends)):
        block[:rows, :] = total[i * rows : (i + 1) * rows, :].astype(block.dtype)
        block[rows:, :] = small.astype(block.dtype)
    split_cores(ids[0], first, keep_one_ref, send_one_ref)


def sum_nodes_kernel(ids, *refs):
    second = refs[:4]
    keep_ref, send_ref = refs[-2:]
    split_cores(ids[0], second, keep_ref, send_ref)
    rows = keep_ref.shape[0]
    send_ref[rows:, :] = quarters(second, slice(2 * rows, second[0].shape[0]))


def columns_kernel(heads, ids, keep_one, got_one, keep_two, got_two, *refs):
    outs = refs[:4] if len(refs) == 4 else refs[1:5]
    core = ids[0]
    rows = keep_one.shape[0]
    cols = heads * HD
    rest = cols - HD
    for c in range(2):
        at = c * cols
        mine = core == c
        one = jnp.where(mine, keep_one[...], got_one[...])
        two = jnp.where(mine, keep_two[...], got_two[:rows, :])
        for i in range(3):
            outs[i][:, at : at + HD] = one[:, i * HD : (i + 1) * HD]
            outs[i][:, at + HD : at + cols] = two[:, i * rest : (i + 1) * rest]
        outs[3][:, at : at + cols] = one[:, 3 * HD : 3 * HD + cols]
    if len(refs) == 4:
        return
    gain_one_ref, gain_two_ref, router_ref, bias_ref = refs[5:]
    small = refs[0][rows:, :] + got_two[rows:, :]
    high = small.shape[0] // 2
    wide = jnp.concatenate([small[:high, :], small[high:, :]], axis=1)
    experts = router_ref.shape[0]
    gain_one_ref[...] = wide[0:1, :]
    gain_two_ref[...] = wide[1:2, :]
    router_ref[...] = wide[2 : 2 + experts, :]
    for i in range(2 * GROUP):
        for h in range(heads):
            row = 2 + experts + h
            bias_ref[i * heads + h : i * heads + h + 1, :] = wide[
                row : row + 1, i * 128 : i * 128 + bias_ref.shape[1]
            ]


def input_kernel(keep_ref, got_ref, grad_ref, x_ref, gain_ref, out_ref):
    grad_normed = keep_ref[...] + got_ref[...].astype(f32)
    wide = x_ref[...].astype(f32)
    scale = lax.rsqrt(jnp.mean(wide * wide, axis=1, keepdims=True) + norm_eps)
    pulled = gain_ref[...] * grad_normed
    inner = jnp.mean(pulled * wide, axis=1, keepdims=True)
    out_ref[...] = grad_ref[...] + scale * pulled - wide * (scale * scale * scale) * inner


def in_order(first, mine, other):
    return jnp.where(first, jnp.concatenate([mine, other]), jnp.concatenate([other, mine]))


def per_device(
    tokens,
    gain_one,
    w_query,
    w_key,
    w_value,
    w_out,
    bias_table,
    gain_two,
    w_router,
    w_up,
    w_down,
    routes,
    doc_lengths,
    buckets,
    cotangent,
):
    own_rows, width = tokens.shape
    block_rows = routes.shape[0]
    seq = block_rows * GROUP
    cols = w_query.shape[1] // GROUP
    heads = cols // HD
    experts = w_router.shape[1]
    capacity = max(2, (5 * block_rows + 4 * experts - 1) // (4 * experts))
    slots = experts * capacity
    nodes = lax.axis_size("node")
    core = lax.axis_index("core")
    side = lax.axis_index("tensor")
    me = lax.axis_index("node")
    direct = nodes == DIRECT
    parts = nodes if direct else 1
    ids = jnp.stack([core, me, side]).astype(jnp.int32)
    node_rows = width // nodes

    def trade(blocks):
        if direct:
            return [blocks[0]] + [across(blocks[i], "node", i) for i in range(1, nodes)]
        stacked = blocks[0].reshape(nodes, -1, blocks[0].shape[1])
        back = lax.all_to_all(stacked, "node", split_axis=0, concat_axis=0, tiled=True)
        return [back.reshape(blocks[0].shape)]

    def trade_natural(rows):
        stacked = rows.reshape(nodes, -1, rows.shape[-1])
        return lax.all_to_all(stacked, "node", split_axis=0, concat_axis=0, tiled=True)

    share = out((w_query.shape[0], 4 * cols), bf16)
    share_kept, share_sent = call(
        shares_kernel,
        "shares",
        [share, share],
        [ids, *(Far(w) for w in (w_query, w_key, w_value, w_out))],
        smem=1,
        scratch=[pltpu.VMEM((4, *w_query.shape), bf16), pltpu.SemaphoreType.DMA((4,))],
    )
    piece = in_order(core == 0, share_kept, across(share_sent, "core", 1))
    if direct:
        pieces = {0: piece}
        for i in (4, 6, 2):
            pieces[i] = across(piece, "node", i)
        for i in (0, 2, 4, 6):
            pieces[i + 1] = across(pieces[i], "node", 1)
        pieces = [pieces[i] for i in range(nodes)]
    else:
        pieces = [lax.all_gather(piece, "node", axis=0, tiled=True)]

    x_rows = call(
        rows_kernel,
        "rows",
        [out((block_rows, width), bf16)],
        [ids, tokens, across(tokens, "tensor", 1), Raw(pieces[min(1, parts - 1)])],
        smem=1,
    )[0]
    x_other = across(x_rows, "core", 1)
    gain_first = gain_one.astype(f32)[None, :]
    gain_second = gain_two.astype(f32)[None, :]

    back_table, plain_back_table = call(
        functools.partial(tables_kernel, experts, capacity, direct),
        "tables",
        [out((block_rows, slots), bf16)] * 2,
        [ids, routes],
        smem=1,
    )

    lengths_row = lax.dynamic_slice_in_dim(doc_lengths, me, 1, 0)[0]
    ends = jnp.cumsum(lengths_row)
    places = jnp.arange(seq, dtype=jnp.int32)
    docs = jnp.sum((ends[None, :] <= places[:, None]).astype(jnp.int32), axis=1)
    bucket_count = bias_table.shape[0]
    bucket_hot = (
        jnp.pad(buckets, (0, 1))[:, None] == jnp.arange(128, dtype=jnp.int32)[None, :]
    ).astype(f32)
    head_start = (side * GROUP + core) * heads
    bias_here = lax.dynamic_slice_in_dim(bias_table, head_start, heads, 1)
    bias_here = jnp.pad(bias_here, ((0, 128 - bucket_count), (0, 0)))
    bias_vectors = lax.dot_general(
        bias_here, bucket_hot, (((0,), (1,)), ((), ())), precision=exact, preferred_element_type=f32
    )

    weights, wo, x_seq, qkv, mixed, mixed_kept, mixed_sent, *probs = call(
        functools.partial(attend_kernel, heads, parts),
        "attend",
        [
            out((width, 4 * cols), bf16),
            out((width, cols), bf16),
            out((seq, width), bf16),
            out((seq, 3 * cols), bf16),
            out((seq, cols), bf16),
            out((block_rows, cols), bf16),
            out((block_rows, cols), bf16),
            *([out((seq, seq), bf16)] * heads),
        ],
        [
            ids,
            x_rows,
            Near(x_other),
            gain_first,
            bias_vectors,
            docs[:, None],
            docs[None, :],
            *(Near(p) for p in pieces),
        ],
        smem=1,
        scratch=[pltpu.VMEM((seq, width), bf16)],
    )
    kept = [weights, wo, x_seq, qkv, mixed, *probs]
    weights, wo_far, x_seq, qkv, mixed, *probs = call(
        functools.partial(move_kernel, len(kept)),
        "park",
        [Far(out(a.shape, a.dtype)) for a in kept],
        [*(Near(a) for a in kept)],
        scratch=[pltpu.SemaphoreType.DMA((len(kept),))],
    )

    natural = (nodes, slots // nodes, width) if direct else (slots, width)
    cot_slots = call(
        slots_kernel,
        "cot_slots",
        [out((slots, width), bf16)],
        [plain_back_table, cotangent, Raw(pieces[min(3, parts - 1)])],
    )[0]
    cots_own = trade_natural(cot_slots).reshape(natural)
    cots_other = across(cots_own, "core", 1)

    mixed_got = across(mixed_sent, "core", 1)
    attended = call(
        attended_kernel,
        "attended",
        [out((block_rows, width), bf16)],
        [mixed_kept, mixed_got, wo, across(wo, "core", 1), Far(mixed)],
    )[0]
    attended_got = across(attended, "tensor", 1)
    block_shapes = [out((slots // parts, width), bf16)] * parts
    hidden = x_rows.astype(f32) + (attended.astype(f32) + attended_got.astype(f32))
    blocks = call(
        dispatch_kernel,
        "dispatch",
        block_shapes,
        [hidden, gain_second, back_table],
    )
    received = trade(blocks)
    cots, back_active = call(
        functools.partial(cots_kernel, parts),
        "cots",
        [Far(out((2 * slots, width), bf16)), Near(out((2 * slots, w_down.shape[1]), f32))],
        [ids, Near(cots_own), Near(cots_other), w_down, Raw(blocks[0])],
        smem=1,
        scratch=[
            pltpu.VMEM((2 * slots, width), bf16),
            pltpu.SemaphoreType.DMA((2,)),
            *([pltpu.VMEM((slots, width), f32)] if direct else []),
        ],
    )
    slots_own = jnp.concatenate(received)
    slots_other = across(slots_own, "core", 1)
    active, grad_upward, chosen, grad_kept, grad_sent, router_part, slots_all = call(
        expert_kernel,
        "expert",
        [
            Near(out((2 * slots, w_up.shape[1]), bf16)),
            Near(out((2 * slots, w_up.shape[1]), bf16)),
            Near(out((2 * slots, 1), f32)),
            out((slots, width), f32),
            out((slots, width), bf16),
            Near(out(w_router.shape[::-1], f32)),
            Near(out((2 * slots, width), bf16)),
        ],
        [ids, slots_own, Near(slots_other), Near(back_active), w_up, w_router.T],
        smem=1,
    )
    grad_blocks = call(
        join_kernel, "join_grad", block_shapes, [grad_kept, Near(across(grad_sent, "core", 1))]
    )
    grad_back = trade(grad_blocks)
    grad_normed_two = call(
        gather_kernel,
        "gather_grad",
        [out((block_rows, width), bf16)],
        [back_table, *grad_back],
    )[0]
    grad_normed_two_got = across(grad_normed_two, "tensor", 1)

    out_kept, out_sent = call(
        expert_out_kernel,
        "expert_out",
        [out((slots, width), f32), out((slots, width), bf16)],
        [Near(active), Near(chosen), w_down, Raw(grad_blocks[-1])],
    )
    out_slots = call(
        functools.partial(join_natural_kernel, parts),
        "join_out",
        [out(natural, bf16)],
        [ids, out_kept, Near(across(out_sent, "core", 1))],
        smem=1,
    )[0]
    out_back = trade_natural(out_slots.reshape(slots, width)).reshape(slots, width)
    half_block = (own_rows, width)

    kept = [weights, wo_far, x_seq, qkv, mixed, *probs]
    weights, wo, x_seq, qkv, mixed, *probs = call(
        functools.partial(move_kernel, len(kept)),
        "unpark",
        [out(a.shape, a.dtype) for a in kept],
        [*(Far(a) for a in kept), Raw(out_slots)],
        scratch=[pltpu.SemaphoreType.DMA((len(kept),))],
    )
    grad_hidden, grad_attended, gain_two_part = call(
        hidden_back_kernel,
        "hidden_back",
        [Far(out(half_block, f32)), out((block_rows, width), bf16), Near(out((1, width), f32))],
        [
            ids,
            Near(hidden),
            grad_normed_two,
            Near(grad_normed_two_got),
            cotangent,
            gain_second,
            Raw(mixed),
        ],
        smem=1,
        scratch=[pltpu.VMEM((block_rows, width), f32), pltpu.SemaphoreType.DMA],
    )
    grad_attended_other = across(grad_attended, "core", 1)
    chunk = 3 * HD + cols
    other_chunk = 3 * (cols - HD)
    small_rows = -(-(2 + experts + heads) // 16) * 16
    if direct:
        first_shapes = [out((width // 2, chunk), t) for t in (f32, bf16)]
        second_shapes = [Far(out((width // 2, other_chunk), f32)), out((width // 2, other_chunk), bf16)]
    else:
        first_shapes = [out((width, chunk), bf16)]
        second_shapes = [out((width, other_chunk), bf16)]
    grad_mixed, first_dqkv, diagonals, normed_seq, *first_chunk = call(
        functools.partial(first_back_kernel, heads, parts),
        "first_back",
        [
            out((seq, cols), bf16),
            out((seq, 3 * HD), bf16),
            out((8, 2 * seq), f32),
            out((seq, width), bf16),
            *first_shapes,
        ],
        [
            ids,
            grad_attended,
            Near(grad_attended_other),
            gain_first,
            *(wo, qkv, probs[0], x_seq, mixed),
        ],
        smem=1,
        flops=FLOPS1,
        scratch=[
            pltpu.VMEM((seq, width), bf16),
            pltpu.VMEM((seq, seq), bf16),
            pltpu.VMEM((width, chunk), f32),
        ],
    )
    grad_kept, grad_sent, small, *second_chunk = call(
        functools.partial(second_back_kernel, heads, parts),
        "second_back",
        [
            out((block_rows, width), f32),
            out((block_rows, width), bf16),
            out((small_rows, width), f32),
            *second_shapes,
        ],
        [
            ids,
            grad_mixed,
            first_dqkv,
            diagonals,
            bucket_hot,
            normed_seq,
            Near(gain_two_part),
            Near(router_part),
            *(qkv, *probs[1:], x_seq, weights),
        ],
        smem=1,
        flops=FLOPS2,
        scratch=[
            pltpu.VMEM((8, 2 * seq), f32),
            pltpu.VMEM((seq, other_chunk), bf16),
            pltpu.VMEM((seq, 3 * cols), bf16),
            pltpu.VMEM((seq, seq), bf16),
            pltpu.VMEM((width, other_chunk), f32),
            pltpu.VMEM((width // 2, other_chunk), f32),
            pltpu.SemaphoreType.DMA,
        ],
    )

    shard_rows = w_query.shape[0]
    returned, returned_sent = call(
        returned_kernel,
        "returned",
        [out(half_block, bf16), out(half_block, bf16)],
        [ids, plain_back_table, Near(out_back), Raw(grad_kept)],
        smem=1,
    )
    part = out((shard_rows, chunk), f32)
    if direct:
        tall = width // 2 + 2 * small_rows
        second_sent, returned_sent, small, own_one, *send_one = call(
            fold_kernel,
            "fold_first",
            [
                out((tall, chunk), bf16),
                out(returned_sent.shape, bf16),
                out((2 * small_rows, chunk), f32),
                out((node_rows, chunk), f32),
                *([out((node_rows, chunk), bf16)] * 3),
            ],
            [
                first_chunk[0],
                across(first_chunk[1], "node", 1),
                small,
                across(small, "tensor", 1),
                second_chunk[1],
                returned_sent,
            ],
        )
        got_one = [across(b, "node", 2 * i + 2) for i, b in enumerate(send_one)]
        first_done = send_one[0]
    else:
        sums = [jnp.sum(trade_natural(c[0]).astype(f32), axis=0) for c in (first_chunk, second_chunk)]
        kept_one, kept_two = (
            lax.dynamic_slice_in_dim(s, core * shard_rows, shard_rows, 0) for s in sums
        )
        sent_one, sent_two = (
            lax.dynamic_slice_in_dim(s, (1 - core) * shard_rows, shard_rows, 0) for s in sums
        )
        first_done, second_done = kept_one, kept_two
    grad_normed, grad_normed_sent = call(
        normed_sum_kernel,
        "normed_sum",
        [Near(out(half_block, f32)), out(half_block, bf16)],
        [ids, grad_kept, Near(across(grad_sent, "core", 1)), Raw(first_done)],
        smem=1,
        scratch=[pltpu.VMEM((block_rows, width), f32)],
    )
    if direct:
        high = node_rows + 2 * small_rows
        grad_normed_sent, kept_one, sent_one, own_two, *send_two = call(
            fold_second_kernel,
            "fold_second",
            [out(half_block, bf16), part, part, out((high, chunk), f32), *([out((high, chunk), bf16)] * 3)],
            [
                ids,
                second_chunk[0],
                across(second_sent, "node", 1),
                small,
                grad_normed_sent,
                own_one,
                *got_one,
            ],
            smem=1,
        )
        got_two = [across(b, "node", 2 * i + 2) for i, b in enumerate(send_two)]
        second_done = send_two[0]
    grad_w_up_here, grad_w_down_here = call(
        expert_grads_kernel,
        "expert_grads",
        [out(w_up.shape, f32), out(w_down.shape, f32)],
        [
            Near(slots_all),
            cots,
            *(Near(a) for a in (active, grad_upward, chosen)),
            Raw(second_done),
        ],
    )
    input_grad = call(
        input_kernel,
        "input_grad",
        [out(half_block, f32)],
        [
            Near(grad_normed),
            Near(across(grad_normed_sent, "tensor", 1)),
            Near(grad_hidden),
            tokens,
            gain_first,
        ],
    )[0]
    activations = call(
        activations_kernel,
        "activations",
        [out(half_block, bf16)],
        [ids, Near(hidden), Near(returned), Near(across(returned_sent, "tensor", 1))],
        smem=1,
    )[0]
    if direct:
        kept_two, sent_two = call(
            sum_nodes_kernel,
            "sum_nodes",
            [part, out((shard_rows + 2 * small_rows, chunk), f32)],
            [
                ids,
                own_two,
                *got_two,
                *(Far(a) for a in (grad_w_up_here, activations, input_grad)),
            ],
            smem=1,
        )
    got_one = across(sent_one, "core", 1)
    got_two = across(sent_two, "core", 1)
    small_outs = []
    if direct:
        small_outs = [
            out((1, width), f32),
            out((1, width), f32),
            out((experts, width), f32),
            out(bias_table.shape[::-1], f32),
        ]
    weight_grads = call(
        functools.partial(columns_kernel, heads),
        "columns",
        [out(w_query.shape, f32)] * 4 + small_outs,
        [ids, kept_one, got_one, kept_two, got_two] + ([sent_two] if direct else []),
        smem=1,
    )
    if direct:
        sum_one, sum_two, sum_router, sum_bias = weight_grads[4:]
    else:
        small = lax.psum(small, ("node", "core", "tensor"))
        sum_one, sum_two, sum_router = small[:1], small[1:2], small[2 : 2 + experts]
        sum_bias = small[2 + experts : 2 + experts + heads, : 4 * 128].reshape(heads, 4, 128)
        sum_bias = sum_bias[:, :, :bucket_count].transpose(1, 0, 2).reshape(bias_table.shape[::-1])
    return (
        activations,
        input_grad,
        sum_one[0],
        *weight_grads[:4],
        sum_bias.T,
        sum_two[0],
        sum_router.T,
        grad_w_up_here,
        grad_w_down_here,
    )


def solution(mesh):
    dp, tensor = mesh.shape["dp"], mesh.shape["tensor"]
    grid = Mesh(mesh.devices.reshape(dp // GROUP, GROUP, tensor), ("node", "core", "tensor"))
    dp = ("node", "core")
    every = ("node", "core", "tensor")
    in_specs = (
        P(every, None),
        P(),
        P(dp, "tensor"),
        P(dp, "tensor"),
        P(dp, "tensor"),
        P(dp, "tensor"),
        P(),
        P(),
        P(),
        P(None, every),
        P(None, every),
        P(dp, None),
        P(),
        P(),
        P(dp, None),
    )
    out_specs = (
        P(every, None),
        P(every, None),
        P(),
        P(dp, "tensor"),
        P(dp, "tensor"),
        P(dp, "tensor"),
        P(dp, "tensor"),
        P(),
        P(),
        P(),
        P(None, every),
        P(None, every),
    )
    return jax.shard_map(
        per_device, mesh=grid, in_specs=in_specs, out_specs=out_specs, check_vma=False
    )
```
